256 devices in a mesh: dp: 16 (over x_lo, z), sp: 16 (over x_hi, y, core).
Axes of the slice: x: 4 (x_hi: 2, x_lo: 2; x = x_hi * 2 + x_lo), y: 4, z: 8, core: 2. Of those that a mesh axis runs over, the one named last changes fastest.
Arguments:
- tokens: bfloat16 [16, 2048, 1536], P('dp', 'sp'), may hold values from -8 to 8
- norm_gain: bfloat16 [1536], replicated, may hold values from 0.099609375 to 1.8984375
- qkv_weight: bfloat16 [1536, 2304], P('sp', 'dp'), may hold values from -2 to 2
- d_context: bfloat16 [16, 2048, 768], P('dp', 'sp'), may hold values from -6 to 6
Outputs:
- context: bfloat16 [16, 2048, 768], P('dp', 'sp')
- d_tokens: bfloat16 [16, 2048, 1536], P('dp', 'sp')
- weight_grad: float32 [1536, 2304], P('sp', 'dp')
- gain_grad: float32 [1536], replicated
The draws below stay inside these ranges and needn't reach their ends.
All inputs are finite; a program needn't handle non-finite values.
Results may differ from the reference program's by a relative error of at most 0.03.
Values may be sent and summed in bfloat16 or wider, within the bound.
A program may use at most 128 MiB of HBM per device.

```python
import math
import jax
import jax.numpy as jnp
from jax import lax

D = 1536
HEADS = 12
HEAD = 64
TOK_DEV = 128
SEQ = 2048
VOLS = 16


def draw_tokens(key, part):
    key = jax.random.fold_in(key, 11)
    first_key = jax.random.fold_in(key, 0)
    baseline = jax.random.normal(first_key, (VOLS, SEQ, D), jnp.float32)
    return jnp.clip(baseline, -8.0, 8.0).astype(jnp.bfloat16)


def draw_qkv_weight(key, part):
    key = jax.random.fold_in(key, 23)
    first_key = jax.random.fold_in(key, 0)
    inner_width = HEADS * HEAD
    baseline = jax.random.normal(first_key, (D, 3 * inner_width), jnp.float32) * (2.0 / math.sqrt(D))
    return jnp.clip(baseline, -2.0, 2.0).astype(jnp.bfloat16)


def with_spikes(entries, key, source, target, shards_of, factor):
    owner, partner = [(jnp.arange(entries.shape[position]) // (entries.shape[position] // shards_of)).reshape([-1 if axis == position else 1 for axis in range(entries.ndim)]) for position in (source, target)]
    chosen = jax.random.permutation(key, shards_of)[partner]
    strong = (owner == chosen) | (owner == (partner + shards_of // 2) % shards_of)
    return jnp.where(strong, factor * entries, entries)


def steps_of(rng, dims, cuts, least, largest):
    gain, own = 1.0, jax.random.fold_in(rng, 6)
    for dim, shards_of in cuts:
        draws = jnp.exp(jax.random.uniform(jax.random.fold_in(own, dim), (shards_of,), jnp.float32, least / len(cuts), largest / len(cuts)))
        gain = gain * jnp.repeat(draws, dims[dim] // shards_of).reshape([-1 if axis == dim else 1 for axis in range(len(dims))])
    return gain


def gaussian_with(key, extent, scale, bound, cuts, heavy, kind=jnp.bfloat16):
    drawn = scale * jax.random.normal(key, extent, jnp.float32)
    if cuts:
        drawn = drawn * steps_of(key, extent, cuts, -0.22, 0.18)
    return jnp.clip(with_spikes(drawn, jax.random.fold_in(key, 3), *heavy), -bound, bound).astype(kind)


def setup_inputs(seed: int = 0) -> dict:
    arg_keys = jax.random.split(jax.random.key(seed), 5)
    tokens = draw_tokens(jax.random.fold_in(arg_keys[4], 71), 0)
    norm_gain = jnp.clip(1.0 + 0.18 * jax.random.normal(arg_keys[1], (D,), jnp.float32), 0.099609375, 1.8984375).astype(jnp.bfloat16)
    qkv_weight = draw_qkv_weight(jax.random.fold_in(arg_keys[4], 71), 0)
    d_context = gaussian_with(arg_keys[3], (VOLS, SEQ, HEADS * HEAD), 1.0, 6.0, ((0, 16), (1, 16)), (1, 2, 16, 2.0))
    return {"tokens": tokens, "norm_gain": norm_gain, "qkv_weight": qkv_weight, "d_context": d_context}


EPS = 1e-05

def layer_norm(values, gain_wide):
    centred = values - lax.optimization_barrier(jnp.mean(values, axis=-1, keepdims=True))
    spread = lax.optimization_barrier(jnp.mean(centred * centred, axis=-1, keepdims=True))
    return centred * lax.rsqrt(spread + EPS) * gain_wide

def rounded(values):
    return lax.optimization_barrier(values.astype(jnp.bfloat16)).astype(jnp.float32)

def reference(tokens, norm_gain, qkv_weight, d_context):
    inner_width = HEADS * HEAD
    score_scale = HEAD ** (-0.5)
    block_count = SEQ // TOK_DEV
    gain_wide = norm_gain.astype(jnp.float32)

    def one_volume(carry, volume):
        weight_acc, gain_acc = carry
        tokens_vol, cotangent = volume
        inputs = tokens_vol.astype(jnp.float32)
        normed = layer_norm(inputs, gain_wide).astype(jnp.bfloat16)
        projected = jnp.dot(normed, qkv_weight, preferred_element_type=jnp.float32).astype(jnp.bfloat16)
        query_heads = projected[:, :inner_width].astype(jnp.float32).reshape(SEQ, HEADS, HEAD)
        key_heads = projected[:, inner_width:2 * inner_width].astype(jnp.float32).reshape(SEQ, HEADS, HEAD)
        value_heads = projected[:, 2 * inner_width:].astype(jnp.float32).reshape(SEQ, HEADS, HEAD)
        cot_heads = cotangent.astype(jnp.float32).reshape(SEQ, HEADS, HEAD)

        def one_block(pair, number):
            key_acc, value_acc = pair
            offset = (number * TOK_DEV).astype(jnp.int32)
            query_block = lax.dynamic_slice_in_dim(query_heads, offset, TOK_DEV, 0)
            cot_block = lax.dynamic_slice_in_dim(cot_heads, offset, TOK_DEV, 0)
            scores = jnp.einsum('thd,shd->hts', query_block, key_heads) * score_scale
            row_top = lax.optimization_barrier(jnp.max(scores, axis=-1, keepdims=True))
            exponent = jnp.exp(scores - row_top)
            attention = exponent / lax.optimization_barrier(jnp.sum(exponent, axis=-1, keepdims=True))
            attention_low = rounded(attention)
            context_block = jnp.einsum('hts,shd->thd', attention_low, value_heads).astype(jnp.bfloat16)
            d_attn = jnp.einsum('thd,shd->hts', cot_block, value_heads)
            row_dot = lax.optimization_barrier(jnp.sum(attention * d_attn, axis=-1, keepdims=True))
            slopes = rounded(attention * (d_attn - row_dot))
            d_query = (score_scale * jnp.einsum('hts,shd->thd', slopes, key_heads)).astype(jnp.bfloat16)
            d_key = rounded(score_scale * jnp.einsum('hts,thd->shd', slopes, query_block))
            d_value = rounded(jnp.einsum('hts,thd->shd', attention_low, cot_block))
            return ((key_acc + d_key, value_acc + d_value), (context_block, d_query))
        zeros = jnp.zeros((SEQ, HEADS, HEAD), jnp.float32)
        (key_acc, value_acc), (context_blocks, query_blocks) = lax.scan(one_block, (zeros, zeros), jnp.arange(block_count))
        context_vol = context_blocks.reshape(SEQ, inner_width)
        d_proj = jnp.concatenate([query_blocks.reshape(SEQ, inner_width), key_acc.astype(jnp.bfloat16).reshape(SEQ, inner_width), value_acc.astype(jnp.bfloat16).reshape(SEQ, inner_width)], axis=1)
        d_normed = jnp.dot(d_proj, qkv_weight.T, preferred_element_type=jnp.float32)
        _, pullback = jax.vjp(layer_norm, inputs, gain_wide)
        d_inputs, d_gain = pullback(d_normed)

        def weight_block(running, number):
            offset = (number * TOK_DEV).astype(jnp.int32)
            normed_slab = lax.dynamic_slice_in_dim(normed, offset, TOK_DEV, 0)
            proj_slab = lax.dynamic_slice_in_dim(d_proj, offset, TOK_DEV, 0)
            term = rounded(jnp.dot(normed_slab.T, proj_slab, preferred_element_type=jnp.float32))
            return (running + term, None)
        weight_sum, _ = lax.scan(weight_block, weight_acc, jnp.arange(block_count))
        return ((weight_sum, gain_acc + d_gain), (context_vol, d_inputs.astype(jnp.bfloat16)))
    start_state = (jnp.zeros((D, 3 * inner_width), jnp.float32), jnp.zeros((D,), jnp.float32))
    (weight_sum, gain_total), (context, d_tokens) = lax.scan(one_volume, start_state, (tokens, d_context))
    factor = 1.0 / math.sqrt(VOLS * SEQ)
    return (context, d_tokens, weight_sum * factor, gain_total * factor)
```

```python
import functools
import math

import jax
import jax.numpy as jnp
from jax import lax
from jax.experimental import pallas as pl
from jax.experimental.pallas import tpu as pltpu
from jax.sharding import PartitionSpec as P

MESH = pl.DeviceIdType.MESH
BF = jnp.bfloat16
F32 = jnp.float32

D = 1536
HEAD = 64
OWN = 3
TOK = 128
NY = 4
NZ = 8
NA = 4
ROWS = NY * TOK
SEQ = NA * ROWS
QW = OWN * HEAD
PW = 3 * QW
SLAB = 96
BLOCK = 144
GW = NY * SLAB
EPS = 1e-05
VMEM = pl.BlockSpec(memory_space=pltpu.VMEM)


class Place:
    def __init__(self):
        d, s = lax.axis_index("dp"), lax.axis_index("sp")
        self.x_lo, self.z = d // NZ, d % NZ
        self.x_hi, self.y, self.core = s // 8, (s // 2) % NY, s % 2
        self.group = self.x_hi * 2 + self.core
        self.far_group = (1 - self.x_hi) * 2 + self.core

    def id(self, x_hi=None, x_lo=None, y=None, z=None, core=None):
        x_hi = self.x_hi if x_hi is None else x_hi
        x_lo = self.x_lo if x_lo is None else x_lo
        y = self.y if y is None else y
        z = self.z if z is None else z
        core = self.core if core is None else core
        return {"dp": x_lo * NZ + z, "sp": x_hi * 8 + y * 2 + core}

    def other_core(self):
        return self.id(core=1 - self.core)

    def mirror(self):
        return self.id(x_hi=1 - self.x_hi, x_lo=1 - self.x_lo)

    def beside(self):
        return self.id(x_lo=1 - self.x_lo)

    def far(self):
        return self.id(x_hi=1 - self.x_hi)

    def along_y(self, step):
        return self.id(y=(self.y + step) % NY)

    def along_z(self, step):
        return self.id(z=(self.z + step) % NZ)

    def along_x(self, step):
        x = (self.x_hi * 2 + self.x_lo + step) % 4
        return self.id(x_hi=x // 2, x_lo=x % 2)


def greet(partners):
    barrier = pltpu.get_barrier_semaphore()
    for partner in partners:
        pl.semaphore_signal(barrier, inc=1, device_id=partner, device_id_type=MESH)
    return functools.partial(pl.semaphore_wait, barrier, len(partners))


def remote(src, dst, send, recv, partner):
    return pltpu.make_async_remote_copy(
        src_ref=src, dst_ref=dst, send_sem=send, recv_sem=recv, device_id=partner, device_id_type=MESH
    )


def rows_at(start, size):
    return pl.ds(pl.multiple_of(start, 16), size)


def lanes_at(start, size):
    return pl.ds(pl.multiple_of(start, 128), size)


def to_grouped(wide):
    parts = []
    for x_hi in range(2):
        for core in range(2):
            for y in range(NY):
                s = x_hi * 8 + y * 2 + core
                parts.append(wide[:, s * SLAB : (s + 1) * SLAB])
    return jnp.concatenate(parts, axis=1)


def to_natural(wide):
    parts = []
    for x_hi in range(2):
        for y in range(NY):
            for core in range(2):
                s = (x_hi * 2 + core) * NY + y
                parts.append(wide[:, s * SLAB : (s + 1) * SLAB])
    return jnp.concatenate(parts, axis=1)


def wire_row(piece):
    if piece < OWN:
        return piece * HEAD
    head, which = (piece - OWN) // 2, (piece - OWN) % 2
    return QW * (1 + which) + head * HEAD


def gather_kernel(x_ref, gain_ref, w_ref, cot_ref, nall, wall, cots,
                  wd, wy, ns, nr, cs, cr, zs, zr, bs, br, ys, yr, gs, gr):
    me = Place()
    y = me.y
    partners = (
        [me.along_z(r) for r in range(1, NZ)]
        + [me.along_y(r) for r in range(1, NY)]
        + [me.beside(), me.mirror(), me.other_core()]
    )
    ready = greet(partners)
    own_rows = rows_at((me.x_lo * NZ + me.z) * BLOCK, BLOCK)
    wd[own_rows, :] = w_ref[...]
    ready()
    z_copies, b_copies = [], []
    for r in range(1, NZ):
        c = remote(wd.at[own_rows, :], wd.at[own_rows, :], zs.at[r], zr.at[r], me.along_z(r))
        c.start()
        z_copies.append(c)
    c = remote(wd.at[own_rows, :], wd.at[own_rows, :], bs.at[0], br.at[0], me.beside())
    c.start()
    b_copies.append(c)

    x = x_ref[...].astype(F32)
    centred = x - jnp.mean(x, axis=1, keepdims=True)
    spread = jnp.mean(centred * centred, axis=1, keepdims=True)
    normed = centred * lax.rsqrt(spread + EPS) * gain_ref[...]
    tok_rows = rows_at(y * TOK, TOK)
    nall[tok_rows, :] = to_grouped(normed).astype(BF)
    right, left = me.along_y(1), me.along_y(3)
    n_right = remote(nall.at[tok_rows, :], nall.at[tok_rows, :], ns.at[0], nr.at[0], right)
    n_left = remote(nall.at[tok_rows, :], nall.at[tok_rows, :], ns.at[1], nr.at[1], left)
    n_right.start()
    n_left.start()
    cot_copies = []
    cot_lanes = lanes_at(y * TOK, TOK)
    for r in range(1, NY):
        to = (y + r) % NY
        c = remote(cot_ref.at[rows_at(to * QW, QW), :], cots.at[:, cot_lanes], cs.at[r], cr.at[r], me.along_y(r))
        c.start()
        cot_copies.append(c)
    cots[:, cot_lanes] = cot_ref[rows_at(y * QW, QW), :]

    for r in (1, 7, 2, 6, 3, 5, 4):
        z_copies[r - 1].wait_recv()
        rows = rows_at((me.x_lo * NZ + (me.z + NZ - r) % NZ) * BLOCK, BLOCK)
        c = remote(wd.at[rows, :], wd.at[rows, :], bs.at[r], br.at[r], me.beside())
        c.start()
        b_copies.append(c)
    half = TOK // 2
    from_left = rows_at(((y + 3) % NY) * TOK, half)
    from_right = rows_at(((y + 1) % NY) * TOK + half, half)
    n_right.wait_recv()
    f_right = remote(nall.at[from_left, :], nall.at[from_left, :], ns.at[2], nr.at[2], right)
    f_right.start()
    n_left.wait_recv()
    f_left = remote(nall.at[from_right, :], nall.at[from_right, :], ns.at[3], nr.at[3], left)
    f_left.start()

    for c in b_copies:
        c.wait_recv()
    y_copies = []
    for r in range(1, NY):
        to = (y + r) % NY
        for k in range(3):
            c = remote(
                wd.at[rows_at(k * NY * QW + to * QW, QW), :],
                wy.at[y, pl.ds(k * QW, QW), :],
                ys.at[r, k],
                yr.at[r, k],
                me.along_y(r),
            )
            c.start()
            y_copies.append(c)
    for k in range(3):
        wy[y, k * QW : (k + 1) * QW, :] = wd[rows_at(k * NY * QW + y * QW, QW), :]
    for c in y_copies:
        c.wait_recv()
    own = lanes_at(me.group * GW, GW)
    for piece in range(3 * OWN):
        row = wire_row(piece)
        parts = [wy[k, row : row + HEAD, :][:, :SLAB].astype(F32) for k in range(NY)]
        wall[piece * HEAD : (piece + 1) * HEAD, own] = jnp.concatenate(parts, axis=1).astype(BF)
    far = lanes_at(me.far_group * GW, GW)
    g_far = remote(wall.at[:, own], wall.at[:, own], gs.at[0], gr.at[0], me.mirror())
    g_core = remote(wall.at[:, own], wall.at[:, own], gs.at[1], gr.at[1], me.other_core())
    g_far.start()
    g_core.start()
    g_far.wait_recv()
    g_pass = remote(wall.at[:, far], wall.at[:, far], gs.at[2], gr.at[2], me.other_core())
    g_pass.start()
    g_core.wait_recv()
    g_pass.wait_recv()
    f_right.wait_recv()
    f_left.wait_recv()
    for c in cot_copies:
        c.wait_recv()
    for c in (
        z_copies + b_copies + y_copies + cot_copies
        + [n_right, n_left, f_right, f_left, g_far, g_core, g_pass]
    ):
        c.wait_send()


def dma(*shape):
    return pltpu.SemaphoreType.DMA(shape)


def gather(x, gain, w, cot):
    return pl.pallas_call(
        gather_kernel,
        out_shape=(
            jax.ShapeDtypeStruct((ROWS, D), BF),
            jax.ShapeDtypeStruct((PW, D), BF),
            jax.ShapeDtypeStruct((QW, ROWS), BF),
        ),
        in_specs=[VMEM] * 4,
        out_specs=(VMEM,) * 3,
        scratch_shapes=[
            pltpu.VMEM((16 * BLOCK, 128), BF),
            pltpu.VMEM((NY, PW, 128), BF),
            dma(4), dma(4), dma(4), dma(4), dma(8), dma(8), dma(8), dma(8),
            dma(4, 3), dma(4, 3), dma(3), dma(3),
        ],
        compiler_params=pltpu.CompilerParams(
            collective_id=0, has_side_effects=True, vmem_limit_bytes=48 * 2**20
        ),
        name="gather",
    )(x, gain, w, cot)


def keys_kernel(kv_ref, kvall, ss, rs):
    me = Place()
    ready = greet([me.far(), me.other_core()])
    own = rows_at(me.group * ROWS, ROWS)
    far = rows_at(me.far_group * ROWS, ROWS)
    ready()
    c_far = remote(kv_ref, kvall.at[own, :], ss.at[0], rs.at[0], me.far())
    c_core = remote(kv_ref, kvall.at[own, :], ss.at[1], rs.at[1], me.other_core())
    c_far.start()
    c_core.start()
    kvall[own, :] = kv_ref[...]
    c_far.wait_recv()
    c_pass = remote(kvall.at[far, :], kvall.at[far, :], ss.at[2], rs.at[2], me.other_core())
    c_pass.start()
    c_core.wait_recv()
    c_pass.wait_recv()
    for c in (c_far, c_core, c_pass):
        c.wait_send()


def keys(kv):
    return pl.pallas_call(
        keys_kernel,
        out_shape=jax.ShapeDtypeStruct((SEQ, 2 * QW), BF),
        in_specs=[VMEM],
        out_specs=VMEM,
        scratch_shapes=[dma(3), dma(3)],
        compiler_params=pltpu.CompilerParams(
            collective_id=1, has_side_effects=True, vmem_limit_bytes=48 * 2**20
        ),
        name="keys",
    )(kv)


CHUNK = 256


def attention_kernel(kv_ref, q_ref, cot_ref, ctx_ref, dq_ref, dkv_ref, s_buf, e_buf):
    chunks = SEQ // CHUNK
    q = q_ref[...] * jnp.asarray(HEAD**-0.5, BF)
    zeros = jnp.zeros((HEAD, ROWS), BF)
    q_pad = jnp.concatenate([q, zeros], axis=0)
    top = jnp.full((8, ROWS), -jnp.inf, F32)
    for i in range(chunks):
        rows = slice(i * CHUNK, (i + 1) * CHUNK)
        s = jnp.dot(kv_ref[rows, :], q_pad, preferred_element_type=F32)
        s_buf[rows, :] = s
        top = jnp.maximum(top, jnp.max(s.reshape(CHUNK // 8, 8, ROWS), axis=0))
    top = jnp.max(top, axis=0, keepdims=True)
    total = jnp.zeros((8, ROWS), F32)
    ctx = jnp.zeros((HEAD, ROWS), F32)
    for i in range(chunks):
        rows = slice(i * CHUNK, (i + 1) * CHUNK)
        e = jnp.exp(s_buf[rows, :] - top)
        total = total + jnp.sum(e.reshape(CHUNK // 8, 8, ROWS), axis=0)
        e_low = e.astype(BF)
        e_buf[rows, :] = e_low
        v_t = kv_ref[rows, :].T[HEAD:, :]
        ctx = ctx + jnp.dot(v_t, e_low, preferred_element_type=F32)
    inverse = 1.0 / jnp.sum(total, axis=0, keepdims=True)
    ctx = ctx * inverse
    ctx_ref[...] = ctx.astype(BF)
    cot = (cot_ref[...].astype(F32) * inverse).astype(BF)
    row_dot = jnp.sum(cot.astype(F32) * ctx, axis=0, keepdims=True)
    cot_pad = jnp.concatenate([zeros, cot], axis=0)
    q_side = jnp.concatenate([q, zeros], axis=0).T
    cot_side = cot_pad.T
    dq = jnp.zeros((HEAD, ROWS), F32)
    for i in range(chunks):
        rows = slice(i * CHUNK, (i + 1) * CHUNK)
        d_attn = jnp.dot(kv_ref[rows, :], cot_pad, preferred_element_type=F32)
        e_low = e_buf[rows, :]
        slopes = (e_low.astype(F32) * (d_attn - row_dot)).astype(BF)
        k_t = kv_ref[rows, :].T[:HEAD, :]
        dq = dq + jnp.dot(k_t, slopes, preferred_element_type=F32)
        dkv_ref[rows, :] = (
            jnp.dot(slopes, q_side, preferred_element_type=F32)
            + jnp.dot(e_low, cot_side, preferred_element_type=F32)
        ).astype(BF)
    dq_ref[...] = (dq * HEAD**-0.5).astype(BF)


def attend(kv, q, cot):
    return pl.pallas_call(
        attention_kernel,
        grid=(OWN,),
        out_shape=(
            jax.ShapeDtypeStruct((QW, ROWS), BF),
            jax.ShapeDtypeStruct((QW, ROWS), BF),
            jax.ShapeDtypeStruct((SEQ, 2 * QW), BF),
        ),
        in_specs=[
            pl.BlockSpec((SEQ, 128), lambda h: (0, h)),
            pl.BlockSpec((HEAD, ROWS), lambda h: (h, 0)),
            pl.BlockSpec((HEAD, ROWS), lambda h: (h, 0)),
        ],
        out_specs=(
            pl.BlockSpec((HEAD, ROWS), lambda h: (h, 0)),
            pl.BlockSpec((HEAD, ROWS), lambda h: (h, 0)),
            pl.BlockSpec((SEQ, 128), lambda h: (0, h)),
        ),
        scratch_shapes=[pltpu.VMEM((SEQ, ROWS), F32), pltpu.VMEM((SEQ, ROWS), BF)],
        compiler_params=pltpu.CompilerParams(vmem_limit_bytes=48 * 2**20),
        name="attention",
    )(kv, q, cot)


def key_sums_kernel(dkv_ref, ctx_ref, out_ref, ctx_out, r1, mid, r2, ss, rs, cs, cr):
    me = Place()
    y = me.y
    ready = greet([me.far(), me.other_core()] + [me.along_y(r) for r in range(1, NY)])
    own = rows_at(me.group * ROWS, ROWS)
    far = rows_at(me.far_group * ROWS, ROWS)
    own_there = rows_at((me.x_hi * 2 + 1 - me.core) * ROWS, ROWS)
    far_there = rows_at(((1 - me.x_hi) * 2 + 1 - me.core) * ROWS, ROWS)
    ready()
    c_far = remote(dkv_ref.at[far_there, :], r1.at[0], ss.at[0], rs.at[0], me.other_core())
    c_own = remote(dkv_ref.at[own_there, :], r1.at[1], ss.at[1], rs.at[1], me.other_core())
    c_far.start()
    c_own.start()
    ctx_copies = []
    mine = rows_at(y * QW, QW)
    for r in range(1, NY):
        to = (y + r) % NY
        c = remote(ctx_ref.at[:, lanes_at(to * TOK, TOK)], ctx_out.at[mine, :], cs.at[r], cr.at[r], me.along_y(r))
        c.start()
        ctx_copies.append(c)
    ctx_out[mine, :] = ctx_ref[:, lanes_at(y * TOK, TOK)]
    c_far.wait_recv()
    mid[...] = (dkv_ref[far, :].astype(F32) + r1[0].astype(F32)).astype(BF)
    c_x = remote(mid, r2, ss.at[2], rs.at[2], me.far())
    c_x.start()
    c_own.wait_recv()
    c_x.wait_recv()
    out_ref[...] = (dkv_ref[own, :].astype(F32) + r1[1].astype(F32) + r2[...].astype(F32)).astype(BF)
    for c in ctx_copies:
        c.wait_recv()
    for c in [c_far, c_own, c_x] + ctx_copies:
        c.wait_send()


def key_sums(dkv, ctx):
    return pl.pallas_call(
        key_sums_kernel,
        out_shape=(
            jax.ShapeDtypeStruct((ROWS, 2 * QW), BF),
            jax.ShapeDtypeStruct((NY * QW, TOK), BF),
        ),
        in_specs=[VMEM] * 2,
        out_specs=(VMEM,) * 2,
        scratch_shapes=[
            pltpu.VMEM((2, ROWS, 2 * QW), BF),
            pltpu.VMEM((ROWS, 2 * QW), BF),
            pltpu.VMEM((ROWS, 2 * QW), BF),
            dma(3), dma(3), dma(4), dma(4),
        ],
        compiler_params=pltpu.CompilerParams(
            collective_id=2, has_side_effects=True, vmem_limit_bytes=48 * 2**20
        ),
        name="key_sums",
    )(dkv, ctx)


def sums_kernel(dn_ref, wg_ref, gg_ref, x_ref, gain_ref, dx_ref, wout_ref, gout_ref,
                half_r, to_right, to_left, full_r, wr1, s1, wr2, wyo, wd, wb, wz, zbuf,
                gcore, gy, gx, gz,
                ns, nr, ws, wr, ys, yr, zs, zr, gs, gr):
    me = Place()
    y = me.y
    partners = (
        [me.along_z(r) for r in range(1, NZ)]
        + [me.along_y(r) for r in range(1, NY)]
        + [me.along_x(r) for r in range(1, 4)]
        + [me.other_core()]
    )
    ready = greet(partners)
    ready()
    sent = []

    def go(*args):
        c = remote(*args)
        c.start()
        sent.append(c)
        return c

    def group(x_hi, core):
        return lanes_at((x_hi * 2 + core) * GW, GW)

    other = 1 - me.core
    w_far = go(wg_ref.at[:, group(1 - me.x_hi, other)], wr1.at[0], ws.at[0], wr.at[0], me.other_core())
    w_own = go(wg_ref.at[:, group(me.x_hi, other)], wr1.at[1], ws.at[1], wr.at[1], me.other_core())
    half = TOK // 2
    right, left = me.along_y(1), me.along_y(3)
    opposite = ((y + 2) % NY) * TOK
    h_right = go(dn_ref.at[rows_at(opposite, half), :], half_r.at[0], ns.at[0], nr.at[0], right)
    h_left = go(dn_ref.at[rows_at(opposite + half, half), :], half_r.at[1], ns.at[1], nr.at[1], left)
    gcore[me.core] = gg_ref[...]
    g_core = go(gg_ref, gcore.at[me.core], gs.at[0], gr.at[0], me.other_core())

    w_far.wait_recv()
    s1[...] = (wg_ref[:, group(1 - me.x_hi, me.core)].astype(F32) + wr1[0].astype(F32)).astype(BF)
    w_x = go(s1, wr2, ws.at[2], wr.at[2], me.mirror())

    h_right.wait_recv()
    block = rows_at(((y + 1) % NY) * TOK, half)
    rest = rows_at(((y + 1) % NY) * TOK + half, half)
    to_right[:half, :] = (dn_ref[block, :].astype(F32) + half_r[0].astype(F32)).astype(BF)
    to_right[half:, :] = dn_ref[rest, :]
    f_right = go(to_right, full_r.at[0], ns.at[2], nr.at[2], right)
    h_left.wait_recv()
    block = rows_at(((y + 3) % NY) * TOK, half)
    rest = rows_at(((y + 3) % NY) * TOK + half, half)
    to_left[:half, :] = dn_ref[block, :]
    to_left[half:, :] = (dn_ref[rest, :].astype(F32) + half_r[1].astype(F32)).astype(BF)
    f_left = go(to_left, full_r.at[1], ns.at[3], nr.at[3], left)

    g_core.wait_recv()
    gy[y] = gcore[0] + gcore[1]
    g_y = [go(gy.at[y], gy.at[y], gs.at[r], gr.at[r], me.along_y(r)) for r in range(1, NY)]

    w_own.wait_recv()
    w_x.wait_recv()
    for piece in range(3 * OWN):
        rows = slice(piece * HEAD, (piece + 1) * HEAD)
        dense = wg_ref[rows, group(me.x_hi, me.core)].astype(F32) + wr1[1, rows, :].astype(F32) + wr2[rows, :].astype(F32)
        row = wire_row(piece)
        for k in range(NY):
            part = dense[:, k * SLAB : (k + 1) * SLAB]
            part = jnp.concatenate([part, jnp.zeros((HEAD, 128 - SLAB), F32)], axis=1)
            wyo[k, row : row + HEAD, :] = part.astype(BF)
    w_y = []
    for r in range(1, NY):
        to = (y + r) % NY
        for k in range(3):
            w_y.append(go(
                wyo.at[to, pl.ds(k * QW, QW), :],
                wd.at[rows_at(k * NY * QW + y * QW, QW), :],
                ys.at[r, k], yr.at[r, k], me.along_y(r),
            ))
    for k in range(3):
        wd[rows_at(k * NY * QW + y * QW, QW), :] = wyo[y, k * QW : (k + 1) * QW, :]

    for c in g_y:
        c.wait_recv()
    x_at = me.x_hi * 2 + me.x_lo
    gx[x_at] = gy[0] + gy[1] + gy[2] + gy[3]
    g_x = [go(gx.at[x_at], gx.at[x_at], gs.at[3 + r], gr.at[3 + r], me.along_x(r)) for r in range(1, 4)]

    for c in w_y:
        c.wait_recv()
    span = NZ * BLOCK
    w_b = go(wd.at[rows_at((1 - me.x_lo) * span, span), :], wb, ws.at[3], wr.at[3], me.beside())

    for c in g_x:
        c.wait_recv()
    gz[me.z] = gx[0] + gx[1] + gx[2] + gx[3]
    g_z = [go(gz.at[me.z], gz.at[me.z], gs.at[6 + r], gr.at[6 + r], me.along_z(r)) for r in range(1, NZ)]

    f_right.wait_recv()
    f_left.wait_recv()
    d_normed = (
        dn_ref[rows_at(y * TOK, TOK), :].astype(F32) + full_r[0].astype(F32) + full_r[1].astype(F32)
    )
    d_normed = to_natural(d_normed)
    x = x_ref[...].astype(F32)
    centred = x - jnp.mean(x, axis=1, keepdims=True)
    spread = jnp.mean(centred * centred, axis=1, keepdims=True)
    scale = lax.rsqrt(spread + EPS)
    hat = centred * scale
    inner = d_normed * gain_ref[...]
    first = jnp.mean(inner, axis=1, keepdims=True)
    second = jnp.mean(inner * hat, axis=1, keepdims=True)
    dx_ref[...] = (scale * (inner - first - hat * second)).astype(BF)

    w_b.wait_recv()
    for k in range(NZ):
        at = rows_at(me.x_lo * span + k * BLOCK, BLOCK)
        wz[k * BLOCK : (k + 1) * BLOCK, :] = (
            wd[at, :].astype(F32) + wb[k * BLOCK : (k + 1) * BLOCK, :].astype(F32)
        ).astype(BF)
    w_z = []
    for r in range(1, NZ):
        to = (me.z + r) % NZ
        w_z.append(go(wz.at[rows_at(to * BLOCK, BLOCK), :], zbuf.at[r], zs.at[r], zr.at[r], me.along_z(r)))
    for c in g_z:
        c.wait_recv()
    total = gz[0]
    for k in range(1, NZ):
        total = total + gz[k]
    gout_ref[...] = total
    total = wz[rows_at(me.z * BLOCK, BLOCK), :].astype(F32)
    for r in range(1, NZ):
        w_z[r - 1].wait_recv()
        total = total + zbuf[r].astype(F32)
    wout_ref[...] = total
    for c in sent:
        c.wait_send()


def sums(dn, wg, gg, x, gain):
    span = NZ * BLOCK
    return pl.pallas_call(
        sums_kernel,
        out_shape=(
            jax.ShapeDtypeStruct((TOK, D), BF),
            jax.ShapeDtypeStruct((BLOCK, 128), F32),
            jax.ShapeDtypeStruct((16, 128), F32),
        ),
        in_specs=[VMEM] * 5,
        out_specs=(VMEM,) * 3,
        scratch_shapes=[
            pltpu.VMEM((2, TOK // 2, D), BF),
            pltpu.VMEM((TOK, D), BF),
            pltpu.VMEM((TOK, D), BF),
            pltpu.VMEM((2, TOK, D), BF),
            pltpu.VMEM((2, PW, GW), BF),
            pltpu.VMEM((PW, GW), BF),
            pltpu.VMEM((PW, GW), BF),
            pltpu.VMEM((NY, PW, 128), BF),
            pltpu.VMEM((2 * span, 128), BF),
            pltpu.VMEM((span, 128), BF),
            pltpu.VMEM((span, 128), BF),
            pltpu.VMEM((NZ, BLOCK, 128), BF),
            pltpu.VMEM((2, 16, 128), F32),
            pltpu.VMEM((NY, 16, 128), F32),
            pltpu.VMEM((4, 16, 128), F32),
            pltpu.VMEM((NZ, 16, 128), F32),
            dma(4), dma(4), dma(4), dma(4), dma(4, 3), dma(4, 3), dma(8), dma(8), dma(14), dma(14),
        ],
        compiler_params=pltpu.CompilerParams(
            collective_id=3, has_side_effects=True, vmem_limit_bytes=48 * 2**20
        ),
        name="sums",
    )(dn, wg, gg, x, gain)


def shards(tokens, norm_gain, qkv_weight, d_context):
    x = tokens[0]
    gain = norm_gain.astype(F32)[None, :]
    w_own = jnp.pad(qkv_weight.T, ((0, 0), (0, 128 - SLAB)))
    normed, weights, cot = gather(x, gain, w_own, d_context[0].T)
    q = lax.dot_general(weights[:QW], normed, (((1,), (1,)), ((), ())), preferred_element_type=F32).astype(BF)
    kv = lax.dot_general(normed, weights[QW:], (((1,), (1,)), ((), ())), preferred_element_type=F32).astype(BF)
    kv_all = keys(kv)
    context, d_query, d_kv = attend(kv_all, q, cot)
    kv_sums, context = key_sums(d_kv, context)
    d_proj = jnp.concatenate([d_query.T, kv_sums], axis=1)
    d_normed = jnp.dot(d_proj, weights, preferred_element_type=F32).astype(BF)
    grad = lax.dot_general(d_proj, normed, (((0,), (0,)), ((), ())), preferred_element_type=F32)
    gain_terms = jnp.sum(grad * weights.astype(F32), axis=0)
    gain_terms = jnp.pad(gain_terms.reshape(12, 128), ((0, 4), (0, 0)))
    d_tokens, weight_sums, gain_sums = sums(d_normed, grad.astype(BF), gain_terms, x, gain)
    factor = 1.0 / math.sqrt(16 * SEQ)
    weight_grad = weight_sums[:, :SLAB].T * factor
    gain_grad = gain_sums[:12].reshape(2, 2, NY, SLAB).transpose(0, 2, 1, 3).reshape(D)
    gain_grad = gain_grad / norm_gain.astype(F32) * factor
    return (context.T[None], d_tokens[None], weight_grad, gain_grad)


def solution(mesh):
    in_specs = (P("dp", "sp", None), P(), P("sp", "dp"), P("dp", "sp", None))
    out_specs = (P("dp", "sp", None), P("dp", "sp", None), P("sp", "dp"), P())
    return jax.shard_map(shards, mesh=mesh, in_specs=in_specs, out_specs=out_specs, check_vma=False)
```

```python
import functools
import math

import jax
import jax.numpy as jnp
from jax import lax
from jax.experimental import pallas as pl
from jax.experimental.pallas import tpu as pltpu
from jax.sharding import PartitionSpec as P

MESH = pl.DeviceIdType.MESH
BF = jnp.bfloat16
F32 = jnp.float32

D = 1536
HEAD = 64
OWN = 3
TOK = 128
NY = 4
NZ = 8
NA = 4
ROWS = NY * TOK
SEQ = NA * ROWS
QW = OWN * HEAD
PW = 3 * QW
SLAB = 96
BLOCK = 144
GW = NY * SLAB
EPS = 1e-05
VMEM = pl.BlockSpec(memory_space=pltpu.VMEM)


class Place:
    def __init__(self):
        d, s = lax.axis_index("dp"), lax.axis_index("sp")
        self.x_lo, self.z = d // NZ, d % NZ
        self.x_hi, self.y, self.core = s // 8, (s // 2) % NY, s % 2
        self.group = self.x_hi * 2 + self.core
        self.far_group = (1 - self.x_hi) * 2 + self.core

    def id(self, x_hi=None, x_lo=None, y=None, z=None, core=None):
        x_hi = self.x_hi if x_hi is None else x_hi
        x_lo = self.x_lo if x_lo is None else x_lo
        y = self.y if y is None else y
        z = self.z if z is None else z
        core = self.core if core is None else core
        return {"dp": x_lo * NZ + z, "sp": x_hi * 8 + y * 2 + core}

    def other_core(self):
        return self.id(core=1 - self.core)

    def mirror(self):
        return self.id(x_hi=1 - self.x_hi, x_lo=1 - self.x_lo)

    def beside(self):
        return self.id(x_lo=1 - self.x_lo)

    def far(self):
        return self.id(x_hi=1 - self.x_hi)

    def along_y(self, step):
        return self.id(y=(self.y + step) % NY)

    def along_z(self, step):
        return self.id(z=(self.z + step) % NZ)

    def along_x(self, step):
        x = (self.x_hi * 2 + self.x_lo + step) % 4
        return self.id(x_hi=x // 2, x_lo=x % 2)


def greet(partners):
    barrier = pltpu.get_barrier_semaphore()
    for partner in partners:
        pl.semaphore_signal(barrier, inc=1, device_id=partner, device_id_type=MESH)
    return functools.partial(pl.semaphore_wait, barrier, len(partners))


def remote(src, dst, send, recv, partner):
    return pltpu.make_async_remote_copy(
        src_ref=src, dst_ref=dst, send_sem=send, recv_sem=recv, device_id=partner, device_id_type=MESH
    )


def rows_at(start, size):
    return pl.ds(pl.multiple_of(start, 16), size)


def lanes_at(start, size):
    return pl.ds(pl.multiple_of(start, 128), size)


def to_grouped(wide):
    parts = []
    for x_hi in range(2):
        for core in range(2):
            for y in range(NY):
                s = x_hi * 8 + y * 2 + core
                parts.append(wide[:, s * SLAB : (s + 1) * SLAB])
    return jnp.concatenate(parts, axis=1)


def to_natural(wide):
    parts = []
    for x_hi in range(2):
        for y in range(NY):
            for core in range(2):
                s = (x_hi * 2 + core) * NY + y
                parts.append(wide[:, s * SLAB : (s + 1) * SLAB])
    return jnp.concatenate(parts, axis=1)


def wire_row(piece):
    if piece < OWN:
        return piece * HEAD
    head, which = (piece - OWN) // 2, (piece - OWN) % 2
    return QW * (1 + which) + head * HEAD


def gather_kernel(x_ref, gain_ref, w_ref, cot_ref, nall, wall, cots,
                  wd, wy, ns, nr, cs, cr, zs, zr, bs, br, ys, yr, gs, gr):
    me = Place()
    y = me.y
    partners = (
        [me.along_z(r) for r in range(1, NZ)]
        + [me.along_y(r) for r in range(1, NY)]
        + [me.beside(), me.mirror(), me.other_core()]
    )
    ready = greet(partners)
    own_rows = rows_at((me.x_lo * NZ + me.z) * BLOCK, BLOCK)
    wd[own_rows, :] = w_ref[...]
    ready()
    z_copies, b_copies = [], []
    for r in range(1, NZ):
        c = remote(wd.at[own_rows, :], wd.at[own_rows, :], zs.at[r], zr.at[r], me.along_z(r))
        c.start()
        z_copies.append(c)
    c = remote(wd.at[own_rows, :], wd.at[own_rows, :], bs.at[0], br.at[0], me.beside())
    c.start()
    b_copies.append(c)

    x = x_ref[...].astype(F32)
    centred = x - jnp.mean(x, axis=1, keepdims=True)
    spread = jnp.mean(centred * centred, axis=1, keepdims=True)
    normed = centred * lax.rsqrt(spread + EPS) * gain_ref[...]
    tok_rows = rows_at(y * TOK, TOK)
    nall[tok_rows, :] = to_grouped(normed).astype(BF)
    right, left = me.along_y(1), me.along_y(3)
    n_right = remote(nall.at[tok_rows, :], nall.at[tok_rows, :], ns.at[0], nr.at[0], right)
    n_left = remote(nall.at[tok_rows, :], nall.at[tok_rows, :], ns.at[1], nr.at[1], left)
    n_right.start()
    n_left.start()
    cot_copies = []
    cot_lanes = lanes_at(y * TOK, TOK)
    for r in range(1, NY):
        to = (y + r) % NY
        c = remote(cot_ref.at[rows_at(to * QW, QW), :], cots.at[:, cot_lanes], cs.at[r], cr.at[r], me.along_y(r))
        c.start()
        cot_copies.append(c)
    cots[:, cot_lanes] = cot_ref[rows_at(y * QW, QW), :]

    for r in (1, 7, 2, 6, 3, 5, 4):
        z_copies[r - 1].wait_recv()
        rows = rows_at((me.x_lo * NZ + (me.z + NZ - r) % NZ) * BLOCK, BLOCK)
        c = remote(wd.at[rows, :], wd.at[rows, :], bs.at[r], br.at[r], me.beside())
        c.start()
        b_copies.append(c)
    half = TOK // 2
    from_left = rows_at(((y + 3) % NY) * TOK, half)
    from_right = rows_at(((y + 1) % NY) * TOK + half, half)
    n_right.wait_recv()
    f_right = remote(nall.at[from_left, :], nall.at[from_left, :], ns.at[2], nr.at[2], right)
    f_right.start()
    n_left.wait_recv()
    f_left = remote(nall.at[from_right, :], nall.at[from_right, :], ns.at[3], nr.at[3], left)
    f_left.start()

    for c in b_copies:
        c.wait_recv()
    y_copies = []
    for r in range(1, NY):
        to = (y + r) % NY
        for k in range(3):
            c = remote(
                wd.at[rows_at(k * NY * QW + to * QW, QW), :],
                wy.at[y, pl.ds(k * QW, QW), :],
                ys.at[r, k],
                yr.at[r, k],
                me.along_y(r),
            )
            c.start()
            y_copies.append(c)
    for k in range(3):
        wy[y, k * QW : (k + 1) * QW, :] = wd[rows_at(k * NY * QW + y * QW, QW), :]
    for c in y_copies:
        c.wait_recv()
    own = lanes_at(me.group * GW, GW)
    for piece in range(3 * OWN):
        row = wire_row(piece)
        parts = [wy[k, row : row + HEAD, :][:, :SLAB].astype(F32) for k in range(NY)]
        wall[piece * HEAD : (piece + 1) * HEAD, own] = jnp.concatenate(parts, axis=1).astype(BF)
    far = lanes_at(me.far_group * GW, GW)
    g_far = remote(wall.at[:, own], wall.at[:, own], gs.at[0], gr.at[0], me.mirror())
    g_core = remote(wall.at[:, own], wall.at[:, own], gs.at[1], gr.at[1], me.other_core())
    g_far.start()
    g_core.start()
    g_far.wait_recv()
    g_pass = remote(wall.at[:, far], wall.at[:, far], gs.at[2], gr.at[2], me.other_core())
    g_pass.start()
    g_core.wait_recv()
    g_pass.wait_recv()
    f_right.wait_recv()
    f_left.wait_recv()
    for c in cot_copies:
        c.wait_recv()
    for c in (
        z_copies + b_copies + y_copies + cot_copies
        + [n_right, n_left, f_right, f_left, g_far, g_core, g_pass]
    ):
        c.wait_send()


def dma(*shape):
    return pltpu.SemaphoreType.DMA(shape)


def gather(x, gain, w, cot):
    return pl.pallas_call(
        gather_kernel,
        out_shape=(
            jax.ShapeDtypeStruct((ROWS, D), BF),
            jax.ShapeDtypeStruct((PW, D), BF),
            jax.ShapeDtypeStruct((QW, ROWS), BF),
        ),
        in_specs=[VMEM] * 4,
        out_specs=(VMEM,) * 3,
        scratch_shapes=[
            pltpu.VMEM((16 * BLOCK, 128), BF),
            pltpu.VMEM((NY, PW, 128), BF),
            dma(4), dma(4), dma(4), dma(4), dma(8), dma(8), dma(8), dma(8),
            dma(4, 3), dma(4, 3), dma(3), dma(3),
        ],
        compiler_params=pltpu.CompilerParams(
            collective_id=0, has_side_effects=True, vmem_limit_bytes=48 * 2**20
        ),
        name="gather",
    )(x, gain, w, cot)


CHUNK = 256
STEPS = SEQ // CHUNK


def attention_kernel(q_ref, kv_ref, cot_ref, dq_ref, out_ref, ctx_out,
                     kvall, dkv, ctx_own, s_buf, e_buf, r1, mid, r2,
                     ks, kr, ss, rs, cs, cr):
    me = Place()
    y = me.y
    ready = greet([me.far(), me.other_core()] + [me.along_y(r) for r in range(1, NY)])
    own = rows_at(me.group * ROWS, ROWS)
    far = rows_at(me.far_group * ROWS, ROWS)
    own_there = rows_at((me.x_hi * 2 + 1 - me.core) * ROWS, ROWS)
    far_there = rows_at(((1 - me.x_hi) * 2 + 1 - me.core) * ROWS, ROWS)
    mine = y * QW
    ready()
    sent = []

    def go(*args):
        c = remote(*args)
        c.start()
        sent.append(c)
        return c

    def head_lanes(h):
        return slice(h * 128, (h + 1) * 128)

    k_far = [go(kv_ref.at[:, head_lanes(h)], kvall.at[own, head_lanes(h)], ks.at[0, h], kr.at[0, h], me.far()) for h in range(OWN)]
    k_core = [go(kv_ref.at[:, head_lanes(h)], kvall.at[own, head_lanes(h)], ks.at[1, h], kr.at[1, h], me.other_core()) for h in range(OWN)]
    k_pass = []
    kvall[own, :] = kv_ref[...]
    d_far, d_own, d_x, ctx_copies = [], [], [], []

    def pass_keys(h):
        k_far[h].wait_recv()
        k_pass.append(go(kvall.at[far, head_lanes(h)], kvall.at[far, head_lanes(h)], ks.at[2, h], kr.at[2, h], me.other_core()))

    def pass_sums(h):
        lanes = head_lanes(h)
        d_far[h].wait_recv()
        mid[:, lanes] = (dkv[far, lanes].astype(F32) + r1[0, :, lanes].astype(F32)).astype(BF)
        d_x.append(go(mid.at[:, lanes], r2.at[:, lanes], ss.at[2, h], rs.at[2, h], me.far()))

    def finish(h):
        lanes = head_lanes(h)
        d_own[h].wait_recv()
        d_x[h].wait_recv()
        out_ref[:, lanes] = (
            dkv[own, lanes].astype(F32) + r1[1, :, lanes].astype(F32) + r2[:, lanes].astype(F32)
        ).astype(BF)

    pass_keys(0)
    zeros = jnp.zeros((HEAD, ROWS), BF)
    for h in range(OWN):
        lanes = head_lanes(h)
        head_rows = slice(h * HEAD, (h + 1) * HEAD)
        q = q_ref[head_rows, :] * jnp.asarray(HEAD**-0.5, BF)
        q_pad = jnp.concatenate([q, zeros], axis=0)
        k_core[h].wait_recv()
        k_pass[h].wait_recv()
        top = jnp.full((8, ROWS), -jnp.inf, F32)
        for i in range(STEPS):
            rows = slice(i * CHUNK, (i + 1) * CHUNK)
            s = jnp.dot(kvall[rows, lanes], q_pad, preferred_element_type=F32)
            s_buf[rows, :] = s
            top = jnp.maximum(top, jnp.max(s.reshape(CHUNK // 8, 8, ROWS), axis=0))
        top = jnp.max(top, axis=0, keepdims=True)
        total = jnp.zeros((8, ROWS), F32)
        ctx = jnp.zeros((HEAD, ROWS), F32)
        for i in range(STEPS):
            rows = slice(i * CHUNK, (i + 1) * CHUNK)
            e = jnp.exp(s_buf[rows, :] - top)
            total = total + jnp.sum(e.reshape(CHUNK // 8, 8, ROWS), axis=0)
            e_low = e.astype(BF)
            e_buf[rows, :] = e_low
            v_t = kvall[rows, lanes].T[HEAD:, :]
            ctx = ctx + jnp.dot(v_t, e_low, preferred_element_type=F32)
        inverse = 1.0 / jnp.sum(total, axis=0, keepdims=True)
        ctx = ctx * inverse
        ctx_own[head_rows, :] = ctx.astype(BF)
        rows_there = rows_at(mine + h * HEAD, HEAD)
        for r in range(1, NY):
            to = lanes_at(((y + r) % NY) * TOK, TOK)
            ctx_copies.append(go(ctx_own.at[head_rows, to], ctx_out.at[rows_there, :], cs.at[h, r], cr.at[h, r], me.along_y(r)))
        ctx_out[rows_there, :] = ctx_own[head_rows, lanes_at(y * TOK, TOK)]
        if h + 1 < OWN:
            pass_keys(h + 1)
        if h > 0:
            pass_sums(h - 1)
        cot = (cot_ref[head_rows, :].astype(F32) * inverse).astype(BF)
        row_dot = jnp.sum(cot.astype(F32) * ctx, axis=0, keepdims=True)
        cot_pad = jnp.concatenate([zeros, cot], axis=0)
        q_side = q_pad.T
        cot_side = cot_pad.T
        dq = jnp.zeros((HEAD, ROWS), F32)
        for i in range(STEPS):
            rows = slice(i * CHUNK, (i + 1) * CHUNK)
            d_attn = jnp.dot(kvall[rows, lanes], cot_pad, preferred_element_type=F32)
            e_low = e_buf[rows, :]
            slopes = (e_low.astype(F32) * (d_attn - row_dot)).astype(BF)
            k_t = kvall[rows, lanes].T[:HEAD, :]
            dq = dq + jnp.dot(k_t, slopes, preferred_element_type=F32)
            dkv[rows, lanes] = (
                jnp.dot(slopes, q_side, preferred_element_type=F32)
                + jnp.dot(e_low, cot_side, preferred_element_type=F32)
            ).astype(BF)
        dq_ref[head_rows, :] = (dq * HEAD**-0.5).astype(BF)
        d_far.append(go(dkv.at[far_there, lanes], r1.at[0, :, lanes], ss.at[0, h], rs.at[0, h], me.other_core()))
        d_own.append(go(dkv.at[own_there, lanes], r1.at[1, :, lanes], ss.at[1, h], rs.at[1, h], me.other_core()))
    pass_sums(OWN - 1)
    for h in range(OWN):
        finish(h)
    for c in ctx_copies:
        c.wait_recv()
    for c in sent:
        c.wait_send()


def attend(q, kv, cot):
    return pl.pallas_call(
        attention_kernel,
        out_shape=(
            jax.ShapeDtypeStruct((QW, ROWS), BF),
            jax.ShapeDtypeStruct((ROWS, 2 * QW), BF),
            jax.ShapeDtypeStruct((NY * QW, TOK), BF),
        ),
        in_specs=[VMEM] * 3,
        out_specs=(VMEM,) * 3,
        scratch_shapes=[
            pltpu.VMEM((SEQ, 2 * QW), BF),
            pltpu.VMEM((SEQ, 2 * QW), BF),
            pltpu.VMEM((QW, ROWS), BF),
            pltpu.VMEM((SEQ, ROWS), F32),
            pltpu.VMEM((SEQ, ROWS), BF),
            pltpu.VMEM((2, ROWS, 2 * QW), BF),
            pltpu.VMEM((ROWS, 2 * QW), BF),
            pltpu.VMEM((ROWS, 2 * QW), BF),
            dma(3, 3), dma(3, 3), dma(3, 3), dma(3, 3), dma(3, 4), dma(3, 4),
        ],
        compiler_params=pltpu.CompilerParams(
            collective_id=1, has_side_effects=True, vmem_limit_bytes=48 * 2**20
        ),
        name="attention",
    )(q, kv, cot)


def sums_kernel(dn_ref, wg_ref, gg_ref, x_ref, gain_ref, dx_ref, wout_ref, gout_ref,
                half_r, to_right, to_left, full_r, wr1, s1, wr2, wyo, wd, wb, wz, zbuf,
                gcore, gy, gx, gz,
                ns, nr, ws, wr, ys, yr, zs, zr, gs, gr):
    me = Place()
    y = me.y
    partners = (
        [me.along_z(r) for r in range(1, NZ)]
        + [me.along_y(r) for r in range(1, NY)]
        + [me.along_x(r) for r in range(1, 4)]
        + [me.other_core()]
    )
    ready = greet(partners)
    ready()
    sent = []

    def go(*args):
        c = remote(*args)
        c.start()
        sent.append(c)
        return c

    def group(x_hi, core):
        return lanes_at((x_hi * 2 + core) * GW, GW)

    other = 1 - me.core
    w_far = go(wg_ref.at[:, group(1 - me.x_hi, other)], wr1.at[0], ws.at[0], wr.at[0], me.other_core())
    w_own = go(wg_ref.at[:, group(me.x_hi, other)], wr1.at[1], ws.at[1], wr.at[1], me.other_core())
    half = TOK // 2
    right, left = me.along_y(1), me.along_y(3)
    opposite = ((y + 2) % NY) * TOK
    h_right = go(dn_ref.at[rows_at(opposite, half), :], half_r.at[0], ns.at[0], nr.at[0], right)
    h_left = go(dn_ref.at[rows_at(opposite + half, half), :], half_r.at[1], ns.at[1], nr.at[1], left)
    gcore[me.core] = gg_ref[...]
    g_core = go(gg_ref, gcore.at[me.core], gs.at[0], gr.at[0], me.other_core())

    w_far.wait_recv()
    s1[...] = (wg_ref[:, group(1 - me.x_hi, me.core)].astype(F32) + wr1[0].astype(F32)).astype(BF)
    w_x = go(s1, wr2, ws.at[2], wr.at[2], me.mirror())

    h_right.wait_recv()
    block = rows_at(((y + 1) % NY) * TOK, half)
    rest = rows_at(((y + 1) % NY) * TOK + half, half)
    to_right[:half, :] = (dn_ref[block, :].astype(F32) + half_r[0].astype(F32)).astype(BF)
    to_right[half:, :] = dn_ref[rest, :]
    f_right = go(to_right, full_r.at[0], ns.at[2], nr.at[2], right)
    h_left.wait_recv()
    block = rows_at(((y + 3) % NY) * TOK, half)
    rest = rows_at(((y + 3) % NY) * TOK + half, half)
    to_left[:half, :] = dn_ref[block, :]
    to_left[half:, :] = (dn_ref[rest, :].astype(F32) + half_r[1].astype(F32)).astype(BF)
    f_left = go(to_left, full_r.at[1], ns.at[3], nr.at[3], left)

    g_core.wait_recv()
    gy[y] = gcore[0] + gcore[1]
    g_y = [go(gy.at[y], gy.at[y], gs.at[r], gr.at[r], me.along_y(r)) for r in range(1, NY)]

    w_own.wait_recv()
    w_x.wait_recv()
    for piece in range(3 * OWN):
        rows = slice(piece * HEAD, (piece + 1) * HEAD)
        dense = wg_ref[rows, group(me.x_hi, me.core)].astype(F32) + wr1[1, rows, :].astype(F32) + wr2[rows, :].astype(F32)
        row = wire_row(piece)
        for k in range(NY):
            part = dense[:, k * SLAB : (k + 1) * SLAB]
            part = jnp.concatenate([part, jnp.zeros((HEAD, 128 - SLAB), F32)], axis=1)
            wyo[k, row : row + HEAD, :] = part.astype(BF)
    w_y = []
    for r in range(1, NY):
        to = (y + r) % NY
        for k in range(3):
            w_y.append(go(
                wyo.at[to, pl.ds(k * QW, QW), :],
                wd.at[rows_at(k * NY * QW + y * QW, QW), :],
                ys.at[r, k], yr.at[r, k], me.along_y(r),
            ))
    for k in range(3):
        wd[rows_at(k * NY * QW + y * QW, QW), :] = wyo[y, k * QW : (k + 1) * QW, :]

    for c in g_y:
        c.wait_recv()
    x_at = me.x_hi * 2 + me.x_lo
    gx[x_at] = gy[0] + gy[1] + gy[2] + gy[3]
    g_x = [go(gx.at[x_at], gx.at[x_at], gs.at[3 + r], gr.at[3 + r], me.along_x(r)) for r in range(1, 4)]

    for c in w_y:
        c.wait_recv()
    span = NZ * BLOCK
    w_b = go(wd.at[rows_at((1 - me.x_lo) * span, span), :], wb, ws.at[3], wr.at[3], me.beside())

    for c in g_x:
        c.wait_recv()
    gz[me.z] = gx[0] + gx[1] + gx[2] + gx[3]
    g_z = [go(gz.at[me.z], gz.at[me.z], gs.at[6 + r], gr.at[6 + r], me.along_z(r)) for r in range(1, NZ)]

    f_right.wait_recv()
    f_left.wait_recv()
    d_normed = (
        dn_ref[rows_at(y * TOK, TOK), :].astype(F32) + full_r[0].astype(F32) + full_r[1].astype(F32)
    )
    d_normed = to_natural(d_normed)
    x = x_ref[...].astype(F32)
    centred = x - jnp.mean(x, axis=1, keepdims=True)
    spread = jnp.mean(centred * centred, axis=1, keepdims=True)
    scale = lax.rsqrt(spread + EPS)
    hat = centred * scale
    inner = d_normed * gain_ref[...]
    first = jnp.mean(inner, axis=1, keepdims=True)
    second = jnp.mean(inner * hat, axis=1, keepdims=True)
    dx_ref[...] = (scale * (inner - first - hat * second)).astype(BF)

    w_b.wait_recv()
    for k in range(NZ):
        at = rows_at(me.x_lo * span + k * BLOCK, BLOCK)
        wz[k * BLOCK : (k + 1) * BLOCK, :] = (
            wd[at, :].astype(F32) + wb[k * BLOCK : (k + 1) * BLOCK, :].astype(F32)
        ).astype(BF)
    w_z = []
    for r in range(1, NZ):
        to = (me.z + r) % NZ
        w_z.append(go(wz.at[rows_at(to * BLOCK, BLOCK), :], zbuf.at[r], zs.at[r], zr.at[r], me.along_z(r)))
    for c in g_z:
        c.wait_recv()
    total = gz[0]
    for k in range(1, NZ):
        total = total + gz[k]
    gout_ref[...] = total
    total = wz[rows_at(me.z * BLOCK, BLOCK), :].astype(F32)
    for r in range(1, NZ):
        w_z[r - 1].wait_recv()
        total = total + zbuf[r].astype(F32)
    wout_ref[...] = total
    for c in sent:
        c.wait_send()


def sums(dn, wg, gg, x, gain):
    span = NZ * BLOCK
    return pl.pallas_call(
        sums_kernel,
        out_shape=(
            jax.ShapeDtypeStruct((TOK, D), BF),
            jax.ShapeDtypeStruct((BLOCK, 128), F32),
            jax.ShapeDtypeStruct((16, 128), F32),
        ),
        in_specs=[VMEM] * 5,
        out_specs=(VMEM,) * 3,
        scratch_shapes=[
            pltpu.VMEM((2, TOK // 2, D), BF),
            pltpu.VMEM((TOK, D), BF),
            pltpu.VMEM((TOK, D), BF),
            pltpu.VMEM((2, TOK, D), BF),
            pltpu.VMEM((2, PW, GW), BF),
            pltpu.VMEM((PW, GW), BF),
            pltpu.VMEM((PW, GW), BF),
            pltpu.VMEM((NY, PW, 128), BF),
            pltpu.VMEM((2 * span, 128), BF),
            pltpu.VMEM((span, 128), BF),
            pltpu.VMEM((span, 128), BF),
            pltpu.VMEM((NZ, BLOCK, 128), BF),
            pltpu.VMEM((2, 16, 128), F32),
            pltpu.VMEM((NY, 16, 128), F32),
            pltpu.VMEM((4, 16, 128), F32),
            pltpu.VMEM((NZ, 16, 128), F32),
            dma(4), dma(4), dma(4), dma(4), dma(4, 3), dma(4, 3), dma(8), dma(8), dma(14), dma(14),
        ],
        compiler_params=pltpu.CompilerParams(
            collective_id=2, has_side_effects=True, vmem_limit_bytes=48 * 2**20
        ),
        name="sums",
    )(dn, wg, gg, x, gain)


def shards(tokens, norm_gain, qkv_weight, d_context):
    x = tokens[0]
    gain = norm_gain.astype(F32)[None, :]
    w_own = jnp.pad(qkv_weight.T, ((0, 0), (0, 128 - SLAB)))
    normed, weights, cot = gather(x, gain, w_own, d_context[0].T)
    q = lax.dot_general(weights[:QW], normed, (((1,), (1,)), ((), ())), preferred_element_type=F32).astype(BF)
    kv = lax.dot_general(normed, weights[QW:], (((1,), (1,)), ((), ())), preferred_element_type=F32).astype(BF)
    d_query, kv_sums, context = attend(q, kv, cot)
    d_proj = jnp.concatenate([d_query.T, kv_sums], axis=1)
    d_normed = jnp.dot(d_proj, weights, preferred_element_type=F32).astype(BF)
    grad = lax.dot_general(d_proj, normed, (((0,), (0,)), ((), ())), preferred_element_type=F32)
    gain_terms = jnp.sum(grad * weights.astype(F32), axis=0)
    gain_terms = jnp.pad(gain_terms.reshape(12, 128), ((0, 4), (0, 0)))
    d_tokens, weight_sums, gain_sums = sums(d_normed, grad.astype(BF), gain_terms, x, gain)
    factor = 1.0 / math.sqrt(16 * SEQ)
    weight_grad = weight_sums[:, :SLAB].T * factor
    gain_grad = gain_sums[:12].reshape(2, 2, NY, SLAB).transpose(0, 2, 1, 3).reshape(D)
    gain_grad = gain_grad / norm_gain.astype(F32) * factor
    return (context.T[None], d_tokens[None], weight_grad, gain_grad)


def solution(mesh):
    in_specs = (P("dp", "sp", None), P(), P("sp", "dp"), P("dp", "sp", None))
    out_specs = (P("dp", "sp", None), P("dp", "sp", None), P("sp", "dp"), P())
    return jax.shard_map(shards, mesh=mesh, in_specs=in_specs, out_specs=out_specs, check_vma=False)
```

```python
import functools
import math

import jax
import jax.numpy as jnp
from jax import lax
from jax.experimental import pallas as pl
from jax.experimental.pallas import tpu as pltpu
from jax.sharding import PartitionSpec as P

MESH = pl.DeviceIdType.MESH
BF = jnp.bfloat16
F32 = jnp.float32

D = 1536
HEAD = 64
OWN = 3
TOK = 128
NY = 4
NZ = 8
NA = 4
ROWS = NY * TOK
SEQ = NA * ROWS
QW = OWN * HEAD
PW = 3 * QW
SLAB = 96
BLOCK = 144
GW = NY * SLAB
EPS = 1e-05
VMEM = pl.BlockSpec(memory_space=pltpu.VMEM)


class Place:
    def __init__(self):
        d, s = lax.axis_index("dp"), lax.axis_index("sp")
        self.x_lo, self.z = d // NZ, d % NZ
        self.x_hi, self.y, self.core = s // 8, (s // 2) % NY, s % 2
        self.group = self.x_hi * 2 + self.core
        self.far_group = (1 - self.x_hi) * 2 + self.core

    def id(self, x_hi=None, x_lo=None, y=None, z=None, core=None):
        x_hi = self.x_hi if x_hi is None else x_hi
        x_lo = self.x_lo if x_lo is None else x_lo
        y = self.y if y is None else y
        z = self.z if z is None else z
        core = self.core if core is None else core
        return {"dp": x_lo * NZ + z, "sp": x_hi * 8 + y * 2 + core}

    def other_core(self):
        return self.id(core=1 - self.core)

    def mirror(self):
        return self.id(x_hi=1 - self.x_hi, x_lo=1 - self.x_lo)

    def beside(self):
        return self.id(x_lo=1 - self.x_lo)

    def far(self):
        return self.id(x_hi=1 - self.x_hi)

    def along_y(self, step):
        return self.id(y=(self.y + step) % NY)

    def along_z(self, step):
        return self.id(z=(self.z + step) % NZ)

    def along_x(self, step):
        x = (self.x_hi * 2 + self.x_lo + step) % 4
        return self.id(x_hi=x // 2, x_lo=x % 2)


def greet(partners):
    barrier = pltpu.get_barrier_semaphore()
    for partner in partners:
        pl.semaphore_signal(barrier, inc=1, device_id=partner, device_id_type=MESH)
    return functools.partial(pl.semaphore_wait, barrier, len(partners))


def remote(src, dst, send, recv, partner):
    return pltpu.make_async_remote_copy(
        src_ref=src, dst_ref=dst, send_sem=send, recv_sem=recv, device_id=partner, device_id_type=MESH
    )


def rows_at(start, size):
    return pl.ds(pl.multiple_of(start, 16), size)


def lanes_at(start, size):
    return pl.ds(pl.multiple_of(start, 128), size)


def to_grouped(wide):
    parts = []
    for x_hi in range(2):
        for core in range(2):
            for y in range(NY):
                s = x_hi * 8 + y * 2 + core
                parts.append(wide[:, s * SLAB : (s + 1) * SLAB])
    return jnp.concatenate(parts, axis=1)


def to_natural(wide):
    parts = []
    for x_hi in range(2):
        for y in range(NY):
            for core in range(2):
                s = (x_hi * 2 + core) * NY + y
                parts.append(wide[:, s * SLAB : (s + 1) * SLAB])
    return jnp.concatenate(parts, axis=1)


UNIT = 48
UNITS = 12
SHARD = 3


def unit_home(u, y):
    column = (u // 4) * 16 + 4 * y + u % 4
    d = column // SHARD
    return column - SHARD * d, d // NZ, d % NZ


def shard_unit(me, j):
    column = (me.x_lo * NZ + me.z) * SHARD + j
    return (column % 16) // 4, (column // 16) * 4 + column % 4


def each_unit(me, here, there):
    def step(u, carry):
        slot, x_lo, z = unit_home(u, me.y)
        if here is not None:
            pl.when(x_lo == me.x_lo)(lambda: here(u, slot, z))
        if there is not None:
            pl.when(x_lo != me.x_lo)(lambda: there(u))
        return carry

    lax.fori_loop(0, UNITS, step, 0)


def unit_rows(u):
    return rows_at(u * UNIT, UNIT)


def wire_row(piece):
    if piece < OWN:
        return piece * HEAD
    head, which = (piece - OWN) // 2, (piece - OWN) % 2
    return QW * (1 + which) + head * HEAD


def gather_kernel(x_ref, gain_ref, w_ref, cot_ref, nall, w_out, cots,
                  wall, ybuf, ns, nr, cs, cr, ys, yr, zs, zr, xs, xr, ds, dr):
    me = Place()
    y = me.y
    right, left = me.along_x(1), me.along_x(3)
    x_at = me.x_hi * 2 + me.x_lo
    own = lanes_at(me.group * GW, GW)
    far = lanes_at(me.far_group * GW, GW)
    hi_left, hi_right = ((x_at + 3) % 4) // 2, ((x_at + 1) % 4) // 2
    of_left = lanes_at((hi_left * 2 + me.core) * GW, GW)
    of_right = lanes_at((hi_right * 2 + me.core) * GW, GW)
    partners = (
        [me.along_z(r) for r in range(1, NZ)]
        + [me.along_y(r) for r in range(1, NY)]
        + [left, right, me.other_core()]
    )
    ready = greet(partners)

    x = x_ref[...].astype(F32)
    centred = x - jnp.mean(x, axis=1, keepdims=True)
    spread = jnp.mean(centred * centred, axis=1, keepdims=True)
    normed = centred * lax.rsqrt(spread + EPS) * gain_ref[...]
    tok_rows = rows_at(y * TOK, TOK)
    nall[tok_rows, :] = to_grouped(normed).astype(BF)
    ready()

    def y_copy(j, to):
        return remote(w_ref.at[pl.ds(j * UNIT, UNIT), :], ybuf.at[y, j], ys.at[j], yr.at[j, y], me.id(y=to))

    for j in range(SHARD):
        to, _ = shard_unit(me, j)
        pl.when(to != y)(lambda: y_copy(j, to).start())

    up, down = me.along_y(1), me.along_y(3)
    n_up = remote(nall.at[tok_rows, :], nall.at[tok_rows, :], ns.at[0], nr.at[0], up)
    n_down = remote(nall.at[tok_rows, :], nall.at[tok_rows, :], ns.at[1], nr.at[1], down)
    n_up.start()
    n_down.start()

    for j in range(SHARD):
        to, u = shard_unit(me, j)

        @pl.when(to == y)
        def _():
            ybuf[y, j] = w_ref[j * UNIT : (j + 1) * UNIT, :]
            for r in range(1, NY):
                k = (y + r) % NY
                remote(ybuf.at[k, j], ybuf.at[k, j], ys.at[j], yr.at[j, k], me.along_y(r)).wait_recv()
            parts = [ybuf[k, j][:, :SLAB].astype(F32) for k in range(NY)]
            wall[unit_rows(u), own] = jnp.concatenate(parts, axis=1).astype(BF)

    def piece(u, lanes):
        return wall.at[unit_rows(u), lanes]

    def z_copy(u, r):
        return remote(piece(u, own), piece(u, own), zs.at[u, r], zr.at[u], me.along_z(r))

    def x_copy(u, lanes, kind, to):
        return remote(piece(u, lanes), piece(u, lanes), xs.at[kind, u], xr.at[kind, u], to)

    def d_copy(u, x_hi, lanes):
        return remote(piece(u, lanes), piece(u, lanes), ds.at[x_hi, u], dr.at[x_hi, u], me.other_core())

    def push(u, slot, z):
        @pl.when(z == me.z)
        def _():
            for r in (1, 7, 2, 6, 3, 5, 4):
                z_copy(u, r).start()

    each_unit(me, push, None)

    cot_copies = []
    cot_lanes = lanes_at(y * TOK, TOK)
    for r in range(1, NY):
        to = (y + r) % NY
        c = remote(cot_ref.at[rows_at(to * QW, QW), :], cots.at[:, cot_lanes], cs.at[r], cr.at[r], me.along_y(r))
        c.start()
        cot_copies.append(c)
    cots[:, cot_lanes] = cot_ref[rows_at(y * QW, QW), :]

    def spread_x(u, slot, z):
        pl.when(z != me.z)(lambda: z_copy(u, 1).wait_recv())
        x_copy(u, own, 0, right).start()
        x_copy(u, own, 1, left).start()
        d_copy(u, me.x_hi, own).start()

    each_unit(me, spread_x, None)

    half = TOK // 2
    from_down = rows_at(((y + 3) % NY) * TOK, half)
    from_up = rows_at(((y + 1) % NY) * TOK + half, half)
    n_up.wait_recv()
    f_up = remote(nall.at[from_down, :], nall.at[from_down, :], ns.at[2], nr.at[2], up)
    f_up.start()
    n_down.wait_recv()
    f_down = remote(nall.at[from_up, :], nall.at[from_up, :], ns.at[3], nr.at[3], down)
    f_down.start()

    def relay(u):
        x_copy(u, of_left, 0, right).wait_recv()
        pl.when(u % 2 == 0)(lambda: x_copy(u, of_left, 2, right).start())
        d_copy(u, hi_left, of_left).start()
        x_copy(u, of_right, 1, left).wait_recv()
        pl.when(u % 2 == 1)(lambda: x_copy(u, of_right, 2, left).start())
        d_copy(u, hi_right, of_right).start()

    each_unit(me, None, relay)

    def last(u, slot, z):
        x_copy(u, far, 2, right).wait_recv()
        d_copy(u, 1 - me.x_hi, far).start()

    each_unit(me, last, None)

    def drain(u, carry):
        for x_hi in range(2):
            lanes = lanes_at((x_hi * 2 + 1 - me.core) * GW, GW)
            d_copy(u, x_hi, lanes).wait_recv()
        return carry

    lax.fori_loop(0, UNITS, drain, 0)
    for p in range(3 * OWN):
        row = wire_row(p)
        w_out[p * HEAD : (p + 1) * HEAD, :] = wall[row : row + HEAD, :]
    f_up.wait_recv()
    f_down.wait_recv()
    for c in cot_copies:
        c.wait_recv()

    def sent_here(u, slot, z):
        @pl.when(z == me.z)
        def _():
            for r in range(1, NZ):
                z_copy(u, r).wait_send()

        x_copy(u, own, 0, right).wait_send()
        x_copy(u, own, 1, left).wait_send()

    def sent_there(u):
        x_copy(u, own, 2, right).wait_send()

    each_unit(me, sent_here, sent_there)

    def sent_core(u, carry):
        for x_hi in range(2):
            d_copy(u, x_hi, own).wait_send()
        return carry

    lax.fori_loop(0, UNITS, sent_core, 0)
    for j in range(SHARD):
        to, _ = shard_unit(me, j)
        pl.when(to != y)(lambda: y_copy(j, to).wait_send())
    for c in cot_copies + [n_up, n_down, f_up, f_down]:
        c.wait_send()


def dma(*shape):
    return pltpu.SemaphoreType.DMA(shape)


def gather(x, gain, w, cot):
    return pl.pallas_call(
        gather_kernel,
        out_shape=(
            jax.ShapeDtypeStruct((ROWS, D), BF),
            jax.ShapeDtypeStruct((PW, D), BF),
            jax.ShapeDtypeStruct((QW, ROWS), BF),
        ),
        in_specs=[VMEM] * 4,
        out_specs=(VMEM,) * 3,
        scratch_shapes=[
            pltpu.VMEM((PW, D), BF),
            pltpu.VMEM((NY, SHARD, UNIT, 128), BF),
            dma(4), dma(4), dma(4), dma(4), dma(3), dma(3, 4), dma(12, 8), dma(12),
            dma(3, 12), dma(3, 12), dma(2, 12), dma(2, 12),
        ],
        compiler_params=pltpu.CompilerParams(
            collective_id=0, has_side_effects=True, vmem_limit_bytes=48 * 2**20
        ),
        name="gather",
    )(x, gain, w, cot)


CHUNK = 256
STEPS = SEQ // CHUNK


def attention_kernel(q_ref, kv_ref, cot_ref, dq_ref, out_ref, ctx_out,
                     kvall, dkv, ctx_own, s_buf, e_buf, r1, mid, r2,
                     ks, kr, ss, rs, cs, cr):
    me = Place()
    y = me.y
    ready = greet([me.far(), me.other_core()] + [me.along_y(r) for r in range(1, NY)])
    own = rows_at(me.group * ROWS, ROWS)
    far = rows_at(me.far_group * ROWS, ROWS)
    own_there = rows_at((me.x_hi * 2 + 1 - me.core) * ROWS, ROWS)
    far_there = rows_at(((1 - me.x_hi) * 2 + 1 - me.core) * ROWS, ROWS)
    mine = y * QW
    ready()
    sent = []

    def go(*args):
        c = remote(*args)
        c.start()
        sent.append(c)
        return c

    def head_lanes(h):
        return slice(h * 128, (h + 1) * 128)

    k_far = [go(kv_ref.at[:, head_lanes(h)], kvall.at[own, head_lanes(h)], ks.at[0, h], kr.at[0, h], me.far()) for h in range(OWN)]
    k_core = [go(kv_ref.at[:, head_lanes(h)], kvall.at[own, head_lanes(h)], ks.at[1, h], kr.at[1, h], me.other_core()) for h in range(OWN)]
    k_pass = []
    kvall[own, :] = kv_ref[...]
    d_far, d_own, d_x, ctx_copies = [], [], [], []

    def pass_keys(h):
        k_far[h].wait_recv()
        k_pass.append(go(kvall.at[far, head_lanes(h)], kvall.at[far, head_lanes(h)], ks.at[2, h], kr.at[2, h], me.other_core()))

    def pass_sums(h):
        lanes = head_lanes(h)
        d_far[h].wait_recv()
        mid[:, lanes] = (dkv[far, lanes].astype(F32) + r1[0, :, lanes].astype(F32)).astype(BF)
        d_x.append(go(mid.at[:, lanes], r2.at[:, lanes], ss.at[2, h], rs.at[2, h], me.far()))

    def finish(h):
        lanes = head_lanes(h)
        d_own[h].wait_recv()
        d_x[h].wait_recv()
        out_ref[:, lanes] = (
            dkv[own, lanes].astype(F32) + r1[1, :, lanes].astype(F32) + r2[:, lanes].astype(F32)
        ).astype(BF)

    pass_keys(0)
    zeros = jnp.zeros((HEAD, ROWS), BF)
    for h in range(OWN):
        lanes = head_lanes(h)
        head_rows = slice(h * HEAD, (h + 1) * HEAD)
        q = q_ref[head_rows, :] * jnp.asarray(HEAD**-0.5, BF)
        q_pad = jnp.concatenate([q, zeros], axis=0)
        k_core[h].wait_recv()
        k_pass[h].wait_recv()
        top = jnp.full((8, ROWS), -jnp.inf, F32)
        for i in range(STEPS):
            rows = slice(i * CHUNK, (i + 1) * CHUNK)
            s = jnp.dot(kvall[rows, lanes], q_pad, preferred_element_type=F32)
            s_buf[rows, :] = s
            top = jnp.maximum(top, jnp.max(s.reshape(CHUNK // 8, 8, ROWS), axis=0))
        top = jnp.max(top, axis=0, keepdims=True)
        total = jnp.zeros((8, ROWS), F32)
        ctx = jnp.zeros((HEAD, ROWS), F32)
        for i in range(STEPS):
            rows = slice(i * CHUNK, (i + 1) * CHUNK)
            e = jnp.exp(s_buf[rows, :] - top)
            total = total + jnp.sum(e.reshape(CHUNK // 8, 8, ROWS), axis=0)
            e_low = e.astype(BF)
            e_buf[rows, :] = e_low
            v_t = kvall[rows, lanes].T[HEAD:, :]
            ctx = ctx + jnp.dot(v_t, e_low, preferred_element_type=F32)
        inverse = 1.0 / jnp.sum(total, axis=0, keepdims=True)
        ctx = ctx * inverse
        ctx_own[head_rows, :] = ctx.astype(BF)
        rows_there = rows_at(mine + h * HEAD, HEAD)
        for r in range(1, NY):
            to = lanes_at(((y + r) % NY) * TOK, TOK)
            ctx_copies.append(go(ctx_own.at[head_rows, to], ctx_out.at[rows_there, :], cs.at[h, r], cr.at[h, r], me.along_y(r)))
        ctx_out[rows_there, :] = ctx_own[head_rows, lanes_at(y * TOK, TOK)]
        if h + 1 < OWN:
            pass_keys(h + 1)
        if h > 0:
            pass_sums(h - 1)
        cot = (cot_ref[head_rows, :].astype(F32) * inverse).astype(BF)
        row_dot = jnp.sum(cot.astype(F32) * ctx, axis=0, keepdims=True)
        cot_pad = jnp.concatenate([zeros, cot], axis=0)
        q_side = q_pad.T
        cot_side = cot_pad.T
        dq = jnp.zeros((HEAD, ROWS), F32)
        for i in range(STEPS):
            rows = slice(i * CHUNK, (i + 1) * CHUNK)
            d_attn = jnp.dot(kvall[rows, lanes], cot_pad, preferred_element_type=F32)
            e_low = e_buf[rows, :]
            slopes = (e_low.astype(F32) * (d_attn - row_dot)).astype(BF)
            k_t = kvall[rows, lanes].T[:HEAD, :]
            dq = dq + jnp.dot(k_t, slopes, preferred_element_type=F32)
            dkv[rows, lanes] = (
                jnp.dot(slopes, q_side, preferred_element_type=F32)
                + jnp.dot(e_low, cot_side, preferred_element_type=F32)
            ).astype(BF)
        dq_ref[head_rows, :] = (dq * HEAD**-0.5).astype(BF)
        d_far.append(go(dkv.at[far_there, lanes], r1.at[0, :, lanes], ss.at[0, h], rs.at[0, h], me.other_core()))
        d_own.append(go(dkv.at[own_there, lanes], r1.at[1, :, lanes], ss.at[1, h], rs.at[1, h], me.other_core()))
    pass_sums(OWN - 1)
    for h in range(OWN):
        finish(h)
    for c in ctx_copies:
        c.wait_recv()
    for c in sent:
        c.wait_send()


def attend(q, kv, cot):
    return pl.pallas_call(
        attention_kernel,
        out_shape=(
            jax.ShapeDtypeStruct((QW, ROWS), BF),
            jax.ShapeDtypeStruct((ROWS, 2 * QW), BF),
            jax.ShapeDtypeStruct((NY * QW, TOK), BF),
        ),
        in_specs=[VMEM] * 3,
        out_specs=(VMEM,) * 3,
        scratch_shapes=[
            pltpu.VMEM((SEQ, 2 * QW), BF),
            pltpu.VMEM((SEQ, 2 * QW), BF),
            pltpu.VMEM((QW, ROWS), BF),
            pltpu.VMEM((SEQ, ROWS), F32),
            pltpu.VMEM((SEQ, ROWS), BF),
            pltpu.VMEM((2, ROWS, 2 * QW), BF),
            pltpu.VMEM((ROWS, 2 * QW), BF),
            pltpu.VMEM((ROWS, 2 * QW), BF),
            dma(3, 3), dma(3, 3), dma(3, 3), dma(3, 3), dma(3, 4), dma(3, 4),
        ],
        compiler_params=pltpu.CompilerParams(
            collective_id=1, has_side_effects=True, vmem_limit_bytes=48 * 2**20
        ),
        name="attention",
    )(q, kv, cot)


def sums_kernel(dn_ref, wg_ref, gg_ref, x_ref, gain_ref, dx_ref, wout_ref, gout_ref,
                half_r, to_up, to_down, full_r, s1, wr1, wr2, mid, zout, zbuf, yout,
                gcore, gy, gx, gz,
                ns, nr, ws, wr, xs, xr, zs, zr, ys, yr, gs, gr):
    me = Place()
    y = me.y
    right, left = me.along_x(1), me.along_x(3)
    x_at = me.x_hi * 2 + me.x_lo
    hi_left, hi_right = ((x_at + 3) % 4) // 2, ((x_at + 1) % 4) // 2
    partners = (
        [me.along_z(r) for r in range(1, NZ)]
        + [me.along_y(r) for r in range(1, NY)]
        + [me.along_x(r) for r in range(1, 4)]
        + [me.other_core()]
    )
    ready = greet(partners)
    ready()
    sent = []

    def go(*args):
        c = remote(*args)
        c.start()
        sent.append(c)
        return c

    part = PW // 4
    w_core = []
    for k in range(4):
        rows = pl.ds(k * part, part)
        for x_hi in range(2):
            there = lanes_at((x_hi * 2 + 1 - me.core) * GW, GW)
            w_core.append(go(wg_ref.at[rows, there], wr1.at[x_hi, rows, :], ws.at[x_hi, k], wr.at[x_hi, k], me.other_core()))
    half = TOK // 2
    up, down = me.along_y(1), me.along_y(3)
    opposite = ((y + 2) % NY) * TOK
    h_up = go(dn_ref.at[rows_at(opposite, half), :], half_r.at[0], ns.at[0], nr.at[0], up)
    h_down = go(dn_ref.at[rows_at(opposite + half, half), :], half_r.at[1], ns.at[1], nr.at[1], down)
    gcore[me.core] = gg_ref[...]
    g_core = go(gg_ref, gcore.at[me.core], gs.at[0], gr.at[0], me.other_core())

    def x_copy(u, src, dst, kind, to):
        return remote(src, dst, xs.at[kind, u], xr.at[kind, u], to)

    def to_opposite(u, slot, z):
        src = s1.at[1 - me.x_hi, unit_rows(u), :]
        dst = wr2.at[0, unit_rows(u), :]
        pl.when(u % 2 == 0)(lambda: x_copy(u, src, dst, 0, right).start())
        pl.when(u % 2 == 1)(lambda: x_copy(u, src, dst, 0, left).start())

    for k in range(4):
        rows = slice(k * part, (k + 1) * part)
        for x_hi in range(2):
            w_core[2 * k + x_hi].wait_recv()
            here = lanes_at((x_hi * 2 + me.core) * GW, GW)
            s1[x_hi, rows, :] = (wg_ref[rows, here].astype(F32) + wr1[x_hi, rows, :].astype(F32)).astype(BF)

        def first(u, carry):
            _, x_lo, _ = unit_home(u, y)
            pl.when(x_lo == me.x_lo)(lambda: to_opposite(u, 0, 0))
            return carry

        lax.fori_loop(k * SHARD, (k + 1) * SHARD, first, 0)

    g_core.wait_recv()
    gy[y] = gcore[0] + gcore[1]
    g_y = [go(gy.at[y], gy.at[y], gs.at[r], gr.at[r], me.along_y(r)) for r in range(1, NY)]

    def pass_on(u):
        rows = unit_rows(u)
        pl.when(u % 2 == 0)(lambda: x_copy(u, s1.at[hi_left, rows, :], wr2.at[2, rows, :], 2, left).start())
        pl.when(u % 2 == 1)(lambda: x_copy(u, s1.at[hi_right, rows, :], wr2.at[1, rows, :], 1, right).start())
        x_copy(u, s1.at[0, rows, :], wr2.at[0, rows, :], 0, right).wait_recv()

        @pl.when(u % 2 == 0)
        def _():
            mid[rows, :] = (s1[hi_right, rows, :].astype(F32) + wr2[0, rows, :].astype(F32)).astype(BF)
            x_copy(u, mid.at[rows, :], wr2.at[1, rows, :], 1, right).start()

        @pl.when(u % 2 == 1)
        def _():
            mid[rows, :] = (s1[hi_left, rows, :].astype(F32) + wr2[0, rows, :].astype(F32)).astype(BF)
            x_copy(u, mid.at[rows, :], wr2.at[2, rows, :], 2, left).start()

    each_unit(me, None, pass_on)

    h_up.wait_recv()
    block = rows_at(((y + 1) % NY) * TOK, half)
    rest = rows_at(((y + 1) % NY) * TOK + half, half)
    to_up[:half, :] = (dn_ref[block, :].astype(F32) + half_r[0].astype(F32)).astype(BF)
    to_up[half:, :] = dn_ref[rest, :]
    f_up = go(to_up, full_r.at[0], ns.at[2], nr.at[2], up)
    h_down.wait_recv()
    block = rows_at(((y + 3) % NY) * TOK, half)
    rest = rows_at(((y + 3) % NY) * TOK + half, half)
    to_down[:half, :] = dn_ref[block, :]
    to_down[half:, :] = (dn_ref[rest, :].astype(F32) + half_r[1].astype(F32)).astype(BF)
    f_down = go(to_down, full_r.at[1], ns.at[3], nr.at[3], down)

    def z_copy(u, slot, z):
        distance = (z + NZ - me.z) % NZ
        return remote(
            zout.at[unit_rows(u), :], zbuf.at[slot, distance], zs.at[u], zr.at[slot, distance],
            me.id(z=z),
        )

    def over_x(u, slot, z):
        rows = unit_rows(u)
        x_copy(u, s1.at[0, rows, :], wr2.at[1, rows, :], 1, right).wait_recv()
        x_copy(u, s1.at[0, rows, :], wr2.at[2, rows, :], 2, left).wait_recv()
        zout[rows, :] = (
            s1[me.x_hi, rows, :].astype(F32) + wr2[1, rows, :].astype(F32) + wr2[2, rows, :].astype(F32)
        ).astype(BF)
        pl.when(z != me.z)(lambda: z_copy(u, slot, z).start())

    each_unit(me, over_x, None)

    for c in g_y:
        c.wait_recv()
    gx[x_at] = gy[0] + gy[1] + gy[2] + gy[3]
    g_x = [go(gx.at[x_at], gx.at[x_at], gs.at[3 + r], gr.at[3 + r], me.along_x(r)) for r in range(1, 4)]

    x = x_ref[...].astype(F32)
    centred = x - jnp.mean(x, axis=1, keepdims=True)
    spread = jnp.mean(centred * centred, axis=1, keepdims=True)
    scale = lax.rsqrt(spread + EPS)
    hat = centred * scale
    f_up.wait_recv()
    f_down.wait_recv()
    d_normed = (
        dn_ref[rows_at(y * TOK, TOK), :].astype(F32) + full_r[0].astype(F32) + full_r[1].astype(F32)
    )
    inner = to_natural(d_normed) * gain_ref[...]
    first_mean = jnp.mean(inner, axis=1, keepdims=True)
    second = jnp.mean(inner * hat, axis=1, keepdims=True)
    dx_ref[...] = (scale * (inner - first_mean - hat * second)).astype(BF)

    for c in g_x:
        c.wait_recv()
    gz[me.z] = gx[0] + gx[1] + gx[2] + gx[3]
    g_z = [go(gz.at[me.z], gz.at[me.z], gs.at[6 + r], gr.at[6 + r], me.along_z(r)) for r in range(1, NZ)]

    def y_copy(j, to):
        return remote(yout.at[j, to], wout_ref.at[pl.ds(j * UNIT, UNIT), :], ys.at[j, to], yr.at[j], me.id(y=to))

    for j in range(SHARD):
        holder, u = shard_unit(me, j)

        @pl.when(holder == y)
        def _():
            total = zout[unit_rows(u), :].astype(F32)
            for r in range(1, NZ):
                remote(zbuf.at[j, r], zbuf.at[j, r], zs.at[u], zr.at[j, r], me.along_z(r)).wait_recv()
                total = total + zbuf[j, r].astype(F32)
            for k in range(NY):
                rows = total[:, k * SLAB : (k + 1) * SLAB]
                rows = jnp.concatenate([rows, jnp.zeros((UNIT, 128 - SLAB), F32)], axis=1)
                yout[j, k] = rows
            for r in range(1, NY):
                y_copy(j, (y + r) % NY).start()
            wout_ref[j * UNIT : (j + 1) * UNIT, :] = yout[j, y]

    for c in g_z:
        c.wait_recv()
    total = gz[0]
    for k in range(1, NZ):
        total = total + gz[k]
    gout_ref[...] = total

    for j in range(SHARD):
        holder, u = shard_unit(me, j)

        @pl.when(holder != y)
        def _():
            y_copy(j, y).wait_recv()

        @pl.when(holder == y)
        def _():
            for r in range(1, NY):
                y_copy(j, (y + r) % NY).wait_send()

    def sent_here(u, slot, z):
        rows = unit_rows(u)
        x_copy(u, mid.at[rows, :], wr2.at[0, rows, :], 0, right).wait_send()
        pl.when(z != me.z)(lambda: z_copy(u, slot, z).wait_send())

    def sent_there(u):
        rows = unit_rows(u)
        x_copy(u, mid.at[rows, :], wr2.at[1, rows, :], 1, right).wait_send()
        x_copy(u, mid.at[rows, :], wr2.at[2, rows, :], 2, left).wait_send()

    each_unit(me, sent_here, sent_there)
    for c in sent:
        c.wait_send()


def sums(dn, wg, gg, x, gain):
    return pl.pallas_call(
        sums_kernel,
        out_shape=(
            jax.ShapeDtypeStruct((TOK, D), BF),
            jax.ShapeDtypeStruct((BLOCK, 128), F32),
            jax.ShapeDtypeStruct((16, 128), F32),
        ),
        in_specs=[VMEM] * 5,
        out_specs=(VMEM,) * 3,
        scratch_shapes=[
            pltpu.VMEM((2, TOK // 2, D), BF),
            pltpu.VMEM((TOK, D), BF),
            pltpu.VMEM((TOK, D), BF),
            pltpu.VMEM((2, TOK, D), BF),
            pltpu.VMEM((2, PW, GW), BF),
            pltpu.VMEM((2, PW, GW), BF),
            pltpu.VMEM((3, PW, GW), BF),
            pltpu.VMEM((PW, GW), BF),
            pltpu.VMEM((PW, GW), BF),
            pltpu.VMEM((SHARD, NZ, UNIT, GW), BF),
            pltpu.VMEM((SHARD, NY, UNIT, 128), F32),
            pltpu.VMEM((2, 16, 128), F32),
            pltpu.VMEM((NY, 16, 128), F32),
            pltpu.VMEM((4, 16, 128), F32),
            pltpu.VMEM((NZ, 16, 128), F32),
            dma(4), dma(4), dma(2, 4), dma(2, 4), dma(3, 12), dma(3, 12), dma(12), dma(3, 8),
            dma(3, 4), dma(3), dma(14), dma(14),
        ],
        compiler_params=pltpu.CompilerParams(
            collective_id=2, has_side_effects=True, vmem_limit_bytes=48 * 2**20
        ),
        name="sums",
    )(dn, wg, gg, x, gain)


def shards(tokens, norm_gain, qkv_weight, d_context):
    x = tokens[0]
    gain = norm_gain.astype(F32)[None, :]
    w_own = jnp.pad(qkv_weight.T, ((0, 0), (0, 128 - SLAB)))
    normed, weights, cot = gather(x, gain, w_own, d_context[0].T)
    q = lax.dot_general(weights[:QW], normed, (((1,), (1,)), ((), ())), preferred_element_type=F32).astype(BF)
    kv = lax.dot_general(normed, weights[QW:], (((1,), (1,)), ((), ())), preferred_element_type=F32).astype(BF)
    d_query, kv_sums, context = attend(q, kv, cot)
    d_query = d_query.T
    d_proj = jnp.concatenate([d_query, kv_sums], axis=1)
    d_normed = jnp.dot(d_proj, weights, preferred_element_type=F32)
    gain_terms = jnp.sum(d_normed * normed.astype(F32), axis=0)
    by_head = [kv_sums[:, h * HEAD : (h + 1) * HEAD] for h in (0, 2, 4, 1, 3, 5)]
    d_proj = jnp.concatenate([d_query] + by_head, axis=1)
    grad = lax.dot_general(d_proj, normed, (((0,), (0,)), ((), ())), preferred_element_type=F32)
    gain_terms = jnp.pad(gain_terms.reshape(12, 128), ((0, 4), (0, 0)))
    d_tokens, weight_sums, gain_sums = sums(d_normed.astype(BF), grad.astype(BF), gain_terms, x, gain)
    factor = 1.0 / math.sqrt(16 * SEQ)
    weight_grad = weight_sums[:, :SLAB].T * factor
    gain_grad = gain_sums[:12].reshape(2, 2, NY, SLAB).transpose(0, 2, 1, 3).reshape(D)
    gain_grad = gain_grad / norm_gain.astype(F32) * factor
    return (context.T[None], d_tokens[None], weight_grad, gain_grad)


def solution(mesh):
    in_specs = (P("dp", "sp", None), P(), P("sp", "dp"), P("dp", "sp", None))
    out_specs = (P("dp", "sp", None), P("dp", "sp", None), P("sp", "dp"), P())
    return jax.shard_map(shards, mesh=mesh, in_specs=in_specs, out_specs=out_specs, check_vma=False)
```

```python
import functools
import math

import jax
import jax.numpy as jnp
from jax import lax
from jax.experimental import pallas as pl
from jax.experimental.pallas import tpu as pltpu
from jax.sharding import PartitionSpec as P

MESH = pl.DeviceIdType.MESH
BF = jnp.bfloat16
F32 = jnp.float32

D = 1536
HEAD = 64
OWN = 3
TOK = 128
NY = 4
NZ = 8
NA = 4
ROWS = NY * TOK
SEQ = NA * ROWS
QW = OWN * HEAD
PW = 3 * QW
SLAB = 96
BLOCK = 144
GW = NY * SLAB
EPS = 1e-05
VMEM = pl.BlockSpec(memory_space=pltpu.VMEM)


class Place:
    def __init__(self):
        d, s = lax.axis_index("dp"), lax.axis_index("sp")
        self.x_lo, self.z = d // NZ, d % NZ
        self.x_hi, self.y, self.core = s // 8, (s // 2) % NY, s % 2
        self.group = self.x_hi * 2 + self.core
        self.far_group = (1 - self.x_hi) * 2 + self.core

    def id(self, x_hi=None, x_lo=None, y=None, z=None, core=None):
        x_hi = self.x_hi if x_hi is None else x_hi
        x_lo = self.x_lo if x_lo is None else x_lo
        y = self.y if y is None else y
        z = self.z if z is None else z
        core = self.core if core is None else core
        return {"dp": x_lo * NZ + z, "sp": x_hi * 8 + y * 2 + core}

    def other_core(self):
        return self.id(core=1 - self.core)

    def mirror(self):
        return self.id(x_hi=1 - self.x_hi, x_lo=1 - self.x_lo)

    def beside(self):
        return self.id(x_lo=1 - self.x_lo)

    def far(self):
        return self.id(x_hi=1 - self.x_hi)

    def along_y(self, step):
        return self.id(y=(self.y + step) % NY)

    def along_z(self, step):
        return self.id(z=(self.z + step) % NZ)

    def along_x(self, step):
        x = (self.x_hi * 2 + self.x_lo + step) % 4
        return self.id(x_hi=x // 2, x_lo=x % 2)


def greet(partners):
    barrier = pltpu.get_barrier_semaphore()
    for partner in partners:
        pl.semaphore_signal(barrier, inc=1, device_id=partner, device_id_type=MESH)
    return functools.partial(pl.semaphore_wait, barrier, len(partners))


def remote(src, dst, send, recv, partner):
    return pltpu.make_async_remote_copy(
        src_ref=src, dst_ref=dst, send_sem=send, recv_sem=recv, device_id=partner, device_id_type=MESH
    )


def rows_at(start, size):
    return pl.ds(pl.multiple_of(start, 16), size)


def lanes_at(start, size):
    return pl.ds(pl.multiple_of(start, 128), size)


def to_grouped(wide):
    parts = []
    for x_hi in range(2):
        for core in range(2):
            for y in range(NY):
                s = x_hi * 8 + y * 2 + core
                parts.append(wide[:, s * SLAB : (s + 1) * SLAB])
    return jnp.concatenate(parts, axis=1)


def to_natural(wide):
    parts = []
    for x_hi in range(2):
        for y in range(NY):
            for core in range(2):
                s = (x_hi * 2 + core) * NY + y
                parts.append(wide[:, s * SLAB : (s + 1) * SLAB])
    return jnp.concatenate(parts, axis=1)


UNIT = 48
UNITS = 12
SHARD = 3


def unit_home(u, y):
    column = (u // 4) * 16 + 4 * y + u % 4
    d = column // SHARD
    return column - SHARD * d, d // NZ, d % NZ


def shard_unit(me, j):
    column = (me.x_lo * NZ + me.z) * SHARD + j
    return (column % 16) // 4, (column // 16) * 4 + column % 4


ALL = ((0, UNITS),)


def each_unit(me, here, there, spans=ALL):
    def step(u, carry):
        slot, x_lo, z = unit_home(u, me.y)
        if here is not None:
            pl.when(x_lo == me.x_lo)(lambda: here(u, slot, z))
        if there is not None:
            pl.when(x_lo != me.x_lo)(lambda: there(u))
        return carry

    for first, end in spans:
        lax.fori_loop(first, end, step, 0)


def unit_rows(u):
    return rows_at(u * UNIT, UNIT)


def gather_phase(me, ready, load, x_ref, gain_ref, w_ref, cot_ref, nall, wall, cots,
                 cot_t, ybuf, ns, nr, cs, cr, ys, yr, zs, zr, xs, xr, ds, dr):
    y = me.y
    right, left = me.along_x(1), me.along_x(3)
    x_at = me.x_hi * 2 + me.x_lo
    own = lanes_at(me.group * GW, GW)
    far = lanes_at(me.far_group * GW, GW)
    hi_left, hi_right = ((x_at + 3) % 4) // 2, ((x_at + 1) % 4) // 2
    of_left = lanes_at((hi_left * 2 + me.core) * GW, GW)
    of_right = lanes_at((hi_right * 2 + me.core) * GW, GW)
    load(w_ref)
    ready()

    def y_copy(j, to):
        return remote(w_ref.at[pl.ds(j * UNIT, UNIT), :], ybuf.at[y, j], ys.at[j], yr.at[j, y], me.id(y=to))

    for j in range(SHARD):
        to, _ = shard_unit(me, j)
        pl.when(to != y)(lambda: y_copy(j, to).start())

    load(x_ref)
    load(gain_ref)
    x = x_ref[...].astype(F32)
    centred = x - jnp.mean(x, axis=1, keepdims=True)
    spread = jnp.mean(centred * centred, axis=1, keepdims=True)
    normed = centred * lax.rsqrt(spread + EPS) * gain_ref[...].astype(F32)
    tok_rows = rows_at(y * TOK, TOK)
    nall[tok_rows, :] = to_grouped(normed).astype(BF)
    up, down = me.along_y(1), me.along_y(3)
    n_up = remote(nall.at[tok_rows, :], nall.at[tok_rows, :], ns.at[0], nr.at[0], up)
    n_down = remote(nall.at[tok_rows, :], nall.at[tok_rows, :], ns.at[1], nr.at[1], down)
    n_up.start()
    n_down.start()

    for j in range(SHARD):
        to, u = shard_unit(me, j)

        @pl.when(to == y)
        def _():
            ybuf[y, j] = w_ref[j * UNIT : (j + 1) * UNIT, :]
            for r in range(1, NY):
                k = (y + r) % NY
                remote(ybuf.at[k, j], ybuf.at[k, j], ys.at[j], yr.at[j, k], me.along_y(r)).wait_recv()
            parts = [ybuf[k, j][:, :SLAB].astype(F32) for k in range(NY)]
            wall[unit_rows(u), own] = jnp.concatenate(parts, axis=1).astype(BF)

    def piece(u, lanes):
        return wall.at[unit_rows(u), lanes]

    def z_copy(u, r):
        return remote(piece(u, own), piece(u, own), zs.at[u, r], zr.at[u], me.along_z(r))

    def x_copy(u, lanes, kind, to):
        return remote(piece(u, lanes), piece(u, lanes), xs.at[kind, u], xr.at[kind, u], to)

    def push(u, slot, z):
        @pl.when(z == me.z)
        def _():
            for r in (1, 7, 2, 6, 3, 5, 4):
                z_copy(u, r).start()

    each_unit(me, push, None)

    cot_copies = []
    load(cot_ref)
    cot_t[...] = cot_ref[...].T
    cot_lanes = lanes_at(y * TOK, TOK)
    for r in range(1, NY):
        to = (y + r) % NY
        c = remote(cot_t.at[rows_at(to * QW, QW), :], cots.at[:, cot_lanes], cs.at[r], cr.at[r], me.along_y(r))
        c.start()
        cot_copies.append(c)
    cots[:, cot_lanes] = cot_t[rows_at(y * QW, QW), :]

    def spread_x(u, slot, z):
        pl.when(z != me.z)(lambda: z_copy(u, 1).wait_recv())
        x_copy(u, own, 0, right).start()
        x_copy(u, own, 1, left).start()

    each_unit(me, spread_x, None)

    half = TOK // 2
    from_down = rows_at(((y + 3) % NY) * TOK, half)
    from_up = rows_at(((y + 1) % NY) * TOK + half, half)
    n_up.wait_recv()
    f_up = remote(nall.at[from_down, :], nall.at[from_down, :], ns.at[2], nr.at[2], up)
    f_up.start()
    n_down.wait_recv()
    f_down = remote(nall.at[from_up, :], nall.at[from_up, :], ns.at[3], nr.at[3], down)
    f_down.start()

    def relay(u):
        x_copy(u, of_left, 0, right).wait_recv()
        pl.when(u % 2 == 0)(lambda: x_copy(u, of_left, 2, right).start())
        x_copy(u, of_right, 1, left).wait_recv()
        pl.when(u % 2 == 1)(lambda: x_copy(u, of_right, 2, left).start())

    each_unit(me, None, relay)

    def last(u, slot, z):
        x_copy(u, far, 2, right).wait_recv()

    each_unit(me, last, None)

    core_copies = []
    for x_hi in range(2):
        lanes = lanes_at((x_hi * 2 + me.core) * GW, GW)
        c = remote(wall.at[:, lanes], wall.at[:, lanes], ds.at[x_hi], dr.at[x_hi], me.other_core())
        c.start()
        core_copies.append(c)
    for c in core_copies:
        c.wait_recv()
    f_up.wait_recv()
    f_down.wait_recv()
    for c in cot_copies:
        c.wait_recv()

    def sent_here(u, slot, z):
        @pl.when(z == me.z)
        def _():
            for r in range(1, NZ):
                z_copy(u, r).wait_send()

        x_copy(u, own, 0, right).wait_send()
        x_copy(u, own, 1, left).wait_send()

    def sent_there(u):
        x_copy(u, own, 2, right).wait_send()

    each_unit(me, sent_here, sent_there)

    for j in range(SHARD):
        to, _ = shard_unit(me, j)
        pl.when(to != y)(lambda: y_copy(j, to).wait_send())
    for c in cot_copies + core_copies + [n_up, n_down, f_up, f_down]:
        c.wait_send()


def dma(*shape):
    return pltpu.SemaphoreType.DMA(shape)


FACTOR = 1.0 / math.sqrt(16 * SEQ)
CHUNK = 256
STEPS = SEQ // CHUNK
EARLY = ((0, 6), (8, 10))
LATE = ((6, 8), (10, 12))


def block_kernel(x_hbm, gain_hbm, w_hbm, cot_hbm, ctx_ref, dx_ref, wout_ref, gout_ref,
                 x_ref, gain_ref, shard_ref, d_ctx, n_ref, w_ref, cot_ref, cot_t, ybuf, ls,
                 *rest):
    me = Place()
    y = me.y
    partners = (
        [me.along_z(r) for r in range(1, NZ)]
        + [me.along_y(r) for r in range(1, NY)]
        + [me.along_x(r) for r in range(1, 4)]
        + [me.other_core()]
    )
    ready = greet(partners)
    loads = {}
    for k, (src, dst) in enumerate(
        ((w_hbm, shard_ref), (x_hbm, x_ref), (gain_hbm, gain_ref), (cot_hbm, d_ctx))
    ):
        c = pltpu.make_async_copy(src, dst, ls.at[k])
        c.start()
        loads[id(dst)] = c
    gather_phase(
        me, ready, lambda ref: loads[id(ref)].wait(), x_ref, gain_ref, shard_ref, d_ctx,
        n_ref, w_ref, cot_ref, cot_t, ybuf, *rest[:12],
    )
    back_phase(
        me, n_ref, w_ref, cot_ref, x_ref, gain_ref, ctx_ref, dx_ref, wout_ref, gout_ref, *rest[12:]
    )


def back_phase(me, n_ref, w_ref, cot_ref, x_ref, gain_ref, ctx_ref, dx_ref, wout_ref, gout_ref,
               wuse, kvall, dkv, ctx_own, ctx_out, dq_ref, dq_own, out_ref, s_buf, e_buf, r1, mid, r2,
               ks, kr, ss, rs, cs, cr,
               dn_ref, wg_ref, gg_ref, w_sums,
               half_r, to_up, to_down, full_r, s1, wr1, wr2, w_mid, zout, zbuf, yout,
               gcore, gy, gx, gz,
               ns, nr, ws, wr, xs, xr, zs, zr, ys, yr, gs, gr):
    y = me.y
    own = rows_at(me.group * ROWS, ROWS)
    far = rows_at(me.far_group * ROWS, ROWS)
    own_there = rows_at((me.x_hi * 2 + 1 - me.core) * ROWS, ROWS)
    far_there = rows_at(((1 - me.x_hi) * 2 + 1 - me.core) * ROWS, ROWS)
    mine = y * QW
    sent = []

    def go(*args):
        c = remote(*args)
        c.start()
        sent.append(c)
        return c

    def head_lanes(h):
        return slice(h * 128, (h + 1) * 128)

    nt = (((1,), (1,)), ((), ()))
    k_far, k_core = [], []
    for h in range(OWN):
        lanes = head_lanes(h)
        for which in range(2):
            row = QW * (1 + which) + h * HEAD
            wuse[h * 128 + which * HEAD : h * 128 + (which + 1) * HEAD, :] = w_ref[row : row + HEAD, :]
        kvall[own, lanes] = lax.dot_general(n_ref[...], wuse[lanes, :], nt, preferred_element_type=F32).astype(BF)
        k_far.append(go(kvall.at[own, lanes], kvall.at[own, lanes], ks.at[0, h], kr.at[0, h], me.far()))
        k_core.append(go(kvall.at[own, lanes], kvall.at[own, lanes], ks.at[1, h], kr.at[1, h], me.other_core()))
    queries = lax.dot_general(w_ref[:QW, :], n_ref[...], nt, preferred_element_type=F32).astype(BF)
    k_pass = []
    d_far, d_own, d_x, ctx_copies = [], [], [], []

    def pass_keys(h):
        k_far[h].wait_recv()
        k_pass.append(go(kvall.at[far, head_lanes(h)], kvall.at[far, head_lanes(h)], ks.at[2, h], kr.at[2, h], me.other_core()))

    def pass_sums(h):
        lanes = head_lanes(h)
        d_far[h].wait_recv()
        mid[:, lanes] = (dkv[far, lanes].astype(F32) + r1[0, :, lanes].astype(F32)).astype(BF)
        d_x.append(go(mid.at[:, lanes], r2.at[:, lanes], ss.at[2, h], rs.at[2, h], me.far()))

    def finish(h):
        lanes = head_lanes(h)
        d_own[h].wait_recv()
        d_x[h].wait_recv()
        out_ref[:, lanes] = (
            dkv[own, lanes].astype(F32) + r1[1, :, lanes].astype(F32) + r2[:, lanes].astype(F32)
        ).astype(BF)

    pass_keys(0)
    zeros = jnp.zeros((HEAD, ROWS), BF)
    for h in range(OWN):
        lanes = head_lanes(h)
        head_rows = slice(h * HEAD, (h + 1) * HEAD)
        q = queries[head_rows, :] * jnp.asarray(HEAD**-0.5, BF)
        q_pad = jnp.concatenate([q, zeros], axis=0)
        k_core[h].wait_recv()
        k_pass[h].wait_recv()
        top = jnp.full((8, ROWS), -jnp.inf, F32)
        for i in range(STEPS):
            rows = slice(i * CHUNK, (i + 1) * CHUNK)
            s = jnp.dot(kvall[rows, lanes], q_pad, preferred_element_type=F32)
            s_buf[rows, :] = s
            top = jnp.maximum(top, jnp.max(s.reshape(CHUNK // 8, 8, ROWS), axis=0))
        top = jnp.max(top, axis=0, keepdims=True)
        total = jnp.zeros((8, ROWS), F32)
        ctx = jnp.zeros((HEAD, ROWS), F32)
        for i in range(STEPS):
            rows = slice(i * CHUNK, (i + 1) * CHUNK)
            e = jnp.exp(s_buf[rows, :] - top)
            total = total + jnp.sum(e.reshape(CHUNK // 8, 8, ROWS), axis=0)
            e_low = e.astype(BF)
            e_buf[rows, :] = e_low
            v_t = kvall[rows, lanes].T[HEAD:, :]
            ctx = ctx + jnp.dot(v_t, e_low, preferred_element_type=F32)
        inverse = 1.0 / jnp.sum(total, axis=0, keepdims=True)
        ctx = ctx * inverse
        ctx_own[head_rows, :] = ctx.astype(BF)
        rows_there = rows_at(mine + h * HEAD, HEAD)
        for r in range(1, NY):
            to = lanes_at(((y + r) % NY) * TOK, TOK)
            ctx_copies.append(go(ctx_own.at[head_rows, to], ctx_out.at[rows_there, :], cs.at[h, r], cr.at[h, r], me.along_y(r)))
        ctx_out[rows_there, :] = ctx_own[head_rows, lanes_at(y * TOK, TOK)]
        if h + 1 < OWN:
            pass_keys(h + 1)
        if h > 0:
            pass_sums(h - 1)
        cot = (cot_ref[head_rows, :].astype(F32) * inverse).astype(BF)
        row_dot = jnp.sum(cot.astype(F32) * ctx, axis=0, keepdims=True)
        cot_pad = jnp.concatenate([zeros, cot], axis=0)
        q_side = q_pad.T
        cot_side = cot_pad.T
        dq = jnp.zeros((HEAD, ROWS), F32)
        for i in range(STEPS):
            rows = slice(i * CHUNK, (i + 1) * CHUNK)
            d_attn = jnp.dot(kvall[rows, lanes], cot_pad, preferred_element_type=F32)
            e_low = e_buf[rows, :]
            slopes = (e_low.astype(F32) * (d_attn - row_dot)).astype(BF)
            k_t = kvall[rows, lanes].T[:HEAD, :]
            dq = dq + jnp.dot(k_t, slopes, preferred_element_type=F32)
            dkv[rows, lanes] = (
                jnp.dot(slopes, q_side, preferred_element_type=F32)
                + jnp.dot(e_low, cot_side, preferred_element_type=F32)
            ).astype(BF)
        dq_ref[head_rows, :] = (dq * HEAD**-0.5).astype(BF)
        d_far.append(go(dkv.at[far_there, lanes], r1.at[0, :, lanes], ss.at[0, h], rs.at[0, h], me.other_core()))
        d_own.append(go(dkv.at[own_there, lanes], r1.at[1, :, lanes], ss.at[1, h], rs.at[1, h], me.other_core()))
    right, left = me.along_x(1), me.along_x(3)
    x_at = me.x_hi * 2 + me.x_lo
    hi_left, hi_right = ((x_at + 3) % 4) // 2, ((x_at + 1) % 4) // 2
    half = TOK // 2
    up, down = me.along_y(1), me.along_y(3)
    opposite = (y + 2) % NY

    def weight_rows(h):
        rows = jnp.dot(out_ref[:, head_lanes(h)].T, n_ref[...], preferred_element_type=F32).astype(BF)
        for which in range(2):
            row = QW * (1 + which) + h * HEAD
            wg_ref[row : row + HEAD, :] = rows[which * HEAD : (which + 1) * HEAD, :]

    w_core = []

    def to_core(first, size):
        rows = pl.ds(first, size)
        k = len(w_core) // 2
        for x_hi in range(2):
            there = lanes_at((x_hi * 2 + 1 - me.core) * GW, GW)
            w_core.append(go(wg_ref.at[rows, there], wr1.at[x_hi, rows, :], ws.at[x_hi, k], wr.at[x_hi, k], me.other_core()))

    def from_core(k, first, size):
        rows = slice(first, first + size)
        for x_hi in range(2):
            w_core[2 * k + x_hi].wait_recv()
            here = lanes_at((x_hi * 2 + me.core) * GW, GW)
            s1[x_hi, rows, :] = (wg_ref[rows, here].astype(F32) + wr1[x_hi, rows, :].astype(F32)).astype(BF)

    def x_copy(u, src, dst, kind, to):
        return remote(src, dst, xs.at[kind, u], xr.at[kind, u], to)

    def to_opposite(u, slot, z):
        src = s1.at[1 - me.x_hi, unit_rows(u), :]
        dst = wr2.at[0, unit_rows(u), :]
        pl.when(u % 2 == 0)(lambda: x_copy(u, src, dst, 0, right).start())
        pl.when(u % 2 == 1)(lambda: x_copy(u, src, dst, 0, left).start())

    def pass_on(u):
        rows = unit_rows(u)
        pl.when(u % 2 == 0)(lambda: x_copy(u, s1.at[hi_left, rows, :], wr2.at[2, rows, :], 2, left).start())
        pl.when(u % 2 == 1)(lambda: x_copy(u, s1.at[hi_right, rows, :], wr2.at[1, rows, :], 1, right).start())
        x_copy(u, s1.at[0, rows, :], wr2.at[0, rows, :], 0, right).wait_recv()

        @pl.when(u % 2 == 0)
        def _():
            w_mid[rows, :] = (s1[hi_right, rows, :].astype(F32) + wr2[0, rows, :].astype(F32)).astype(BF)
            x_copy(u, w_mid.at[rows, :], wr2.at[1, rows, :], 1, right).start()

        @pl.when(u % 2 == 1)
        def _():
            w_mid[rows, :] = (s1[hi_left, rows, :].astype(F32) + wr2[0, rows, :].astype(F32)).astype(BF)
            x_copy(u, w_mid.at[rows, :], wr2.at[2, rows, :], 2, left).start()


    def z_copy(u, slot, z):
        distance = (z + NZ - me.z) % NZ
        return remote(
            zout.at[unit_rows(u), :], zbuf.at[slot, distance], zs.at[u], zr.at[slot, distance],
            me.id(z=z),
        )

    def over_x(u, slot, z):
        rows = unit_rows(u)
        x_copy(u, s1.at[0, rows, :], wr2.at[1, rows, :], 1, right).wait_recv()
        x_copy(u, s1.at[0, rows, :], wr2.at[2, rows, :], 2, left).wait_recv()
        zout[rows, :] = (
            s1[me.x_hi, rows, :].astype(F32) + wr2[1, rows, :].astype(F32) + wr2[2, rows, :].astype(F32)
        ).astype(BF)
        pl.when(z != me.z)(lambda: z_copy(u, slot, z).start())


    wg_ref[:QW, :] = jnp.dot(dq_ref[...], n_ref[...], preferred_element_type=F32).astype(BF)
    pass_sums(OWN - 1)
    for h in range(OWN - 1):
        finish(h)
        weight_rows(h)
    to_core(0, 288)
    to_core(384, 96)
    from_core(0, 0, 288)
    from_core(1, 384, 96)
    each_unit(me, to_opposite, None, EARLY)
    finish(OWN - 1)
    dq_own[...] = dq_ref[...].T
    gain_terms = jnp.zeros((8, D), F32)
    for r in (2, 1, 3, 0):
        at = (y + r) % NY
        rows = rows_at(at * TOK, TOK)
        first_rows = rows_at(at * TOK, half)
        rest_rows = rows_at(at * TOK + half, half)
        part = jnp.dot(dq_own[rows, :], w_ref[:QW, :], preferred_element_type=F32) + jnp.dot(
            out_ref[rows, :], wuse[...], preferred_element_type=F32
        )
        dn_ref[rows, :] = part.astype(BF)
        if r == 2:
            h_up = go(dn_ref.at[first_rows, :], half_r.at[0], ns.at[0], nr.at[0], up)
            h_down = go(dn_ref.at[rest_rows, :], half_r.at[1], ns.at[1], nr.at[1], down)
            weight_rows(OWN - 1)
            to_core(288, 96)
            to_core(480, 96)
        terms = part * n_ref[rows, :].astype(F32)
        gain_terms = gain_terms + jnp.sum(terms.reshape(TOK // 8, 8, D), axis=0)
    gain_terms = jnp.sum(gain_terms, axis=0, keepdims=True)
    gg_ref[...] = jnp.zeros((16, 128), F32)
    for k in range(D // 128):
        gg_ref[k : k + 1, :] = gain_terms[:, k * 128 : (k + 1) * 128]
    gcore[me.core] = gg_ref[...]
    g_core = go(gg_ref, gcore.at[me.core], gs.at[0], gr.at[0], me.other_core())
    from_core(2, 288, 96)
    from_core(3, 480, 96)
    each_unit(me, to_opposite, None, LATE)
    each_unit(me, None, pass_on, EARLY)
    g_core.wait_recv()
    gy[y] = gcore[0] + gcore[1]
    g_y = [go(gy.at[y], gy.at[y], gs.at[r], gr.at[r], me.along_y(r)) for r in range(1, NY)]
    each_unit(me, None, pass_on, LATE)
    each_unit(me, over_x, None, EARLY)
    h_up.wait_recv()
    block = rows_at(((y + 1) % NY) * TOK, half)
    rest = rows_at(((y + 1) % NY) * TOK + half, half)
    to_up[:half, :] = (dn_ref[block, :].astype(F32) + half_r[0].astype(F32)).astype(BF)
    to_up[half:, :] = dn_ref[rest, :]
    f_up = go(to_up, full_r.at[0], ns.at[2], nr.at[2], up)
    h_down.wait_recv()
    block = rows_at(((y + 3) % NY) * TOK, half)
    rest = rows_at(((y + 3) % NY) * TOK + half, half)
    to_down[:half, :] = dn_ref[block, :]
    to_down[half:, :] = (dn_ref[rest, :].astype(F32) + half_r[1].astype(F32)).astype(BF)
    f_down = go(to_down, full_r.at[1], ns.at[3], nr.at[3], down)

    for c in g_y:
        c.wait_recv()
    gx[x_at] = gy[0] + gy[1] + gy[2] + gy[3]
    g_x = [go(gx.at[x_at], gx.at[x_at], gs.at[3 + r], gr.at[3 + r], me.along_x(r)) for r in range(1, 4)]

    each_unit(me, over_x, None, LATE)
    for c in g_x:
        c.wait_recv()
    gz[me.z] = gx[0] + gx[1] + gx[2] + gx[3]
    g_z = [go(gz.at[me.z], gz.at[me.z], gs.at[6 + r], gr.at[6 + r], me.along_z(r)) for r in range(1, NZ)]

    def y_copy(j, to):
        return remote(yout.at[j, to], w_sums.at[pl.ds(j * UNIT, UNIT), :], ys.at[j, to], yr.at[j], me.id(y=to))

    for j in range(SHARD):
        holder, u = shard_unit(me, j)

        @pl.when(holder == y)
        def _():
            total = zout[unit_rows(u), :].astype(F32)
            for r in range(1, NZ):
                remote(zbuf.at[j, r], zbuf.at[j, r], zs.at[u], zr.at[j, r], me.along_z(r)).wait_recv()
                total = total + zbuf[j, r].astype(F32)
            for k in range(NY):
                rows = total[:, k * SLAB : (k + 1) * SLAB]
                rows = jnp.concatenate([rows, jnp.zeros((UNIT, 128 - SLAB), F32)], axis=1)
                yout[j, k] = rows
            for r in range(1, NY):
                y_copy(j, (y + r) % NY).start()
            w_sums[j * UNIT : (j + 1) * UNIT, :] = yout[j, y]

    x = x_ref[...].astype(F32)
    centred = x - jnp.mean(x, axis=1, keepdims=True)
    spread = jnp.mean(centred * centred, axis=1, keepdims=True)
    scale = lax.rsqrt(spread + EPS)
    hat = centred * scale
    f_up.wait_recv()
    f_down.wait_recv()
    d_normed = (
        dn_ref[rows_at(y * TOK, TOK), :].astype(F32) + full_r[0].astype(F32) + full_r[1].astype(F32)
    )
    inner = to_natural(d_normed) * gain_ref[...].astype(F32)
    first_mean = jnp.mean(inner, axis=1, keepdims=True)
    second = jnp.mean(inner * hat, axis=1, keepdims=True)
    dx_ref[...] = (scale * (inner - first_mean - hat * second)).astype(BF)

    for c in g_z:
        c.wait_recv()
    total = gz[0]
    for k in range(1, NZ):
        total = total + gz[k]
    total = jnp.concatenate([total[k : k + 1, :] for k in range(D // 128)], axis=1)
    gout_ref[...] = to_natural(total) / gain_ref[...].astype(F32) * FACTOR

    for j in range(SHARD):
        holder, u = shard_unit(me, j)

        @pl.when(holder != y)
        def _():
            y_copy(j, y).wait_recv()

        @pl.when(holder == y)
        def _():
            for r in range(1, NY):
                y_copy(j, (y + r) % NY).wait_send()

    wout_ref[...] = w_sums[...][:, :SLAB] * FACTOR
    for c in ctx_copies:
        c.wait_recv()
    ctx_ref[...] = ctx_out[...].T

    def sent_here(u, slot, z):
        rows = unit_rows(u)
        x_copy(u, w_mid.at[rows, :], wr2.at[0, rows, :], 0, right).wait_send()
        pl.when(z != me.z)(lambda: z_copy(u, slot, z).wait_send())

    def sent_there(u):
        rows = unit_rows(u)
        x_copy(u, w_mid.at[rows, :], wr2.at[1, rows, :], 1, right).wait_send()
        x_copy(u, w_mid.at[rows, :], wr2.at[2, rows, :], 2, left).wait_send()

    each_unit(me, sent_here, sent_there)
    for c in sent:
        c.wait_send()


def block(x, gain, w, cot):
    return pl.pallas_call(
        block_kernel,
        out_shape=(
            jax.ShapeDtypeStruct((TOK, NY * QW), BF),
            jax.ShapeDtypeStruct((TOK, D), BF),
            jax.ShapeDtypeStruct((BLOCK, SLAB), F32),
            jax.ShapeDtypeStruct((1, D), F32),
        ),
        in_specs=[pl.BlockSpec(memory_space=pl.ANY)] * 4,
        out_specs=(VMEM,) * 4,
        scratch_shapes=[
            pltpu.VMEM((TOK, D), BF),
            pltpu.VMEM((1, D), BF),
            pltpu.VMEM((BLOCK, 128), BF),
            pltpu.VMEM((TOK, NY * QW), BF),
            pltpu.VMEM((ROWS, D), BF),
            pltpu.VMEM((PW, D), BF),
            pltpu.VMEM((QW, ROWS), BF),
            pltpu.VMEM((NY * QW, TOK), BF),
            pltpu.VMEM((NY, SHARD, UNIT, 128), BF),
            dma(4),
            dma(4), dma(4), dma(4), dma(4), dma(3), dma(3, 4), dma(12, 8), dma(12),
            dma(3, 12), dma(3, 12), dma(2), dma(2),
            pltpu.VMEM((2 * QW, D), BF),
            pltpu.VMEM((SEQ, 2 * QW), BF),
            pltpu.VMEM((SEQ, 2 * QW), BF),
            pltpu.VMEM((QW, ROWS), BF),
            pltpu.VMEM((NY * QW, TOK), BF),
            pltpu.VMEM((QW, ROWS), BF),
            pltpu.VMEM((ROWS, QW), BF),
            pltpu.VMEM((ROWS, 2 * QW), BF),
            pltpu.VMEM((SEQ, ROWS), F32),
            pltpu.VMEM((SEQ, ROWS), BF),
            pltpu.VMEM((2, ROWS, 2 * QW), BF),
            pltpu.VMEM((ROWS, 2 * QW), BF),
            pltpu.VMEM((ROWS, 2 * QW), BF),
            dma(3, 3), dma(3, 3), dma(3, 3), dma(3, 3), dma(3, 4), dma(3, 4),
            pltpu.VMEM((ROWS, D), BF),
            pltpu.VMEM((PW, D), BF),
            pltpu.VMEM((16, 128), F32),
            pltpu.VMEM((BLOCK, 128), F32),
            pltpu.VMEM((2, TOK // 2, D), BF),
            pltpu.VMEM((TOK, D), BF),
            pltpu.VMEM((TOK, D), BF),
            pltpu.VMEM((2, TOK, D), BF),
            pltpu.VMEM((2, PW, GW), BF),
            pltpu.VMEM((2, PW, GW), BF),
            pltpu.VMEM((3, PW, GW), BF),
            pltpu.VMEM((PW, GW), BF),
            pltpu.VMEM((PW, GW), BF),
            pltpu.VMEM((SHARD, NZ, UNIT, GW), BF),
            pltpu.VMEM((SHARD, NY, UNIT, 128), F32),
            pltpu.VMEM((2, 16, 128), F32),
            pltpu.VMEM((NY, 16, 128), F32),
            pltpu.VMEM((4, 16, 128), F32),
            pltpu.VMEM((NZ, 16, 128), F32),
            dma(4), dma(4), dma(2, 4), dma(2, 4), dma(3, 12), dma(3, 12), dma(12), dma(3, 8),
            dma(3, 4), dma(3), dma(14), dma(14),
        ],
        compiler_params=pltpu.CompilerParams(
            collective_id=0, has_side_effects=True, vmem_limit_bytes=56 * 2**20
        ),
        name="block",
    )(x, gain, w, cot)


def shards(tokens, norm_gain, qkv_weight, d_context):
    x, gain = tokens[0], norm_gain[None, :]
    w = jnp.pad(qkv_weight.T, ((0, 0), (0, 128 - SLAB)))
    context, d_tokens, weight_grad, gain_grad = block(x, gain, w, d_context[0])
    return (context[None], d_tokens[None], weight_grad.T, gain_grad.reshape(D))


def solution(mesh):
    in_specs = (P("dp", "sp", None), P(), P("sp", "dp"), P("dp", "sp", None))
    out_specs = (P("dp", "sp", None), P("dp", "sp", None), P("sp", "dp"), P())
    return jax.shard_map(shards, mesh=mesh, in_specs=in_specs, out_specs=out_specs, check_vma=False)
```

```python
import functools
import math

import jax
import jax.numpy as jnp
from jax import lax
from jax.experimental import pallas as pl
from jax.experimental.pallas import tpu as pltpu
from jax.sharding import PartitionSpec as P

MESH = pl.DeviceIdType.MESH
BF = jnp.bfloat16
F32 = jnp.float32

D = 1536
HEAD = 64
OWN = 3
TOK = 128
NY = 4
NZ = 8
NA = 4
ROWS = NY * TOK
SEQ = NA * ROWS
QW = OWN * HEAD
PW = 3 * QW
SLAB = 96
BLOCK = 144
GW = NY * SLAB
EPS = 1e-05
VMEM = pl.BlockSpec(memory_space=pltpu.VMEM)


class Place:
    def __init__(self):
        d, s = lax.axis_index("dp"), lax.axis_index("sp")
        self.x_lo, self.z = d // NZ, d % NZ
        self.x_hi, self.y, self.core = s // 8, (s // 2) % NY, s % 2
        self.group = self.x_hi * 2 + self.core
        self.far_group = (1 - self.x_hi) * 2 + self.core

    def id(self, x_hi=None, x_lo=None, y=None, z=None, core=None):
        x_hi = self.x_hi if x_hi is None else x_hi
        x_lo = self.x_lo if x_lo is None else x_lo
        y = self.y if y is None else y
        z = self.z if z is None else z
        core = self.core if core is None else core
        return {"dp": x_lo * NZ + z, "sp": x_hi * 8 + y * 2 + core}

    def find_units(self):
        self.homes, self.sends = [], []
        for j in range(SHARD):
            y, u = shard_unit(self, j)
            x_lo, z = unit_home(u, y)
            self.homes.append(self.id(x_lo=x_lo, z=z, y=y))
            self.sends.append((y != self.y) | (x_lo != self.x_lo) | (z != self.z))
        self.has, self.unit = unit_at(self.x_lo, self.z, self.y)
        volume, self.place = unit_source(self.unit, self.y)
        elsewhere = volume != self.x_lo * NZ + self.z
        self.sources = [self.id(x_lo=volume // NZ, z=volume % NZ, y=k) for k in range(NY)]
        self.gets = [self.has & ((self.y != k) | elsewhere) for k in range(NY)]
        self.keeps = [self.has & (self.y == k) & jnp.logical_not(elsewhere) for k in range(NY)]

    def other_core(self):
        return self.id(core=1 - self.core)

    def mirror(self):
        return self.id(x_hi=1 - self.x_hi, x_lo=1 - self.x_lo)

    def beside(self):
        return self.id(x_lo=1 - self.x_lo)

    def far(self):
        return self.id(x_hi=1 - self.x_hi)

    def along_y(self, step):
        return self.id(y=(self.y + step) % NY)

    def along_z(self, step):
        return self.id(z=(self.z + step) % NZ)

    def along_x(self, step):
        x = (self.x_hi * 2 + self.x_lo + step) % 4
        return self.id(x_hi=x // 2, x_lo=x % 2)


def greet(me):
    barrier = pltpu.get_barrier_semaphore()
    partners = (
        [me.along_z(r) for r in range(1, NZ)]
        + [me.along_y(r) for r in range(1, NY)]
        + [me.along_x(r) for r in range(1, 4)]
        + [me.other_core()]
    )

    def tell(partner):
        pl.semaphore_signal(barrier, inc=1, device_id=partner, device_id_type=MESH)

    for partner in partners:
        tell(partner)
    count = jnp.int32(len(partners))
    for j in range(SHARD):
        pl.when(me.sends[j])(lambda: tell(me.homes[j]))
        count = count + me.sends[j].astype(jnp.int32)
    for k in range(NY):
        pl.when(me.gets[k])(lambda: tell(me.sources[k]))
        count = count + me.gets[k].astype(jnp.int32)
    return functools.partial(pl.semaphore_wait, barrier, count)


def remote(src, dst, send, recv, partner):
    return pltpu.make_async_remote_copy(
        src_ref=src, dst_ref=dst, send_sem=send, recv_sem=recv, device_id=partner, device_id_type=MESH
    )


def rows_at(start, size):
    return pl.ds(pl.multiple_of(start, 16), size)


def lanes_at(start, size):
    return pl.ds(pl.multiple_of(start, 128), size)


def to_grouped(wide):
    parts = []
    for x_hi in range(2):
        for core in range(2):
            for y in range(NY):
                s = x_hi * 8 + y * 2 + core
                parts.append(wide[:, s * SLAB : (s + 1) * SLAB])
    return jnp.concatenate(parts, axis=1)


def to_natural(wide):
    parts = []
    for x_hi in range(2):
        for y in range(NY):
            for core in range(2):
                s = (x_hi * 2 + core) * NY + y
                parts.append(wide[:, s * SLAB : (s + 1) * SLAB])
    return jnp.concatenate(parts, axis=1)


UNIT = 48
UNITS = 12
SHARD = 3


def unit_source(u, y):
    column = (u // 4) * 16 + 4 * y + u % 4
    return column // SHARD, column % SHARD


def unit_home(u, y):
    return u % 2, ((16 * (u // 4) + 4 * y) // SHARD + (u % 4) // 2) % NZ


def unit_at(x_lo, z, y):
    found, unit = jnp.int32(0), jnp.int32(0)
    for k in range(SHARD):
        for h in range(2):
            hit = (((16 * k + 4 * y) // SHARD + h) % NZ == z).astype(jnp.int32)
            found, unit = found + hit, unit + hit * (4 * k + 2 * h)
    return found > 0, unit + x_lo


def shard_unit(me, j):
    column = (me.x_lo * NZ + me.z) * SHARD + j
    return (column % 16) // 4, (column // 16) * 4 + column % 4


def each_unit(me, here, there, spans):
    def step(u, carry):
        x_lo, z = unit_home(u, me.y)
        if here is not None:
            pl.when(x_lo == me.x_lo)(lambda: here(u, z))
        if there is not None:
            pl.when(x_lo != me.x_lo)(lambda: there(u))
        return carry

    for first, end in spans:
        lax.fori_loop(first, end, step, 0)


def near_first(me, x_lo, act):
    def step(n, carry):
        r = jnp.where(n % 2 == 1, (n + 1) // 2, (NZ - n // 2) % NZ)
        has, u = unit_at(x_lo, (me.z + NZ - r) % NZ, me.y)
        pl.when(has)(lambda: act(r, u))
        return carry

    lax.fori_loop(0, NZ, step, 0)


def unit_rows(u):
    return rows_at(u * UNIT, UNIT)


def gather_phase(me, ready, load, x_ref, gain_ref, raw_ref, cot_ref, nall, wall, cots,
                 w_ref, cot_t, ybuf, ns, nr, cs, cr, ys, yr, zs, zr, xs, xr, ds, dr):
    y = me.y
    right, left = me.along_x(1), me.along_x(3)
    x_at = me.x_hi * 2 + me.x_lo
    own = lanes_at(me.group * GW, GW)
    far = lanes_at(me.far_group * GW, GW)
    hi_left, hi_right = ((x_at + 3) % 4) // 2, ((x_at + 1) % 4) // 2
    of_left = lanes_at((hi_left * 2 + me.core) * GW, GW)
    of_right = lanes_at((hi_right * 2 + me.core) * GW, GW)
    load(raw_ref)
    w_ref[...] = jnp.concatenate([raw_ref[...], jnp.zeros((BLOCK, 128 - SLAB), BF)], axis=1)
    ready()

    def y_copy(j):
        return remote(w_ref.at[pl.ds(j * UNIT, UNIT), :], ybuf.at[y], ys.at[j], yr.at[y], me.homes[j])

    for j in range(SHARD):
        pl.when(me.sends[j])(lambda: y_copy(j).start())

    load(x_ref)
    load(gain_ref)
    x = x_ref[...].astype(F32)
    centred = x - jnp.mean(x, axis=1, keepdims=True)
    spread = jnp.mean(centred * centred, axis=1, keepdims=True)
    normed = centred * lax.rsqrt(spread + EPS) * gain_ref[...].astype(F32)
    tok_rows = rows_at(y * TOK, TOK)
    nall[tok_rows, :] = to_grouped(normed).astype(BF)
    up, down = me.along_y(1), me.along_y(3)
    n_up = remote(nall.at[tok_rows, :], nall.at[tok_rows, :], ns.at[0], nr.at[0], up)
    n_down = remote(nall.at[tok_rows, :], nall.at[tok_rows, :], ns.at[1], nr.at[1], down)
    n_up.start()
    n_down.start()

    for k in range(NY):
        pl.when(me.gets[k])(lambda: remote(ybuf.at[k], ybuf.at[k], ys.at[0], yr.at[k], me.sources[k]).wait_recv())

        @pl.when(me.keeps[k])
        def _():
            ybuf[k] = w_ref[rows_at(me.place * UNIT, UNIT), :]

    @pl.when(me.has)
    def _():
        parts = [ybuf[k][:, :SLAB].astype(F32) for k in range(NY)]
        wall[unit_rows(me.unit), own] = jnp.concatenate(parts, axis=1).astype(BF)

    def piece(u, lanes):
        return wall.at[unit_rows(u), lanes]

    def z_copy(u, r):
        return remote(piece(u, own), piece(u, own), zs.at[r], zr.at[r], me.along_z(r))

    def x_copy(u, r, lanes, kind, to):
        return remote(piece(u, lanes), piece(u, lanes), xs.at[kind, r], xr.at[kind, r], to)

    @pl.when(me.has)
    def _():
        for r in (1, 7, 2, 6, 3, 5, 4):
            z_copy(me.unit, r).start()

    cot_copies = []
    load(cot_ref)
    cot_t[...] = cot_ref[...].T
    cot_lanes = lanes_at(y * TOK, TOK)
    for r in range(1, NY):
        to = (y + r) % NY
        c = remote(cot_t.at[rows_at(to * QW, QW), :], cots.at[:, cot_lanes], cs.at[r], cr.at[r], me.along_y(r))
        c.start()
        cot_copies.append(c)
    cots[:, cot_lanes] = cot_t[rows_at(y * QW, QW), :]

    def spread_x(r, u):
        pl.when(r != 0)(lambda: z_copy(u, r).wait_recv())
        x_copy(u, r, own, 0, right).start()
        x_copy(u, r, own, 1, left).start()

    near_first(me, me.x_lo, spread_x)

    half = TOK // 2
    from_down = rows_at(((y + 3) % NY) * TOK, half)
    from_up = rows_at(((y + 1) % NY) * TOK + half, half)
    n_up.wait_recv()
    f_up = remote(nall.at[from_down, :], nall.at[from_down, :], ns.at[2], nr.at[2], up)
    f_up.start()
    n_down.wait_recv()
    f_down = remote(nall.at[from_up, :], nall.at[from_up, :], ns.at[3], nr.at[3], down)
    f_down.start()

    def relay(r, u):
        x_copy(u, r, of_left, 0, right).wait_recv()
        pl.when((u // 2) % 2 == 0)(lambda: x_copy(u, r, of_left, 2, right).start())
        x_copy(u, r, of_right, 1, left).wait_recv()
        pl.when((u // 2) % 2 == 1)(lambda: x_copy(u, r, of_right, 2, left).start())

    near_first(me, 1 - me.x_lo, relay)
    near_first(me, me.x_lo, lambda r, u: x_copy(u, r, far, 2, right).wait_recv())

    core_copies = []
    for x_hi in range(2):
        lanes = lanes_at((x_hi * 2 + me.core) * GW, GW)
        c = remote(wall.at[:, lanes], wall.at[:, lanes], ds.at[x_hi], dr.at[x_hi], me.other_core())
        c.start()
        core_copies.append(c)
    for c in core_copies:
        c.wait_recv()
    f_up.wait_recv()
    f_down.wait_recv()
    for c in cot_copies:
        c.wait_recv()

    @pl.when(me.has)
    def _():
        for r in range(1, NZ):
            z_copy(me.unit, r).wait_send()

    def sent_here(r, u):
        x_copy(u, r, own, 0, right).wait_send()
        x_copy(u, r, own, 1, left).wait_send()

    near_first(me, me.x_lo, sent_here)
    near_first(me, 1 - me.x_lo, lambda r, u: x_copy(u, r, own, 2, right).wait_send())
    for j in range(SHARD):
        pl.when(me.sends[j])(lambda: y_copy(j).wait_send())
    for c in cot_copies + core_copies + [n_up, n_down, f_up, f_down]:
        c.wait_send()


def dma(*shape):
    return pltpu.SemaphoreType.DMA(shape)


FACTOR = 1.0 / math.sqrt(16 * SEQ)
CHUNK = 256
EARLY = ((0, 6), (8, 10))
LATE = ((6, 8), (10, 12))


def block_kernel(x_hbm, gain_hbm, w_hbm, cot_hbm, ctx_ref, dx_ref, wout_ref, gout_ref,
                 x_ref, gain_ref, shard_ref, d_ctx, n_ref, w_ref, cot_ref, w_pad, cot_t, ybuf, ls,
                 *rest):
    me = Place()
    y = me.y
    me.find_units()
    ready = greet(me)
    loads = {}
    for k, (src, dst) in enumerate(
        ((w_hbm, shard_ref), (x_hbm, x_ref), (gain_hbm, gain_ref), (cot_hbm, d_ctx))
    ):
        c = pltpu.make_async_copy(src, dst, ls.at[k])
        c.start()
        loads[id(dst)] = c
    gather_phase(
        me, ready, lambda ref: loads[id(ref)].wait(), x_ref, gain_ref, shard_ref, d_ctx,
        n_ref, w_ref, cot_ref, w_pad, cot_t, ybuf, *rest[:12],
    )
    back_phase(
        me, n_ref, w_ref, cot_ref, x_ref, gain_ref, ctx_ref, dx_ref, wout_ref, gout_ref, *rest[12:]
    )


def back_phase(me, n_ref, w_ref, cot_ref, x_ref, gain_ref, ctx_ref, dx_ref, wout_ref, gout_ref,
               wuse, kvall, dkv, ctx_own, ctx_out, dq_ref, dq_own, out_ref, s_buf, e_buf, r1, mid, r2,
               ks, kr, ss, rs, cs, cr,
               dn_ref, wg_ref, gg_ref, w_sums,
               half_r, to_up, to_down, full_r, s1, wr1, wr2, w_mid, zout, zbuf, yout,
               gcore, gy, gx, gz,
               ns, nr, ws, wr, xs, xr, zs, zr, ys, yr, gs, gr):
    y = me.y
    own = rows_at(me.group * ROWS, ROWS)
    far = rows_at(me.far_group * ROWS, ROWS)
    near = me.x_hi * 2 + 1 - me.core
    beyond = (1 - me.x_hi) * 2 + 1 - me.core
    own_there = rows_at(near * ROWS, ROWS)
    far_there = rows_at(beyond * ROWS, ROWS)
    groups = (me.group, near, me.far_group, beyond)

    def chunks(at):
        for i in range(ROWS // CHUNK):
            here = at * ROWS + i * CHUNK
            yield rows_at(groups[at] * ROWS + i * CHUNK, CHUNK), slice(here, here + CHUNK)

    mine = y * QW
    sent = []

    def go(*args):
        c = remote(*args)
        c.start()
        sent.append(c)
        return c

    def head_lanes(h):
        return slice(h * 128, (h + 1) * 128)

    nt = (((1,), (1,)), ((), ()))
    k_far, k_core = [], []
    for h in range(OWN):
        lanes = head_lanes(h)
        for which in range(2):
            row = QW * (1 + which) + h * HEAD
            wuse[h * 128 + which * HEAD : h * 128 + (which + 1) * HEAD, :] = w_ref[row : row + HEAD, :]
        kvall[own, lanes] = lax.dot_general(n_ref[...], wuse[lanes, :], nt, preferred_element_type=F32).astype(BF)
        k_far.append(go(kvall.at[own, lanes], kvall.at[own, lanes], ks.at[0, h], kr.at[0, h], me.far()))
        k_core.append(go(kvall.at[own, lanes], kvall.at[own, lanes], ks.at[1, h], kr.at[1, h], me.other_core()))
    queries = lax.dot_general(w_ref[:QW, :], n_ref[...], nt, preferred_element_type=F32).astype(BF)
    k_pass = []
    d_far, d_own, d_x, ctx_copies = [], [], [], []

    def pass_keys(h):
        k_far[h].wait_recv()
        k_pass.append(go(kvall.at[far, head_lanes(h)], kvall.at[far, head_lanes(h)], ks.at[2, h], kr.at[2, h], me.other_core()))

    def pass_sums(h):
        lanes = head_lanes(h)
        d_far[h].wait_recv()
        mid[:, lanes] = (dkv[far, lanes].astype(F32) + r1[0, :, lanes].astype(F32)).astype(BF)
        d_x.append(go(mid.at[:, lanes], r2.at[:, lanes], ss.at[2, h], rs.at[2, h], me.far()))

    def finish(h):
        lanes = head_lanes(h)
        d_own[h].wait_recv()
        d_x[h].wait_recv()
        out_ref[:, lanes] = (
            dkv[own, lanes].astype(F32) + r1[1, :, lanes].astype(F32) + r2[:, lanes].astype(F32)
        ).astype(BF)

    zeros = jnp.zeros((HEAD, ROWS), BF)
    for h in range(OWN):
        lanes = head_lanes(h)
        head_rows = slice(h * HEAD, (h + 1) * HEAD)
        q = queries[head_rows, :] * jnp.asarray(HEAD**-0.5, BF)
        q_pad = jnp.concatenate([q, zeros], axis=0)
        top = jnp.full((8, ROWS), -jnp.inf, F32)
        for at in range(NA):
            if at == 1:
                k_core[h].wait_recv()
            if at == 2 and h == 0:
                pass_keys(0)
            if at == 3:
                k_pass[h].wait_recv()
            for keys, rows in chunks(at):
                s = jnp.dot(kvall[keys, lanes], q_pad, preferred_element_type=F32)
                s_buf[rows, :] = s
                top = jnp.maximum(top, jnp.max(s.reshape(CHUNK // 8, 8, ROWS), axis=0))
        top = jnp.max(top, axis=0, keepdims=True)
        total = jnp.zeros((8, ROWS), F32)
        ctx = jnp.zeros((HEAD, ROWS), F32)
        for at in range(NA):
            for keys, rows in chunks(at):
                e = jnp.exp(s_buf[rows, :] - top)
                total = total + jnp.sum(e.reshape(CHUNK // 8, 8, ROWS), axis=0)
                e_low = e.astype(BF)
                e_buf[rows, :] = e_low
                v_t = kvall[keys, lanes].T[HEAD:, :]
                ctx = ctx + jnp.dot(v_t, e_low, preferred_element_type=F32)
        inverse = 1.0 / jnp.sum(total, axis=0, keepdims=True)
        ctx = ctx * inverse
        ctx_own[head_rows, :] = ctx.astype(BF)
        rows_there = rows_at(mine + h * HEAD, HEAD)
        for r in range(1, NY):
            to = lanes_at(((y + r) % NY) * TOK, TOK)
            ctx_copies.append(go(ctx_own.at[head_rows, to], ctx_out.at[rows_there, :], cs.at[h, r], cr.at[h, r], me.along_y(r)))
        ctx_out[rows_there, :] = ctx_own[head_rows, lanes_at(y * TOK, TOK)]
        if h + 1 < OWN:
            pass_keys(h + 1)
        if h > 0:
            pass_sums(h - 1)
        cot = (cot_ref[head_rows, :].astype(F32) * inverse).astype(BF)
        row_dot = jnp.sum(cot.astype(F32) * ctx, axis=0, keepdims=True)
        cot_pad = jnp.concatenate([zeros, cot], axis=0)
        q_side = q_pad.T
        cot_side = cot_pad.T
        dq = jnp.zeros((HEAD, ROWS), F32)
        for at in (3, 2, 1, 0):
            for keys, rows in chunks(at):
                d_attn = jnp.dot(kvall[keys, lanes], cot_pad, preferred_element_type=F32)
                e_low = e_buf[rows, :]
                slopes = (e_low.astype(F32) * (d_attn - row_dot)).astype(BF)
                k_t = kvall[keys, lanes].T[:HEAD, :]
                dq = dq + jnp.dot(k_t, slopes, preferred_element_type=F32)
                dkv[keys, lanes] = (
                    jnp.dot(slopes, q_side, preferred_element_type=F32)
                    + jnp.dot(e_low, cot_side, preferred_element_type=F32)
                ).astype(BF)
            if at == 3:
                d_far.append(go(dkv.at[far_there, lanes], r1.at[0, :, lanes], ss.at[0, h], rs.at[0, h], me.other_core()))
            if at == 1:
                d_own.append(go(dkv.at[own_there, lanes], r1.at[1, :, lanes], ss.at[1, h], rs.at[1, h], me.other_core()))
        dq_ref[head_rows, :] = (dq * HEAD**-0.5).astype(BF)
        if h == OWN - 1:
            pass_sums(h)

    right, left = me.along_x(1), me.along_x(3)
    x_at = me.x_hi * 2 + me.x_lo
    hi_left, hi_right = ((x_at + 3) % 4) // 2, ((x_at + 1) % 4) // 2
    half = TOK // 2
    up, down = me.along_y(1), me.along_y(3)
    opposite = (y + 2) % NY

    def weight_rows(h):
        rows = jnp.dot(out_ref[:, head_lanes(h)].T, n_ref[...], preferred_element_type=F32).astype(BF)
        for which in range(2):
            row = QW * (1 + which) + h * HEAD
            wg_ref[row : row + HEAD, :] = rows[which * HEAD : (which + 1) * HEAD, :]

    w_core = []

    def to_core(first, size):
        rows = pl.ds(first, size)
        k = len(w_core) // 2
        for x_hi in range(2):
            there = lanes_at((x_hi * 2 + 1 - me.core) * GW, GW)
            w_core.append(go(wg_ref.at[rows, there], wr1.at[x_hi, rows, :], ws.at[x_hi, k], wr.at[x_hi, k], me.other_core()))

    def from_core(k, first, size):
        rows = slice(first, first + size)
        for x_hi in range(2):
            w_core[2 * k + x_hi].wait_recv()
            here = lanes_at((x_hi * 2 + me.core) * GW, GW)
            s1[x_hi, rows, :] = (wg_ref[rows, here].astype(F32) + wr1[x_hi, rows, :].astype(F32)).astype(BF)

    def x_copy(u, src, dst, kind, to):
        return remote(src, dst, xs.at[kind, u], xr.at[kind, u], to)

    def to_opposite(u, z):
        src = s1.at[1 - me.x_hi, unit_rows(u), :]
        dst = wr2.at[0, unit_rows(u), :]
        pl.when((u // 2) % 2 == 0)(lambda: x_copy(u, src, dst, 0, right).start())
        pl.when((u // 2) % 2 == 1)(lambda: x_copy(u, src, dst, 0, left).start())

    def pass_on(u):
        rows = unit_rows(u)
        pl.when((u // 2) % 2 == 0)(lambda: x_copy(u, s1.at[hi_left, rows, :], wr2.at[2, rows, :], 2, left).start())
        pl.when((u // 2) % 2 == 1)(lambda: x_copy(u, s1.at[hi_right, rows, :], wr2.at[1, rows, :], 1, right).start())
        x_copy(u, s1.at[0, rows, :], wr2.at[0, rows, :], 0, right).wait_recv()

        @pl.when((u // 2) % 2 == 0)
        def _():
            w_mid[rows, :] = (s1[hi_right, rows, :].astype(F32) + wr2[0, rows, :].astype(F32)).astype(BF)
            x_copy(u, w_mid.at[rows, :], wr2.at[1, rows, :], 1, right).start()

        @pl.when((u // 2) % 2 == 1)
        def _():
            w_mid[rows, :] = (s1[hi_left, rows, :].astype(F32) + wr2[0, rows, :].astype(F32)).astype(BF)
            x_copy(u, w_mid.at[rows, :], wr2.at[2, rows, :], 2, left).start()


    def z_copy(u, z):
        distance = (z + NZ - me.z) % NZ
        return remote(zout.at[unit_rows(u), :], zbuf.at[distance], zs.at[u], zr.at[distance], me.id(z=z))

    def over_x(u, z):
        rows = unit_rows(u)
        x_copy(u, s1.at[0, rows, :], wr2.at[1, rows, :], 1, right).wait_recv()
        x_copy(u, s1.at[0, rows, :], wr2.at[2, rows, :], 2, left).wait_recv()
        zout[rows, :] = (
            s1[me.x_hi, rows, :].astype(F32) + wr2[1, rows, :].astype(F32) + wr2[2, rows, :].astype(F32)
        ).astype(BF)
        pl.when(z != me.z)(lambda: z_copy(u, z).start())


    wg_ref[:QW, :] = jnp.dot(dq_ref[...], n_ref[...], preferred_element_type=F32).astype(BF)
    for h in range(OWN - 1):
        finish(h)
        weight_rows(h)
    to_core(0, 288)
    to_core(384, 96)
    from_core(0, 0, 288)
    from_core(1, 384, 96)
    each_unit(me, to_opposite, None, EARLY)
    finish(OWN - 1)
    dq_own[...] = dq_ref[...].T
    gain_terms = jnp.zeros((8, D), F32)
    for r in (2, 1, 3, 0):
        at = (y + r) % NY
        rows = rows_at(at * TOK, TOK)
        first_rows = rows_at(at * TOK, half)
        rest_rows = rows_at(at * TOK + half, half)
        part = jnp.dot(dq_own[rows, :], w_ref[:QW, :], preferred_element_type=F32) + jnp.dot(
            out_ref[rows, :], wuse[...], preferred_element_type=F32
        )
        dn_ref[rows, :] = part.astype(BF)
        if r == 2:
            h_up = go(dn_ref.at[first_rows, :], half_r.at[0], ns.at[0], nr.at[0], up)
            h_down = go(dn_ref.at[rest_rows, :], half_r.at[1], ns.at[1], nr.at[1], down)
            weight_rows(OWN - 1)
            to_core(288, 96)
            to_core(480, 96)
        terms = part * n_ref[rows, :].astype(F32)
        gain_terms = gain_terms + jnp.sum(terms.reshape(TOK // 8, 8, D), axis=0)
    gain_terms = jnp.sum(gain_terms, axis=0, keepdims=True)
    gg_ref[...] = jnp.zeros((16, 128), F32)
    for k in range(D // 128):
        gg_ref[k : k + 1, :] = gain_terms[:, k * 128 : (k + 1) * 128]
    gcore[me.core] = gg_ref[...]
    g_core = go(gg_ref, gcore.at[me.core], gs.at[0], gr.at[0], me.other_core())
    from_core(2, 288, 96)
    from_core(3, 480, 96)
    each_unit(me, to_opposite, None, LATE)
    each_unit(me, None, pass_on, EARLY)
    g_core.wait_recv()
    gy[y] = gcore[0] + gcore[1]
    g_y = [go(gy.at[y], gy.at[y], gs.at[r], gr.at[r], me.along_y(r)) for r in range(1, NY)]
    h_up.wait_recv()
    block = rows_at(((y + 1) % NY) * TOK, half)
    rest = rows_at(((y + 1) % NY) * TOK + half, half)
    to_up[:half, :] = (dn_ref[block, :].astype(F32) + half_r[0].astype(F32)).astype(BF)
    to_up[half:, :] = dn_ref[rest, :]
    f_up = go(to_up, full_r.at[0], ns.at[2], nr.at[2], up)
    h_down.wait_recv()
    block = rows_at(((y + 3) % NY) * TOK, half)
    rest = rows_at(((y + 3) % NY) * TOK + half, half)
    to_down[:half, :] = dn_ref[block, :]
    to_down[half:, :] = (dn_ref[rest, :].astype(F32) + half_r[1].astype(F32)).astype(BF)
    f_down = go(to_down, full_r.at[1], ns.at[3], nr.at[3], down)

    each_unit(me, None, pass_on, LATE)
    each_unit(me, over_x, None, EARLY)
    for c in g_y:
        c.wait_recv()
    gx[x_at] = gy[0] + gy[1] + gy[2] + gy[3]
    g_x = [go(gx.at[x_at], gx.at[x_at], gs.at[3 + r], gr.at[3 + r], me.along_x(r)) for r in range(1, 4)]

    each_unit(me, over_x, None, LATE)
    for c in g_x:
        c.wait_recv()
    gz[me.z] = gx[0] + gx[1] + gx[2] + gx[3]
    g_z = [go(gz.at[me.z], gz.at[me.z], gs.at[6 + r], gr.at[6 + r], me.along_z(r)) for r in range(1, NZ)]

    own_place = rows_at(me.place * UNIT, UNIT)

    def y_copy(k):
        return remote(yout.at[k], w_sums.at[own_place, :], ys.at[k], yr.at[me.place], me.sources[k])

    @pl.when(me.has)
    def _():
        total = zout[unit_rows(me.unit), :].astype(F32)
        for r in range(1, NZ):
            remote(zbuf.at[r], zbuf.at[r], zs.at[0], zr.at[r], me.along_z(r)).wait_recv()
            total = total + zbuf[r].astype(F32)
        for k in range(NY):
            part = total[:, k * SLAB : (k + 1) * SLAB]
            yout[k] = jnp.concatenate([part, jnp.zeros((UNIT, 128 - SLAB), F32)], axis=1)

    for k in range(NY):
        pl.when(me.gets[k])(lambda: y_copy(k).start())

        @pl.when(me.keeps[k])
        def _():
            w_sums[own_place, :] = yout[k]

    x = x_ref[...].astype(F32)
    centred = x - jnp.mean(x, axis=1, keepdims=True)
    spread = jnp.mean(centred * centred, axis=1, keepdims=True)
    scale = lax.rsqrt(spread + EPS)
    hat = centred * scale
    f_up.wait_recv()
    f_down.wait_recv()
    d_normed = (
        dn_ref[rows_at(y * TOK, TOK), :].astype(F32) + full_r[0].astype(F32) + full_r[1].astype(F32)
    )
    inner = to_natural(d_normed) * gain_ref[...].astype(F32)
    first_mean = jnp.mean(inner, axis=1, keepdims=True)
    second = jnp.mean(inner * hat, axis=1, keepdims=True)
    dx_ref[...] = (scale * (inner - first_mean - hat * second)).astype(BF)

    for c in g_z:
        c.wait_recv()
    total = gz[0]
    for k in range(1, NZ):
        total = total + gz[k]
    total = jnp.concatenate([total[k : k + 1, :] for k in range(D // 128)], axis=1)
    gout_ref[...] = to_natural(total) / gain_ref[...].astype(F32) * FACTOR

    for j in range(SHARD):
        rows = pl.ds(j * UNIT, UNIT)
        pl.when(me.sends[j])(
            lambda: remote(w_sums.at[rows, :], w_sums.at[rows, :], ys.at[0], yr.at[j], me.homes[j]).wait_recv()
        )
    for k in range(NY):
        pl.when(me.gets[k])(lambda: y_copy(k).wait_send())
    wout_ref[...] = w_sums[...][:, :SLAB] * FACTOR
    for c in ctx_copies:
        c.wait_recv()
    ctx_ref[...] = ctx_out[...].T

    def sent_here(u, z):
        rows = unit_rows(u)
        x_copy(u, w_mid.at[rows, :], wr2.at[0, rows, :], 0, right).wait_send()
        pl.when(z != me.z)(lambda: z_copy(u, z).wait_send())

    def sent_there(u):
        rows = unit_rows(u)
        x_copy(u, w_mid.at[rows, :], wr2.at[1, rows, :], 1, right).wait_send()
        x_copy(u, w_mid.at[rows, :], wr2.at[2, rows, :], 2, left).wait_send()

    each_unit(me, sent_here, sent_there, ((0, UNITS),))
    for c in sent:
        c.wait_send()


def block(x, gain, w, cot):
    return pl.pallas_call(
        block_kernel,
        out_shape=(
            jax.ShapeDtypeStruct((TOK, NY * QW), BF),
            jax.ShapeDtypeStruct((TOK, D), BF),
            jax.ShapeDtypeStruct((BLOCK, SLAB), F32),
            jax.ShapeDtypeStruct((1, D), F32),
        ),
        in_specs=[pl.BlockSpec(memory_space=pl.ANY)] * 4,
        out_specs=(VMEM,) * 4,
        scratch_shapes=[
            pltpu.VMEM((TOK, D), BF),
            pltpu.VMEM((1, D), BF),
            pltpu.VMEM((BLOCK, SLAB), BF),
            pltpu.VMEM((TOK, NY * QW), BF),
            pltpu.VMEM((ROWS, D), BF),
            pltpu.VMEM((PW, D), BF),
            pltpu.VMEM((QW, ROWS), BF),
            pltpu.VMEM((BLOCK, 128), BF),
            pltpu.VMEM((NY * QW, TOK), BF),
            pltpu.VMEM((NY, UNIT, 128), BF),
            dma(4),
            dma(4), dma(4), dma(4), dma(4), dma(3), dma(4), dma(8), dma(8),
            dma(3, 8), dma(3, 8), dma(2), dma(2),
            pltpu.VMEM((2 * QW, D), BF),
            pltpu.VMEM((SEQ, 2 * QW), BF),
            pltpu.VMEM((SEQ, 2 * QW), BF),
            pltpu.VMEM((QW, ROWS), BF),
            pltpu.VMEM((NY * QW, TOK), BF),
            pltpu.VMEM((QW, ROWS), BF),
            pltpu.VMEM((ROWS, QW), BF),
            pltpu.VMEM((ROWS, 2 * QW), BF),
            pltpu.VMEM((SEQ, ROWS), F32),
            pltpu.VMEM((SEQ, ROWS), BF),
            pltpu.VMEM((2, ROWS, 2 * QW), BF),
            pltpu.VMEM((ROWS, 2 * QW), BF),
            pltpu.VMEM((ROWS, 2 * QW), BF),
            dma(3, 3), dma(3, 3), dma(3, 3), dma(3, 3), dma(3, 4), dma(3, 4),
            pltpu.VMEM((ROWS, D), BF),
            pltpu.VMEM((PW, D), BF),
            pltpu.VMEM((16, 128), F32),
            pltpu.VMEM((BLOCK, 128), F32),
            pltpu.VMEM((2, TOK // 2, D), BF),
            pltpu.VMEM((TOK, D), BF),
            pltpu.VMEM((TOK, D), BF),
            pltpu.VMEM((2, TOK, D), BF),
            pltpu.VMEM((2, PW, GW), BF),
            pltpu.VMEM((2, PW, GW), BF),
            pltpu.VMEM((3, PW, GW), BF),
            pltpu.VMEM((PW, GW), BF),
            pltpu.VMEM((PW, GW), BF),
            pltpu.VMEM((NZ, UNIT, GW), BF),
            pltpu.VMEM((NY, UNIT, 128), F32),
            pltpu.VMEM((2, 16, 128), F32),
            pltpu.VMEM((NY, 16, 128), F32),
            pltpu.VMEM((4, 16, 128), F32),
            pltpu.VMEM((NZ, 16, 128), F32),
            dma(4), dma(4), dma(2, 4), dma(2, 4), dma(3, 12), dma(3, 12), dma(12), dma(8),
            dma(4), dma(3), dma(14), dma(14),
        ],
        compiler_params=pltpu.CompilerParams(
            collective_id=0, has_side_effects=True, vmem_limit_bytes=56 * 2**20
        ),
        name="block",
    )(x, gain, w, cot)


def shards(tokens, norm_gain, qkv_weight, d_context):
    x, gain = tokens[0], norm_gain[None, :]
    context, d_tokens, weight_grad, gain_grad = block(x, gain, qkv_weight.T, d_context[0])
    return (context[None], d_tokens[None], weight_grad.T, gain_grad.reshape(D))


def solution(mesh):
    in_specs = (P("dp", "sp", None), P(), P("sp", "dp"), P("dp", "sp", None))
    out_specs = (P("dp", "sp", None), P("dp", "sp", None), P("sp", "dp"), P())
    return jax.shard_map(shards, mesh=mesh, in_specs=in_specs, out_specs=out_specs, check_vma=False)
```

```python
import functools
import math

import jax
import jax.numpy as jnp
from jax import lax
from jax.experimental import pallas as pl
from jax.experimental.pallas import tpu as pltpu
from jax.sharding import PartitionSpec as P

MESH = pl.DeviceIdType.MESH
BF = jnp.bfloat16
F32 = jnp.float32

D = 1536
HEAD = 64
OWN = 3
TOK = 128
NY = 4
NZ = 8
NA = 4
ROWS = NY * TOK
SEQ = NA * ROWS
QW = OWN * HEAD
PW = 3 * QW
SLAB = 96
BLOCK = 144
GW = NY * SLAB
EPS = 1e-05
VMEM = pl.BlockSpec(memory_space=pltpu.VMEM)


class Place:
    def __init__(self):
        d, s = lax.axis_index("dp"), lax.axis_index("sp")
        self.x_lo, self.z = d // NZ, d % NZ
        self.x_hi, self.y, self.core = s // 8, (s // 2) % NY, s % 2
        self.group = self.x_hi * 2 + self.core
        self.far_group = (1 - self.x_hi) * 2 + self.core

    def id(self, x_hi=None, x_lo=None, y=None, z=None, core=None):
        x_hi = self.x_hi if x_hi is None else x_hi
        x_lo = self.x_lo if x_lo is None else x_lo
        y = self.y if y is None else y
        z = self.z if z is None else z
        core = self.core if core is None else core
        return {"dp": x_lo * NZ + z, "sp": x_hi * 8 + y * 2 + core}

    def find_units(self):
        self.homes, self.sends = [], []
        for j in range(SHARD):
            y, u = shard_unit(self, j)
            x_lo, z = unit_home(u, y)
            self.homes.append(self.id(x_lo=x_lo, z=z, y=y))
            self.sends.append((y != self.y) | (x_lo != self.x_lo) | (z != self.z))
        self.has, self.unit = unit_at(self.x_lo, self.z, self.y)
        volume, self.place = unit_source(self.unit, self.y)
        elsewhere = volume != self.x_lo * NZ + self.z
        self.sources = [self.id(x_lo=volume // NZ, z=volume % NZ, y=k) for k in range(NY)]
        self.gets = [self.has & ((self.y != k) | elsewhere) for k in range(NY)]
        self.keeps = [self.has & (self.y == k) & jnp.logical_not(elsewhere) for k in range(NY)]

    def other_core(self):
        return self.id(core=1 - self.core)

    def mirror(self):
        return self.id(x_hi=1 - self.x_hi, x_lo=1 - self.x_lo)

    def beside(self):
        return self.id(x_lo=1 - self.x_lo)

    def far(self):
        return self.id(x_hi=1 - self.x_hi)

    def along_y(self, step):
        return self.id(y=(self.y + step) % NY)

    def along_z(self, step):
        return self.id(z=(self.z + step) % NZ)

    def along_x(self, step):
        x = (self.x_hi * 2 + self.x_lo + step) % 4
        return self.id(x_hi=x // 2, x_lo=x % 2)


def greet(me):
    barrier = pltpu.get_barrier_semaphore()
    partners = (
        [me.along_z(r) for r in range(1, NZ)]
        + [me.along_y(r) for r in range(1, NY)]
        + [me.along_x(r) for r in range(1, 4)]
        + [me.other_core()]
    )

    def tell(partner):
        pl.semaphore_signal(barrier, inc=1, device_id=partner, device_id_type=MESH)

    for partner in partners:
        tell(partner)
    count = jnp.int32(len(partners))
    for j in range(SHARD):
        pl.when(me.sends[j])(lambda: tell(me.homes[j]))
        count = count + me.sends[j].astype(jnp.int32)
    for k in range(NY):
        pl.when(me.gets[k])(lambda: tell(me.sources[k]))
        count = count + me.gets[k].astype(jnp.int32)
    return functools.partial(pl.semaphore_wait, barrier, count)


def remote(src, dst, send, recv, partner):
    return pltpu.make_async_remote_copy(
        src_ref=src, dst_ref=dst, send_sem=send, recv_sem=recv, device_id=partner, device_id_type=MESH
    )


def rows_at(start, size):
    return pl.ds(pl.multiple_of(start, 16), size)


def lanes_at(start, size):
    return pl.ds(pl.multiple_of(start, 128), size)


def to_grouped(wide):
    parts = []
    for x_hi in range(2):
        for core in range(2):
            for y in range(NY):
                s = x_hi * 8 + y * 2 + core
                parts.append(wide[:, s * SLAB : (s + 1) * SLAB])
    return jnp.concatenate(parts, axis=1)


def to_natural(wide):
    parts = []
    for x_hi in range(2):
        for y in range(NY):
            for core in range(2):
                s = (x_hi * 2 + core) * NY + y
                parts.append(wide[:, s * SLAB : (s + 1) * SLAB])
    return jnp.concatenate(parts, axis=1)


UNIT = 48
UNITS = 12
SHARD = 3


def unit_source(u, y):
    column = (u // 4) * 16 + 4 * y + u % 4
    return column // SHARD, column % SHARD


def unit_home(u, y):
    return u % 2, ((16 * (u // 4) + 4 * y) // SHARD + (u % 4) // 2) % NZ


def unit_at(x_lo, z, y):
    found, unit = jnp.int32(0), jnp.int32(0)
    for k in range(SHARD):
        for h in range(2):
            hit = (((16 * k + 4 * y) // SHARD + h) % NZ == z).astype(jnp.int32)
            found, unit = found + hit, unit + hit * (4 * k + 2 * h)
    return found > 0, unit + x_lo


def shard_unit(me, j):
    column = (me.x_lo * NZ + me.z) * SHARD + j
    return (column % 16) // 4, (column // 16) * 4 + column % 4


def each_unit(me, here, there, spans):
    def step(u, carry):
        x_lo, z = unit_home(u, me.y)
        if here is not None:
            pl.when(x_lo == me.x_lo)(lambda: here(u, z))
        if there is not None:
            pl.when(x_lo != me.x_lo)(lambda: there(u))
        return carry

    for first, end in spans:
        lax.fori_loop(first, end, step, 0)


def near_first(me, x_lo, act, first=0, end=NZ):
    def step(n, carry):
        r = jnp.where(n % 2 == 1, (n + 1) // 2, (NZ - n // 2) % NZ)
        has, u = unit_at(x_lo, (me.z + NZ - r) % NZ, me.y)
        pl.when(has)(lambda: act(r, u))
        return carry

    lax.fori_loop(first, end, step, 0)


def unit_rows(u):
    return rows_at(u * UNIT, UNIT)


def gather_phase(me, ready, load, x_ref, gain_ref, raw_ref, cot_ref, nall, wall, cots,
                 w_ref, cot_t, ybuf, ns, nr, cs, cr, ys, yr, zs, zr, xs, xr, ds, dr):
    y = me.y
    right, left = me.along_x(1), me.along_x(3)
    x_at = me.x_hi * 2 + me.x_lo
    own = lanes_at(me.group * GW, GW)
    far = lanes_at(me.far_group * GW, GW)
    hi_left, hi_right = ((x_at + 3) % 4) // 2, ((x_at + 1) % 4) // 2
    of_left = lanes_at((hi_left * 2 + me.core) * GW, GW)
    of_right = lanes_at((hi_right * 2 + me.core) * GW, GW)
    load(raw_ref)
    w_ref[...] = jnp.concatenate([raw_ref[...], jnp.zeros((BLOCK, 128 - SLAB), BF)], axis=1)
    ready()

    def y_copy(j):
        return remote(w_ref.at[pl.ds(j * UNIT, UNIT), :], ybuf.at[y], ys.at[j], yr.at[y], me.homes[j])

    for j in range(SHARD):
        pl.when(me.sends[j])(lambda: y_copy(j).start())

    load(x_ref)
    load(gain_ref)
    x = x_ref[...].astype(F32)
    centred = x - jnp.mean(x, axis=1, keepdims=True)
    spread = jnp.mean(centred * centred, axis=1, keepdims=True)
    normed = centred * lax.rsqrt(spread + EPS) * gain_ref[...].astype(F32)
    tok_rows = rows_at(y * TOK, TOK)
    nall[tok_rows, :] = to_grouped(normed).astype(BF)
    up, down = me.along_y(1), me.along_y(3)
    half = TOK // 2
    low, high = rows_at(y * TOK, half), rows_at(y * TOK + half, half)

    def n_copy(rows, k, to):
        c = remote(nall.at[rows, :], nall.at[rows, :], ns.at[k], nr.at[k], to)
        c.start()
        return c

    n_up, n_down = n_copy(low, 0, up), n_copy(high, 1, down)
    n_rest = [n_copy(high, 4, up), n_copy(low, 5, down)]
    for k in range(NY):
        pl.when(me.gets[k])(lambda: remote(ybuf.at[k], ybuf.at[k], ys.at[0], yr.at[k], me.sources[k]).wait_recv())

        @pl.when(me.keeps[k])
        def _():
            ybuf[k] = w_ref[rows_at(me.place * UNIT, UNIT), :]

    @pl.when(me.has)
    def _():
        parts = [ybuf[k][:, :SLAB].astype(F32) for k in range(NY)]
        wall[unit_rows(me.unit), own] = jnp.concatenate(parts, axis=1).astype(BF)

    def piece(u, lanes):
        return wall.at[unit_rows(u), lanes]

    def z_copy(u, r):
        return remote(piece(u, own), piece(u, own), zs.at[r], zr.at[r], me.along_z(r))

    def x_copy(u, r, lanes, kind, to):
        return remote(piece(u, lanes), piece(u, lanes), xs.at[kind, r], xr.at[kind, r], to)

    @pl.when(me.has)
    def _():
        for r in (1, 7, 2, 6, 3, 5, 4):
            z_copy(me.unit, r).start()

    cot_copies = []
    load(cot_ref)
    cot_t[...] = cot_ref[...].T
    cot_lanes = lanes_at(y * TOK, TOK)
    for r in range(1, NY):
        to = (y + r) % NY
        c = remote(cot_t.at[rows_at(to * QW, QW), :], cots.at[:, cot_lanes], cs.at[r], cr.at[r], me.along_y(r))
        c.start()
        cot_copies.append(c)
    cots[:, cot_lanes] = cot_t[rows_at(y * QW, QW), :]

    def spread_x(r, u):
        pl.when(r != 0)(lambda: z_copy(u, r).wait_recv())
        x_copy(u, r, own, 0, right).start()
        x_copy(u, r, own, 1, left).start()

    near_first(me, me.x_lo, spread_x, 0, 3)
    from_down = rows_at(((y + 3) % NY) * TOK, half)
    from_up = rows_at(((y + 1) % NY) * TOK + half, half)
    n_up.wait_recv()
    f_up = n_copy(from_down, 2, up)
    n_down.wait_recv()
    f_down = n_copy(from_up, 3, down)
    near_first(me, me.x_lo, spread_x, 3, NZ)

    def relay(r, u):
        x_copy(u, r, of_left, 0, right).wait_recv()
        pl.when((u // 2) % 2 == 0)(lambda: x_copy(u, r, of_left, 2, right).start())
        x_copy(u, r, of_right, 1, left).wait_recv()
        pl.when((u // 2) % 2 == 1)(lambda: x_copy(u, r, of_right, 2, left).start())

    near_first(me, 1 - me.x_lo, relay)
    near_first(me, me.x_lo, lambda r, u: x_copy(u, r, far, 2, right).wait_recv())

    core_copies = []
    for x_hi in range(2):
        lanes = lanes_at((x_hi * 2 + me.core) * GW, GW)
        c = remote(wall.at[:, lanes], wall.at[:, lanes], ds.at[x_hi], dr.at[x_hi], me.other_core())
        c.start()
        core_copies.append(c)
    for c in core_copies:
        c.wait_recv()
    for c in n_rest + [f_up, f_down]:
        c.wait_recv()
    for c in cot_copies:
        c.wait_recv()

    @pl.when(me.has)
    def _():
        for r in range(1, NZ):
            z_copy(me.unit, r).wait_send()

    def sent_here(r, u):
        x_copy(u, r, own, 0, right).wait_send()
        x_copy(u, r, own, 1, left).wait_send()

    near_first(me, me.x_lo, sent_here)
    near_first(me, 1 - me.x_lo, lambda r, u: x_copy(u, r, own, 2, right).wait_send())
    for j in range(SHARD):
        pl.when(me.sends[j])(lambda: y_copy(j).wait_send())
    for c in cot_copies + core_copies + n_rest + [n_up, n_down, f_up, f_down]:
        c.wait_send()


def dma(*shape):
    return pltpu.SemaphoreType.DMA(shape)


FACTOR = 1.0 / math.sqrt(16 * SEQ)
CHUNK = 256
EARLY = ((0, 6), (8, 10))
LATE = ((6, 8), (10, 12))


def block_kernel(x_hbm, gain_hbm, w_hbm, cot_hbm, ctx_ref, dx_ref, wout_ref, gout_ref,
                 x_ref, gain_ref, shard_ref, d_ctx, n_ref, w_ref, cot_ref, w_pad, cot_t, ybuf, ls,
                 *rest):
    me = Place()
    y = me.y
    me.find_units()
    ready = greet(me)
    loads = {}
    for k, (src, dst) in enumerate(
        ((w_hbm, shard_ref), (x_hbm, x_ref), (gain_hbm, gain_ref), (cot_hbm, d_ctx))
    ):
        c = pltpu.make_async_copy(src, dst, ls.at[k])
        c.start()
        loads[id(dst)] = c
    gather_phase(
        me, ready, lambda ref: loads[id(ref)].wait(), x_ref, gain_ref, shard_ref, d_ctx,
        n_ref, w_ref, cot_ref, w_pad, cot_t, ybuf, *rest[:12],
    )
    back_phase(
        me, n_ref, w_ref, cot_ref, x_ref, gain_ref, ctx_ref, dx_ref, wout_ref, gout_ref, *rest[12:]
    )


def back_phase(me, n_ref, w_ref, cot_ref, x_ref, gain_ref, ctx_ref, dx_ref, wout_ref, gout_ref,
               wuse, kvall, dkv, ctx_own, ctx_out, dq_ref, dq_own, out_ref, s_buf, e_buf, r1, mid, r2,
               ks, kr, ss, rs, cs, cr,
               dn_ref, wg_ref, gg_ref, w_sums,
               half_r, to_up, to_down, full_r, s1, wr1, wr2, w_mid, zout, zbuf, yout,
               gcore, gy, gx, gz,
               ns, nr, ws, wr, xs, xr, zs, zr, ys, yr, gs, gr):
    y = me.y
    own = rows_at(me.group * ROWS, ROWS)
    far = rows_at(me.far_group * ROWS, ROWS)
    near = me.x_hi * 2 + 1 - me.core
    beyond = (1 - me.x_hi) * 2 + 1 - me.core
    own_there = rows_at(near * ROWS, ROWS)
    far_there = rows_at(beyond * ROWS, ROWS)
    groups = (me.group, near, me.far_group, beyond)

    def chunks(at):
        for i in range(ROWS // CHUNK):
            here = at * ROWS + i * CHUNK
            yield rows_at(groups[at] * ROWS + i * CHUNK, CHUNK), slice(here, here + CHUNK)

    mine = y * QW
    sent = []

    def go(*args):
        c = remote(*args)
        c.start()
        sent.append(c)
        return c

    def head_lanes(h):
        return slice(h * 128, (h + 1) * 128)

    nt = (((1,), (1,)), ((), ()))
    k_far, k_core = [], []
    for h in range(OWN):
        lanes = head_lanes(h)
        for which in range(2):
            row = QW * (1 + which) + h * HEAD
            wuse[h * 128 + which * HEAD : h * 128 + (which + 1) * HEAD, :] = w_ref[row : row + HEAD, :]
        kvall[own, lanes] = lax.dot_general(n_ref[...], wuse[lanes, :], nt, preferred_element_type=F32).astype(BF)
        k_far.append(go(kvall.at[own, lanes], kvall.at[own, lanes], ks.at[0, h], kr.at[0, h], me.far()))
        k_core.append(go(kvall.at[own, lanes], kvall.at[own, lanes], ks.at[1, h], kr.at[1, h], me.other_core()))
    queries = lax.dot_general(w_ref[:QW, :], n_ref[...], nt, preferred_element_type=F32).astype(BF)
    k_pass = []
    d_far, d_own, d_x, ctx_copies = [], [], [], []

    def pass_keys(h):
        k_far[h].wait_recv()
        k_pass.append(go(kvall.at[far, head_lanes(h)], kvall.at[far, head_lanes(h)], ks.at[2, h], kr.at[2, h], me.other_core()))

    def pass_sums(h):
        lanes = head_lanes(h)
        d_far[h].wait_recv()
        mid[:, lanes] = (dkv[far, lanes].astype(F32) + r1[0, :, lanes].astype(F32)).astype(BF)
        d_x.append(go(mid.at[:, lanes], r2.at[:, lanes], ss.at[2, h], rs.at[2, h], me.far()))

    def finish(h):
        lanes = head_lanes(h)
        d_own[h].wait_recv()
        d_x[h].wait_recv()
        out_ref[:, lanes] = (
            dkv[own, lanes].astype(F32) + r1[1, :, lanes].astype(F32) + r2[:, lanes].astype(F32)
        ).astype(BF)

    zeros = jnp.zeros((HEAD, ROWS), BF)
    for h in range(OWN):
        lanes = head_lanes(h)
        head_rows = slice(h * HEAD, (h + 1) * HEAD)
        q = queries[head_rows, :] * jnp.asarray(HEAD**-0.5, BF)
        q_pad = jnp.concatenate([q, zeros], axis=0)
        top = jnp.full((8, ROWS), -jnp.inf, F32)
        for at in range(NA):
            if at == 1:
                k_core[h].wait_recv()
            if at == 2 and h == 0:
                pass_keys(0)
            if at == 3:
                k_pass[h].wait_recv()
            for keys, rows in chunks(at):
                s = jnp.dot(kvall[keys, lanes], q_pad, preferred_element_type=F32)
                s_buf[rows, :] = s
                top = jnp.maximum(top, jnp.max(s.reshape(CHUNK // 8, 8, ROWS), axis=0))
        top = jnp.max(top, axis=0, keepdims=True)
        total = jnp.zeros((8, ROWS), F32)
        ctx = jnp.zeros((HEAD, ROWS), F32)
        for at in range(NA):
            for keys, rows in chunks(at):
                e = jnp.exp(s_buf[rows, :] - top)
                total = total + jnp.sum(e.reshape(CHUNK // 8, 8, ROWS), axis=0)
                e_low = e.astype(BF)
                e_buf[rows, :] = e_low
                v_t = kvall[keys, lanes].T[HEAD:, :]
                ctx = ctx + jnp.dot(v_t, e_low, preferred_element_type=F32)
        inverse = 1.0 / jnp.sum(total, axis=0, keepdims=True)
        ctx = ctx * inverse
        ctx_own[head_rows, :] = ctx.astype(BF)
        rows_there = rows_at(mine + h * HEAD, HEAD)
        for r in range(1, NY):
            to = lanes_at(((y + r) % NY) * TOK, TOK)
            ctx_copies.append(go(ctx_own.at[head_rows, to], ctx_out.at[rows_there, :], cs.at[h, r], cr.at[h, r], me.along_y(r)))
        ctx_out[rows_there, :] = ctx_own[head_rows, lanes_at(y * TOK, TOK)]
        if h + 1 < OWN:
            pass_keys(h + 1)
        cot = (cot_ref[head_rows, :].astype(F32) * inverse).astype(BF)
        row_dot = jnp.sum(cot.astype(F32) * ctx, axis=0, keepdims=True)
        cot_pad = jnp.concatenate([zeros, cot], axis=0)
        q_side = q_pad.T
        cot_side = cot_pad.T
        dq = jnp.zeros((HEAD, ROWS), F32)
        for at in (3, 2, 1, 0):
            for keys, rows in chunks(at):
                d_attn = jnp.dot(kvall[keys, lanes], cot_pad, preferred_element_type=F32)
                e_low = e_buf[rows, :]
                slopes = (e_low.astype(F32) * (d_attn - row_dot)).astype(BF)
                k_t = kvall[keys, lanes].T[:HEAD, :]
                dq = dq + jnp.dot(k_t, slopes, preferred_element_type=F32)
                dkv[keys, lanes] = (
                    jnp.dot(slopes, q_side, preferred_element_type=F32)
                    + jnp.dot(e_low, cot_side, preferred_element_type=F32)
                ).astype(BF)
            if at == 3:
                d_far.append(go(dkv.at[far_there, lanes], r1.at[0, :, lanes], ss.at[0, h], rs.at[0, h], me.other_core()))
            if at == 1:
                d_own.append(go(dkv.at[own_there, lanes], r1.at[1, :, lanes], ss.at[1, h], rs.at[1, h], me.other_core()))
                pass_sums(h)
        dq_ref[head_rows, :] = (dq * HEAD**-0.5).astype(BF)

    right, left = me.along_x(1), me.along_x(3)
    x_at = me.x_hi * 2 + me.x_lo
    hi_left, hi_right = ((x_at + 3) % 4) // 2, ((x_at + 1) % 4) // 2
    half = TOK // 2
    up, down = me.along_y(1), me.along_y(3)
    opposite = (y + 2) % NY

    def weight_rows(h):
        rows = jnp.dot(out_ref[:, head_lanes(h)].T, n_ref[...], preferred_element_type=F32).astype(BF)
        for which in range(2):
            row = QW * (1 + which) + h * HEAD
            wg_ref[row : row + HEAD, :] = rows[which * HEAD : (which + 1) * HEAD, :]

    w_core = []

    def to_core(first, size):
        rows = pl.ds(first, size)
        k = len(w_core) // 2
        for x_hi in range(2):
            there = lanes_at((x_hi * 2 + 1 - me.core) * GW, GW)
            w_core.append(go(wg_ref.at[rows, there], wr1.at[x_hi, rows, :], ws.at[x_hi, k], wr.at[x_hi, k], me.other_core()))

    def from_core(k, first, size):
        rows = slice(first, first + size)
        for x_hi in range(2):
            w_core[2 * k + x_hi].wait_recv()
            here = lanes_at((x_hi * 2 + me.core) * GW, GW)
            s1[x_hi, rows, :] = (wg_ref[rows, here].astype(F32) + wr1[x_hi, rows, :].astype(F32)).astype(BF)

    def x_copy(u, src, dst, kind, to):
        return remote(src, dst, xs.at[kind, u], xr.at[kind, u], to)

    def to_opposite(u, z):
        src = s1.at[1 - me.x_hi, unit_rows(u), :]
        dst = wr2.at[0, unit_rows(u), :]
        pl.when((u // 2) % 2 == 0)(lambda: x_copy(u, src, dst, 0, right).start())
        pl.when((u // 2) % 2 == 1)(lambda: x_copy(u, src, dst, 0, left).start())

    def straight(u):
        rows = unit_rows(u)
        x_copy(u, s1.at[hi_left, rows, :], wr2.at[2, rows, :], 2, left).start()
        x_copy(u, s1.at[hi_right, rows, :], wr2.at[1, rows, :], 1, right).start()

    def straight_opposite(u, z):
        rows = unit_rows(u)
        x_copy(u, s1.at[1 - me.x_hi, rows, :], wr2.at[0, rows, :], 0, me.far()).start()

    def pass_on(u):
        rows = unit_rows(u)
        pl.when((u // 2) % 2 == 0)(lambda: x_copy(u, s1.at[hi_left, rows, :], wr2.at[2, rows, :], 2, left).start())
        pl.when((u // 2) % 2 == 1)(lambda: x_copy(u, s1.at[hi_right, rows, :], wr2.at[1, rows, :], 1, right).start())
        x_copy(u, s1.at[0, rows, :], wr2.at[0, rows, :], 0, right).wait_recv()

        @pl.when((u // 2) % 2 == 0)
        def _():
            w_mid[rows, :] = (s1[hi_right, rows, :].astype(F32) + wr2[0, rows, :].astype(F32)).astype(BF)
            x_copy(u, w_mid.at[rows, :], wr2.at[1, rows, :], 1, right).start()

        @pl.when((u // 2) % 2 == 1)
        def _():
            w_mid[rows, :] = (s1[hi_left, rows, :].astype(F32) + wr2[0, rows, :].astype(F32)).astype(BF)
            x_copy(u, w_mid.at[rows, :], wr2.at[2, rows, :], 2, left).start()


    def z_copy(u, z):
        distance = (z + NZ - me.z) % NZ
        return remote(zout.at[unit_rows(u), :], zbuf.at[distance], zs.at[u], zr.at[distance], me.id(z=z))

    def over_x(u, z):
        rows = unit_rows(u)
        x_copy(u, s1.at[0, rows, :], wr2.at[1, rows, :], 1, right).wait_recv()
        x_copy(u, s1.at[0, rows, :], wr2.at[2, rows, :], 2, left).wait_recv()
        zout[rows, :] = (
            s1[me.x_hi, rows, :].astype(F32) + wr2[1, rows, :].astype(F32) + wr2[2, rows, :].astype(F32)
        ).astype(BF)
        pl.when(z != me.z)(lambda: z_copy(u, z).start())

    def over_x_straight(u, z):
        rows = unit_rows(u)
        for kind in range(3):
            x_copy(u, s1.at[0, rows, :], wr2.at[kind, rows, :], kind, right).wait_recv()
        zout[rows, :] = (
            s1[me.x_hi, rows, :].astype(F32) + wr2[0, rows, :].astype(F32)
            + wr2[1, rows, :].astype(F32) + wr2[2, rows, :].astype(F32)
        ).astype(BF)
        pl.when(z != me.z)(lambda: z_copy(u, z).start())


    wg_ref[:QW, :] = jnp.dot(dq_ref[...], n_ref[...], preferred_element_type=F32).astype(BF)
    for h in range(OWN - 1):
        finish(h)
        weight_rows(h)
    to_core(0, 288)
    to_core(384, 96)
    from_core(0, 0, 288)
    from_core(1, 384, 96)
    each_unit(me, to_opposite, None, EARLY)
    finish(OWN - 1)
    dq_own[...] = dq_ref[...].T
    gain_terms = jnp.zeros((8, D), F32)
    for r in (2, 1, 3, 0):
        at = (y + r) % NY
        rows = rows_at(at * TOK, TOK)
        first_rows = rows_at(at * TOK, half)
        rest_rows = rows_at(at * TOK + half, half)
        part = jnp.dot(dq_own[rows, :], w_ref[:QW, :], preferred_element_type=F32) + jnp.dot(
            out_ref[rows, :], wuse[...], preferred_element_type=F32
        )
        dn_ref[rows, :] = part.astype(BF)
        if r == 2:
            h_up = go(dn_ref.at[first_rows, :], half_r.at[0], ns.at[0], nr.at[0], up)
            h_down = go(dn_ref.at[rest_rows, :], half_r.at[1], ns.at[1], nr.at[1], down)
            weight_rows(OWN - 1)
            to_core(288, 96)
            to_core(480, 96)
        if r == 1:
            f_rest = [go(dn_ref.at[rest_rows, :], full_r.at[0, pl.ds(half, half), :], ns.at[4], nr.at[4], up)]
        if r == 3:
            f_rest.append(go(dn_ref.at[first_rows, :], full_r.at[1, pl.ds(0, half), :], ns.at[5], nr.at[5], down))
        terms = part * n_ref[rows, :].astype(F32)
        gain_terms = gain_terms + jnp.sum(terms.reshape(TOK // 8, 8, D), axis=0)
    gain_terms = jnp.sum(gain_terms, axis=0, keepdims=True)
    gg_ref[...] = jnp.zeros((16, 128), F32)
    for k in range(D // 128):
        gg_ref[k : k + 1, :] = gain_terms[:, k * 128 : (k + 1) * 128]
    gcore[me.core] = gg_ref[...]
    g_core = go(gg_ref, gcore.at[me.core], gs.at[0], gr.at[0], me.other_core())
    from_core(2, 288, 96)
    from_core(3, 480, 96)
    each_unit(me, to_opposite, None, LATE)
    each_unit(me, None, pass_on, EARLY)
    g_core.wait_recv()
    gy[y] = gcore[0] + gcore[1]
    g_y = [go(gy.at[y], gy.at[y], gs.at[r], gr.at[r], me.along_y(r)) for r in range(1, NY)]
    h_up.wait_recv()
    block = rows_at(((y + 1) % NY) * TOK, half)
    to_up[...] = (dn_ref[block, :].astype(F32) + half_r[0].astype(F32)).astype(BF)
    f_up = go(to_up, full_r.at[0, pl.ds(0, half), :], ns.at[2], nr.at[2], up)
    h_down.wait_recv()
    block = rows_at(((y + 3) % NY) * TOK + half, half)
    to_down[...] = (dn_ref[block, :].astype(F32) + half_r[1].astype(F32)).astype(BF)
    f_down = go(to_down, full_r.at[1, pl.ds(half, half), :], ns.at[3], nr.at[3], down)

    each_unit(me, None, pass_on, LATE)
    each_unit(me, over_x, None, EARLY)
    for c in g_y:
        c.wait_recv()
    gx[x_at] = gy[0] + gy[1] + gy[2] + gy[3]
    g_x = [go(gx.at[x_at], gx.at[x_at], gs.at[3 + r], gr.at[3 + r], me.along_x(r)) for r in range(1, 4)]

    each_unit(me, over_x, None, LATE)
    for c in g_x:
        c.wait_recv()
    gz[me.z] = gx[0] + gx[1] + gx[2] + gx[3]
    g_z = [go(gz.at[me.z], gz.at[me.z], gs.at[6 + r], gr.at[6 + r], me.along_z(r)) for r in range(1, NZ)]

    own_place = rows_at(me.place * UNIT, UNIT)

    def y_copy(k):
        return remote(yout.at[k], w_sums.at[own_place, :], ys.at[k], yr.at[me.place], me.sources[k])

    @pl.when(me.has)
    def _():
        total = zout[unit_rows(me.unit), :].astype(F32)
        for r in range(1, NZ):
            remote(zbuf.at[r], zbuf.at[r], zs.at[0], zr.at[r], me.along_z(r)).wait_recv()
            total = total + zbuf[r].astype(F32)
        for k in range(NY):
            part = total[:, k * SLAB : (k + 1) * SLAB]
            yout[k] = jnp.concatenate([part, jnp.zeros((UNIT, 128 - SLAB), F32)], axis=1)

    for k in range(NY):
        pl.when(me.gets[k])(lambda: y_copy(k).start())

        @pl.when(me.keeps[k])
        def _():
            w_sums[own_place, :] = yout[k]

    x = x_ref[...].astype(F32)
    centred = x - jnp.mean(x, axis=1, keepdims=True)
    spread = jnp.mean(centred * centred, axis=1, keepdims=True)
    scale = lax.rsqrt(spread + EPS)
    hat = centred * scale
    for c in f_rest + [f_up, f_down]:
        c.wait_recv()
    d_normed = (
        dn_ref[rows_at(y * TOK, TOK), :].astype(F32) + full_r[0].astype(F32) + full_r[1].astype(F32)
    )
    inner = to_natural(d_normed) * gain_ref[...].astype(F32)
    first_mean = jnp.mean(inner, axis=1, keepdims=True)
    second = jnp.mean(inner * hat, axis=1, keepdims=True)
    dx_ref[...] = (scale * (inner - first_mean - hat * second)).astype(BF)

    for c in g_z:
        c.wait_recv()
    total = gz[0]
    for k in range(1, NZ):
        total = total + gz[k]
    total = jnp.concatenate([total[k : k + 1, :] for k in range(D // 128)], axis=1)
    gout_ref[...] = to_natural(total) / gain_ref[...].astype(F32) * FACTOR

    for j in range(SHARD):
        rows = pl.ds(j * UNIT, UNIT)
        pl.when(me.sends[j])(
            lambda: remote(w_sums.at[rows, :], w_sums.at[rows, :], ys.at[0], yr.at[j], me.homes[j]).wait_recv()
        )
    for k in range(NY):
        pl.when(me.gets[k])(lambda: y_copy(k).wait_send())
    wout_ref[...] = w_sums[...][:, :SLAB] * FACTOR
    for c in ctx_copies:
        c.wait_recv()
    ctx_ref[...] = ctx_out[...].T

    def sent_here(u, z):
        rows = unit_rows(u)
        x_copy(u, w_mid.at[rows, :], wr2.at[0, rows, :], 0, right).wait_send()
        pl.when(z != me.z)(lambda: z_copy(u, z).wait_send())

    def sent_there(u):
        rows = unit_rows(u)
        x_copy(u, w_mid.at[rows, :], wr2.at[1, rows, :], 1, right).wait_send()
        x_copy(u, w_mid.at[rows, :], wr2.at[2, rows, :], 2, left).wait_send()

    each_unit(me, sent_here, sent_there, ((0, UNITS),))
    for c in sent:
        c.wait_send()


def block(x, gain, w, cot):
    return pl.pallas_call(
        block_kernel,
        out_shape=(
            jax.ShapeDtypeStruct((TOK, NY * QW), BF),
            jax.ShapeDtypeStruct((TOK, D), BF),
            jax.ShapeDtypeStruct((BLOCK, SLAB), F32),
            jax.ShapeDtypeStruct((1, D), F32),
        ),
        in_specs=[pl.BlockSpec(memory_space=pl.ANY)] * 4,
        out_specs=(VMEM,) * 4,
        scratch_shapes=[
            pltpu.VMEM((TOK, D), BF),
            pltpu.VMEM((1, D), BF),
            pltpu.VMEM((BLOCK, SLAB), BF),
            pltpu.VMEM((TOK, NY * QW), BF),
            pltpu.VMEM((ROWS, D), BF),
            pltpu.VMEM((PW, D), BF),
            pltpu.VMEM((QW, ROWS), BF),
            pltpu.VMEM((BLOCK, 128), BF),
            pltpu.VMEM((NY * QW, TOK), BF),
            pltpu.VMEM((NY, UNIT, 128), BF),
            dma(4),
            dma(6), dma(6), dma(4), dma(4), dma(3), dma(4), dma(8), dma(8),
            dma(3, 8), dma(3, 8), dma(2), dma(2),
            pltpu.VMEM((2 * QW, D), BF),
            pltpu.VMEM((SEQ, 2 * QW), BF),
            pltpu.VMEM((SEQ, 2 * QW), BF),
            pltpu.VMEM((QW, ROWS), BF),
            pltpu.VMEM((NY * QW, TOK), BF),
            pltpu.VMEM((QW, ROWS), BF),
            pltpu.VMEM((ROWS, QW), BF),
            pltpu.VMEM((ROWS, 2 * QW), BF),
            pltpu.VMEM((SEQ, ROWS), F32),
            pltpu.VMEM((SEQ, ROWS), BF),
            pltpu.VMEM((2, ROWS, 2 * QW), BF),
            pltpu.VMEM((ROWS, 2 * QW), BF),
            pltpu.VMEM((ROWS, 2 * QW), BF),
            dma(3, 3), dma(3, 3), dma(3, 3), dma(3, 3), dma(3, 4), dma(3, 4),
            pltpu.VMEM((ROWS, D), BF),
            pltpu.VMEM((PW, D), BF),
            pltpu.VMEM((16, 128), F32),
            pltpu.VMEM((BLOCK, 128), F32),
            pltpu.VMEM((2, TOK // 2, D), BF),
            pltpu.VMEM((TOK // 2, D), BF),
            pltpu.VMEM((TOK // 2, D), BF),
            pltpu.VMEM((2, TOK, D), BF),
            pltpu.VMEM((2, PW, GW), BF),
            pltpu.VMEM((2, PW, GW), BF),
            pltpu.VMEM((3, PW, GW), BF),
            pltpu.VMEM((PW, GW), BF),
            pltpu.VMEM((PW, GW), BF),
            pltpu.VMEM((NZ, UNIT, GW), BF),
            pltpu.VMEM((NY, UNIT, 128), F32),
            pltpu.VMEM((2, 16, 128), F32),
            pltpu.VMEM((NY, 16, 128), F32),
            pltpu.VMEM((4, 16, 128), F32),
            pltpu.VMEM((NZ, 16, 128), F32),
            dma(6), dma(6), dma(2, 4), dma(2, 4), dma(3, 12), dma(3, 12), dma(12), dma(8),
            dma(4), dma(3), dma(14), dma(14),
        ],
        compiler_params=pltpu.CompilerParams(
            collective_id=0, has_side_effects=True, vmem_limit_bytes=56 * 2**20
        ),
        name="block",
    )(x, gain, w, cot)


def hand_over_kernel(a, b, c, g, a_out, b_out, c_out, g_out):
    a_out[...] = a[...]
    b_out[...] = b[...]
    c_out[...] = c[...]
    g_out[...] = g[...].reshape(D)


def hand_over(*arrays):
    shapes = [jax.ShapeDtypeStruct(v.shape, v.dtype) for v in arrays[:3]]
    return pl.pallas_call(
        hand_over_kernel,
        out_shape=tuple(shapes) + (jax.ShapeDtypeStruct((D,), F32),),
        in_specs=[VMEM] * 4,
        out_specs=(VMEM,) * 4,
        name="hand_over",
    )(*arrays)


def shards(tokens, norm_gain, qkv_weight, d_context):
    outputs = block(tokens[0], norm_gain[None, :], qkv_weight.T, d_context[0])
    context, d_tokens, weight_grad, gain_grad = hand_over(*outputs)
    return (context[None], d_tokens[None], weight_grad.T, gain_grad)


def solution(mesh):
    in_specs = (P("dp", "sp", None), P(), P("sp", "dp"), P("dp", "sp", None))
    out_specs = (P("dp", "sp", None), P("dp", "sp", None), P("sp", "dp"), P())
    return jax.shard_map(shards, mesh=mesh, in_specs=in_specs, out_specs=out_specs, check_vma=False)
```

```python
import functools
import math

import jax
import jax.numpy as jnp
from jax import lax
from jax.experimental import pallas as pl
from jax.experimental.pallas import tpu as pltpu
from jax.sharding import PartitionSpec as P

MESH = pl.DeviceIdType.MESH
BF = jnp.bfloat16
F32 = jnp.float32

D = 1536
HEAD = 64
OWN = 3
TOK = 128
NY = 4
NZ = 8
NA = 4
ROWS = NY * TOK
SEQ = NA * ROWS
QW = OWN * HEAD
PW = 3 * QW
SLAB = 96
BLOCK = 144
GW = NY * SLAB
EPS = 1e-05
VMEM = pl.BlockSpec(memory_space=pltpu.VMEM)


class Place:
    def __init__(self):
        d, s = lax.axis_index("dp"), lax.axis_index("sp")
        self.x_lo, self.z = d // NZ, d % NZ
        self.x_hi, self.y, self.core = s // 8, (s // 2) % NY, s % 2
        self.group = self.x_hi * 2 + self.core
        self.far_group = (1 - self.x_hi) * 2 + self.core

    def id(self, x_hi=None, x_lo=None, y=None, z=None, core=None):
        x_hi = self.x_hi if x_hi is None else x_hi
        x_lo = self.x_lo if x_lo is None else x_lo
        y = self.y if y is None else y
        z = self.z if z is None else z
        core = self.core if core is None else core
        return {"dp": x_lo * NZ + z, "sp": x_hi * 8 + y * 2 + core}

    def find_units(self):
        self.homes, self.sends = [], []
        for j in range(SHARD):
            y, u = shard_unit(self, j)
            x_lo, z = unit_home(u, y)
            self.homes.append(self.id(x_lo=x_lo, z=z, y=y))
            self.sends.append((y != self.y) | (x_lo != self.x_lo) | (z != self.z))
        self.starts = [((16 * k + 4 * self.y) // SHARD) % NZ for k in range(SHARD)]
        self.has, self.unit = unit_at(self.x_lo, self.z, self.starts)
        volume, self.place = unit_source(self.unit, self.y)
        elsewhere = volume != self.x_lo * NZ + self.z
        self.sources = [self.id(x_lo=volume // NZ, z=volume % NZ, y=k) for k in range(NY)]
        self.gets = [self.has & ((self.y != k) | elsewhere) for k in range(NY)]
        self.keeps = [self.has & (self.y == k) & jnp.logical_not(elsewhere) for k in range(NY)]

    def other_core(self):
        return self.id(core=1 - self.core)

    def mirror(self):
        return self.id(x_hi=1 - self.x_hi, x_lo=1 - self.x_lo)

    def beside(self):
        return self.id(x_lo=1 - self.x_lo)

    def far(self):
        return self.id(x_hi=1 - self.x_hi)

    def along_y(self, step):
        return self.id(y=(self.y + step) % NY)

    def along_z(self, step):
        return self.id(z=(self.z + step) % NZ)

    def along_x(self, step):
        x = (self.x_hi * 2 + self.x_lo + step) % 4
        return self.id(x_hi=x // 2, x_lo=x % 2)


def greet(me):
    barrier = pltpu.get_barrier_semaphore()
    partners = (
        [me.along_z(r) for r in range(1, NZ)]
        + [me.along_y(r) for r in range(1, NY)]
        + [me.along_x(r) for r in range(1, 4)]
        + [me.other_core()]
    )

    def tell(partner):
        pl.semaphore_signal(barrier, inc=1, device_id=partner, device_id_type=MESH)

    for partner in partners:
        tell(partner)
    count = jnp.int32(len(partners))
    for j in range(SHARD):
        pl.when(me.sends[j])(lambda: tell(me.homes[j]))
        count = count + me.sends[j].astype(jnp.int32)
    for k in range(NY):
        pl.when(me.gets[k])(lambda: tell(me.sources[k]))
        count = count + me.gets[k].astype(jnp.int32)
    return functools.partial(pl.semaphore_wait, barrier, count)


def remote(src, dst, send, recv, partner):
    return pltpu.make_async_remote_copy(
        src_ref=src, dst_ref=dst, send_sem=send, recv_sem=recv, device_id=partner, device_id_type=MESH
    )


def rows_at(start, size):
    return pl.ds(pl.multiple_of(start, 16), size)


def lanes_at(start, size):
    return pl.ds(pl.multiple_of(start, 128), size)


def to_grouped(wide):
    parts = []
    for x_hi in range(2):
        for core in range(2):
            for y in range(NY):
                s = x_hi * 8 + y * 2 + core
                parts.append(wide[:, s * SLAB : (s + 1) * SLAB])
    return jnp.concatenate(parts, axis=1)


def to_natural(wide):
    parts = []
    for x_hi in range(2):
        for y in range(NY):
            for core in range(2):
                s = (x_hi * 2 + core) * NY + y
                parts.append(wide[:, s * SLAB : (s + 1) * SLAB])
    return jnp.concatenate(parts, axis=1)


UNIT = 48
UNITS = 12
SHARD = 3


def unit_source(u, y):
    column = (u // 4) * 16 + 4 * y + u % 4
    return column // SHARD, column % SHARD


def unit_home(u, y):
    return u % 2, ((16 * (u // 4) + 4 * y) // SHARD + (u % 4) // 2) % NZ


def unit_at(x_lo, z, starts):
    found, unit = jnp.int32(0), jnp.int32(0)
    for k in range(SHARD):
        ahead = z - starts[k]
        for h in range(2):
            hit = ((ahead == h) | (ahead == h - NZ)).astype(jnp.int32)
            found, unit = found + hit, unit + hit * (4 * k + 2 * h)
    return found > 0, unit + x_lo


def shard_unit(me, j):
    column = (me.x_lo * NZ + me.z) * SHARD + j
    return (column % 16) // 4, (column // 16) * 4 + column % 4


def each_unit(me, here, there, spans):
    def step(u, carry):
        k, i = u // 4, u % 4
        z = jnp.where(k == 0, me.starts[0], jnp.where(k == 1, me.starts[1], me.starts[2])) + i // 2
        x_lo, z = i % 2, jnp.where(z >= NZ, z - NZ, z)
        if here is not None:
            pl.when(x_lo == me.x_lo)(lambda: here(u, z))
        if there is not None:
            pl.when(x_lo != me.x_lo)(lambda: there(u))
        return carry

    for first, end in spans:
        lax.fori_loop(first, end, step, 0)


def near_first(me, x_lo, act, first=0, end=NZ):
    def step(n, carry):
        r = jnp.where(n % 2 == 1, (n + 1) // 2, (NZ - n // 2) % NZ)
        z = me.z - r
        has, u = unit_at(x_lo, jnp.where(z < 0, z + NZ, z), me.starts)
        pl.when(has)(lambda: act(r, u))
        return carry

    lax.fori_loop(first, end, step, 0)


def unit_rows(u):
    return rows_at(u * UNIT, UNIT)


def gather_phase(me, ready, load, x_ref, gain_ref, raw_ref, cot_ref, nall, wall, cots,
                 w_ref, cot_t, ybuf, ns, nr, cs, cr, ys, yr, zs, zr, xs, xr, ds, dr):
    y = me.y
    right, left = me.along_x(1), me.along_x(3)
    x_at = me.x_hi * 2 + me.x_lo
    own = lanes_at(me.group * GW, GW)
    far = lanes_at(me.far_group * GW, GW)
    hi_left, hi_right = ((x_at + 3) % 4) // 2, ((x_at + 1) % 4) // 2
    of_left = lanes_at((hi_left * 2 + me.core) * GW, GW)
    of_right = lanes_at((hi_right * 2 + me.core) * GW, GW)
    load(raw_ref)
    w_ref[...] = jnp.concatenate([raw_ref[...], jnp.zeros((BLOCK, 128 - SLAB), BF)], axis=1)
    ready()

    def y_copy(j):
        return remote(w_ref.at[pl.ds(j * UNIT, UNIT), :], ybuf.at[y], ys.at[j], yr.at[y], me.homes[j])

    for j in range(SHARD):
        pl.when(me.sends[j])(lambda: y_copy(j).start())

    load(x_ref)
    x = x_ref[...].astype(F32)
    centred = x - jnp.mean(x, axis=1, keepdims=True)
    spread = jnp.mean(centred * centred, axis=1, keepdims=True)
    normed = centred * lax.rsqrt(spread + EPS) * gain_ref[...].astype(F32)
    tok_rows = rows_at(y * TOK, TOK)
    nall[tok_rows, :] = to_grouped(normed).astype(BF)
    up, down = me.along_y(1), me.along_y(3)
    half = TOK // 2
    low, high = rows_at(y * TOK, half), rows_at(y * TOK + half, half)

    def n_copy(rows, k, to):
        c = remote(nall.at[rows, :], nall.at[rows, :], ns.at[k], nr.at[k], to)
        c.start()
        return c

    n_up, n_down = n_copy(low, 0, up), n_copy(high, 1, down)
    n_rest = [n_copy(high, 4, up), n_copy(low, 5, down)]
    for k in range(NY):
        pl.when(me.gets[k])(lambda: remote(ybuf.at[k], ybuf.at[k], ys.at[0], yr.at[k], me.sources[k]).wait_recv())

        @pl.when(me.keeps[k])
        def _():
            ybuf[k] = w_ref[rows_at(me.place * UNIT, UNIT), :]

    @pl.when(me.has)
    def _():
        parts = [ybuf[k][:, :SLAB].astype(F32) for k in range(NY)]
        wall[unit_rows(me.unit), own] = jnp.concatenate(parts, axis=1).astype(BF)

    def piece(u, lanes):
        return wall.at[unit_rows(u), lanes]

    def z_copy(u, r):
        return remote(piece(u, own), piece(u, own), zs.at[r], zr.at[r], me.along_z(r))

    def x_copy(u, r, lanes, kind, to):
        return remote(piece(u, lanes), piece(u, lanes), xs.at[kind, r], xr.at[kind, r], to)

    @pl.when(me.has)
    def _():
        for r in (1, 7, 2, 6, 3, 5, 4):
            z_copy(me.unit, r).start()

    cot_copies = []
    load(cot_ref)
    cot_t[...] = cot_ref[...].T
    cot_lanes = lanes_at(y * TOK, TOK)
    for r in range(1, NY):
        to = (y + r) % NY
        c = remote(cot_t.at[rows_at(to * QW, QW), :], cots.at[:, cot_lanes], cs.at[r], cr.at[r], me.along_y(r))
        c.start()
        cot_copies.append(c)
    cots[:, cot_lanes] = cot_t[rows_at(y * QW, QW), :]

    def spread_x(r, u):
        pl.when(r != 0)(lambda: z_copy(u, r).wait_recv())
        x_copy(u, r, own, 0, right).start()
        x_copy(u, r, own, 1, left).start()

    near_first(me, me.x_lo, spread_x, 0, 3)
    from_down = rows_at(((y + 3) % NY) * TOK, half)
    from_up = rows_at(((y + 1) % NY) * TOK + half, half)
    n_up.wait_recv()
    f_up = n_copy(from_down, 2, up)
    n_down.wait_recv()
    f_down = n_copy(from_up, 3, down)
    near_first(me, me.x_lo, spread_x, 3, NZ)

    def relay(r, u):
        x_copy(u, r, of_left, 0, right).wait_recv()
        pl.when((u // 2) % 2 == 0)(lambda: x_copy(u, r, of_left, 2, right).start())
        x_copy(u, r, of_right, 1, left).wait_recv()
        pl.when((u // 2) % 2 == 1)(lambda: x_copy(u, r, of_right, 2, left).start())

    near_first(me, 1 - me.x_lo, relay)
    near_first(me, me.x_lo, lambda r, u: x_copy(u, r, far, 2, right).wait_recv())

    core_copies = []
    for x_hi in range(2):
        lanes = lanes_at((x_hi * 2 + me.core) * GW, GW)
        c = remote(wall.at[:, lanes], wall.at[:, lanes], ds.at[x_hi], dr.at[x_hi], me.other_core())
        c.start()
        core_copies.append(c)
    for c in core_copies:
        c.wait_recv()
    for c in n_rest + [f_up, f_down]:
        c.wait_recv()
    for c in cot_copies:
        c.wait_recv()

    def drain():
        @pl.when(me.has)
        def _():
            for r in range(1, NZ):
                z_copy(me.unit, r).wait_send()

        def sent_here(r, u):
            x_copy(u, r, own, 0, right).wait_send()
            x_copy(u, r, own, 1, left).wait_send()

        near_first(me, me.x_lo, sent_here)
        near_first(me, 1 - me.x_lo, lambda r, u: x_copy(u, r, own, 2, right).wait_send())
        for j in range(SHARD):
            pl.when(me.sends[j])(lambda: y_copy(j).wait_send())
        for c in cot_copies + core_copies + n_rest + [n_up, n_down, f_up, f_down]:
            c.wait_send()

    return drain


def dma(*shape):
    return pltpu.SemaphoreType.DMA(shape)


FACTOR = 1.0 / math.sqrt(16 * SEQ)
CHUNK = 256
EARLY = ((0, 6), (8, 10))
LATE = ((6, 8), (10, 12))


def block_kernel(x_hbm, gain_in, w_hbm, cot_hbm, ctx_ref, dx_ref, wout_ref, gout_ref,
                 x_ref, gain_ref, shard_ref, d_ctx, n_ref, w_ref, cot_ref, w_pad, cot_t, ybuf, ls,
                 *rest):
    me = Place()
    y = me.y
    me.find_units()
    ready = greet(me)
    gain_ref[...] = gain_in[...].astype(F32).reshape(1, D)
    loads = {}
    for k, (src, dst) in enumerate(
        ((w_hbm, shard_ref), (x_hbm, x_ref), (cot_hbm, d_ctx))
    ):
        c = pltpu.make_async_copy(src, dst, ls.at[k])
        c.start()
        loads[id(dst)] = c
    drain = gather_phase(
        me, ready, lambda ref: loads[id(ref)].wait(), x_ref, gain_ref, shard_ref, d_ctx,
        n_ref, w_ref, cot_ref, w_pad, cot_t, ybuf, *rest[:12],
    )
    back_phase(
        me, drain, n_ref, w_ref, cot_ref, x_ref, gain_ref, ctx_ref, dx_ref, wout_ref, gout_ref, *rest[12:]
    )


def back_phase(me, drain, n_ref, w_ref, cot_ref, x_ref, gain_ref, ctx_ref, dx_ref, wout_ref, gout_ref,
               wuse, kvall, dkv, ctx_own, ctx_out, dq_ref, dq_own, out_ref, s_buf, e_buf, r1, mid, r2,
               ks, kr, ss, rs, cs, cr,
               dn_ref, wg_ref, gg_ref, w_sums,
               half_r, to_up, to_down, full_r, s1, wr1, wr2, w_mid, zout, zbuf, yout,
               gcore, gy, gx, gz,
               ns, nr, ws, wr, xs, xr, zs, zr, ys, yr, gs, gr):
    y = me.y
    own = rows_at(me.group * ROWS, ROWS)
    far = rows_at(me.far_group * ROWS, ROWS)
    near = me.x_hi * 2 + 1 - me.core
    beyond = (1 - me.x_hi) * 2 + 1 - me.core
    own_there = rows_at(near * ROWS, ROWS)
    far_there = rows_at(beyond * ROWS, ROWS)
    groups = (me.group, near, me.far_group, beyond)

    def chunks(at):
        for i in range(ROWS // CHUNK):
            here = at * ROWS + i * CHUNK
            yield rows_at(groups[at] * ROWS + i * CHUNK, CHUNK), slice(here, here + CHUNK)

    mine = y * QW
    sent = []

    def go(*args):
        c = remote(*args)
        c.start()
        sent.append(c)
        return c

    def head_lanes(h):
        return slice(h * 128, (h + 1) * 128)

    nt = (((1,), (1,)), ((), ()))
    k_far, k_core = [], []
    for h in range(OWN):
        lanes = head_lanes(h)
        for which in range(2):
            row = QW * (1 + which) + h * HEAD
            wuse[h * 128 + which * HEAD : h * 128 + (which + 1) * HEAD, :] = w_ref[row : row + HEAD, :]
        kvall[own, lanes] = lax.dot_general(n_ref[...], wuse[lanes, :], nt, preferred_element_type=F32).astype(BF)
        k_far.append(go(kvall.at[own, lanes], kvall.at[own, lanes], ks.at[0, h], kr.at[0, h], me.far()))
        k_core.append(go(kvall.at[own, lanes], kvall.at[own, lanes], ks.at[1, h], kr.at[1, h], me.other_core()))
    queries = lax.dot_general(w_ref[:QW, :], n_ref[...], nt, preferred_element_type=F32).astype(BF)
    k_pass = []
    d_far, d_own, d_x, ctx_copies = [], [], [], []

    def pass_keys(h):
        k_far[h].wait_recv()
        k_pass.append(go(kvall.at[far, head_lanes(h)], kvall.at[far, head_lanes(h)], ks.at[2, h], kr.at[2, h], me.other_core()))

    def pass_sums(h):
        lanes = head_lanes(h)
        d_far[h].wait_recv()
        mid[:, lanes] = (dkv[far, lanes].astype(F32) + r1[0, :, lanes].astype(F32)).astype(BF)
        d_x.append(go(mid.at[:, lanes], r2.at[:, lanes], ss.at[2, h], rs.at[2, h], me.far()))

    def finish(h):
        lanes = head_lanes(h)
        d_own[h].wait_recv()
        d_x[h].wait_recv()
        out_ref[:, lanes] = (
            dkv[own, lanes].astype(F32) + r1[1, :, lanes].astype(F32) + r2[:, lanes].astype(F32)
        ).astype(BF)

    zeros = jnp.zeros((HEAD, ROWS), BF)
    q_pads, tops = [], []

    def score(h, at):
        for keys, rows in chunks(at):
            s = jnp.dot(kvall[keys, head_lanes(h)], q_pads[h], preferred_element_type=F32)
            s_buf[h, rows, :] = s
            tops[h] = jnp.maximum(tops[h], jnp.max(s.reshape(CHUNK // 8, 8, ROWS), axis=0))

    for h in range(OWN):
        q = queries[h * HEAD : (h + 1) * HEAD, :] * jnp.asarray(HEAD**-0.5, BF)
        q_pads.append(jnp.concatenate([q, zeros], axis=0))
        tops.append(jnp.full((8, ROWS), -jnp.inf, F32))
        score(h, 0)
    for h in range(OWN):
        k_core[h].wait_recv()
        score(h, 1)
    drain()
    pass_keys(0)
    for h in range(OWN):
        lanes = head_lanes(h)
        head_rows = slice(h * HEAD, (h + 1) * HEAD)
        q_pad = q_pads[h]
        score(h, 2)
        k_pass[h].wait_recv()
        score(h, 3)
        top = tops[h]
        top = jnp.max(top, axis=0, keepdims=True)
        total = jnp.zeros((8, ROWS), F32)
        ctx = jnp.zeros((HEAD, ROWS), F32)
        for at in range(NA):
            for keys, rows in chunks(at):
                e = jnp.exp(s_buf[h, rows, :] - top)
                total = total + jnp.sum(e.reshape(CHUNK // 8, 8, ROWS), axis=0)
                e_low = e.astype(BF)
                e_buf[rows, :] = e_low
                v_t = kvall[keys, lanes].T[HEAD:, :]
                ctx = ctx + jnp.dot(v_t, e_low, preferred_element_type=F32)
        inverse = 1.0 / jnp.sum(total, axis=0, keepdims=True)
        ctx = ctx * inverse
        ctx_own[head_rows, :] = ctx.astype(BF)
        rows_there = rows_at(mine + h * HEAD, HEAD)
        for r in range(1, NY):
            to = lanes_at(((y + r) % NY) * TOK, TOK)
            ctx_copies.append(go(ctx_own.at[head_rows, to], ctx_out.at[rows_there, :], cs.at[h, r], cr.at[h, r], me.along_y(r)))
        ctx_out[rows_there, :] = ctx_own[head_rows, lanes_at(y * TOK, TOK)]
        if h + 1 < OWN:
            pass_keys(h + 1)
        cot = (cot_ref[head_rows, :].astype(F32) * inverse).astype(BF)
        row_dot = jnp.sum(cot.astype(F32) * ctx, axis=0, keepdims=True)
        cot_pad = jnp.concatenate([zeros, cot], axis=0)
        q_side = q_pad.T
        cot_side = cot_pad.T
        dq = jnp.zeros((HEAD, ROWS), F32)
        for at in (3, 2, 1, 0):
            for keys, rows in chunks(at):
                d_attn = jnp.dot(kvall[keys, lanes], cot_pad, preferred_element_type=F32)
                e_low = e_buf[rows, :]
                slopes = (e_low.astype(F32) * (d_attn - row_dot)).astype(BF)
                k_t = kvall[keys, lanes].T[:HEAD, :]
                dq = dq + jnp.dot(k_t, slopes, preferred_element_type=F32)
                dkv[keys, lanes] = (
                    jnp.dot(slopes, q_side, preferred_element_type=F32)
                    + jnp.dot(e_low, cot_side, preferred_element_type=F32)
                ).astype(BF)
            if at == 3:
                d_far.append(go(dkv.at[far_there, lanes], r1.at[0, :, lanes], ss.at[0, h], rs.at[0, h], me.other_core()))
            if at == 1:
                d_own.append(go(dkv.at[own_there, lanes], r1.at[1, :, lanes], ss.at[1, h], rs.at[1, h], me.other_core()))
                pass_sums(h)
        dq_ref[head_rows, :] = (dq * HEAD**-0.5).astype(BF)

    right, left = me.along_x(1), me.along_x(3)
    x_at = me.x_hi * 2 + me.x_lo
    hi_left, hi_right = ((x_at + 3) % 4) // 2, ((x_at + 1) % 4) // 2
    half = TOK // 2
    up, down = me.along_y(1), me.along_y(3)
    opposite = (y + 2) % NY

    def weight_rows(h):
        rows = jnp.dot(out_ref[:, head_lanes(h)].T, n_ref[...], preferred_element_type=F32).astype(BF)
        for which in range(2):
            row = QW * (1 + which) + h * HEAD
            wg_ref[row : row + HEAD, :] = rows[which * HEAD : (which + 1) * HEAD, :]

    w_core = []

    def to_core(first, size):
        rows = pl.ds(first, size)
        k = len(w_core) // 2
        for x_hi in range(2):
            there = lanes_at((x_hi * 2 + 1 - me.core) * GW, GW)
            w_core.append(go(wg_ref.at[rows, there], wr1.at[x_hi, rows, :], ws.at[x_hi, k], wr.at[x_hi, k], me.other_core()))

    def from_core(k, first, size):
        rows = slice(first, first + size)
        for x_hi in range(2):
            w_core[2 * k + x_hi].wait_recv()
            here = lanes_at((x_hi * 2 + me.core) * GW, GW)
            s1[x_hi, rows, :] = (wg_ref[rows, here].astype(F32) + wr1[x_hi, rows, :].astype(F32)).astype(BF)

    def x_copy(u, src, dst, kind, to):
        return remote(src, dst, xs.at[kind, u], xr.at[kind, u], to)

    def to_opposite(u, z):
        src = s1.at[1 - me.x_hi, unit_rows(u), :]
        dst = wr2.at[0, unit_rows(u), :]
        pl.when((u // 2) % 2 == 0)(lambda: x_copy(u, src, dst, 0, right).start())
        pl.when((u // 2) % 2 == 1)(lambda: x_copy(u, src, dst, 0, left).start())

    def straight(u):
        rows = unit_rows(u)
        x_copy(u, s1.at[hi_left, rows, :], wr2.at[2, rows, :], 2, left).start()
        x_copy(u, s1.at[hi_right, rows, :], wr2.at[1, rows, :], 1, right).start()

    def straight_opposite(u, z):
        rows = unit_rows(u)
        x_copy(u, s1.at[1 - me.x_hi, rows, :], wr2.at[0, rows, :], 0, me.far()).start()

    def pass_on(u):
        rows = unit_rows(u)
        pl.when((u // 2) % 2 == 0)(lambda: x_copy(u, s1.at[hi_left, rows, :], wr2.at[2, rows, :], 2, left).start())
        pl.when((u // 2) % 2 == 1)(lambda: x_copy(u, s1.at[hi_right, rows, :], wr2.at[1, rows, :], 1, right).start())
        x_copy(u, s1.at[0, rows, :], wr2.at[0, rows, :], 0, right).wait_recv()

        @pl.when((u // 2) % 2 == 0)
        def _():
            w_mid[rows, :] = (s1[hi_right, rows, :].astype(F32) + wr2[0, rows, :].astype(F32)).astype(BF)
            x_copy(u, w_mid.at[rows, :], wr2.at[1, rows, :], 1, right).start()

        @pl.when((u // 2) % 2 == 1)
        def _():
            w_mid[rows, :] = (s1[hi_left, rows, :].astype(F32) + wr2[0, rows, :].astype(F32)).astype(BF)
            x_copy(u, w_mid.at[rows, :], wr2.at[2, rows, :], 2, left).start()


    def z_copy(u, z):
        distance = (z + NZ - me.z) % NZ
        return remote(zout.at[unit_rows(u), :], zbuf.at[distance], zs.at[u], zr.at[distance], me.id(z=z))

    def over_x(u, z):
        rows = unit_rows(u)
        x_copy(u, s1.at[0, rows, :], wr2.at[1, rows, :], 1, right).wait_recv()
        x_copy(u, s1.at[0, rows, :], wr2.at[2, rows, :], 2, left).wait_recv()
        zout[rows, :] = (
            s1[me.x_hi, rows, :].astype(F32) + wr2[1, rows, :].astype(F32) + wr2[2, rows, :].astype(F32)
        ).astype(BF)
        pl.when(z != me.z)(lambda: z_copy(u, z).start())

    def over_x_straight(u, z):
        rows = unit_rows(u)
        for kind in range(3):
            x_copy(u, s1.at[0, rows, :], wr2.at[kind, rows, :], kind, right).wait_recv()
        zout[rows, :] = (
            s1[me.x_hi, rows, :].astype(F32) + wr2[0, rows, :].astype(F32)
            + wr2[1, rows, :].astype(F32) + wr2[2, rows, :].astype(F32)
        ).astype(BF)
        pl.when(z != me.z)(lambda: z_copy(u, z).start())


    wg_ref[:QW, :] = jnp.dot(dq_ref[...], n_ref[...], preferred_element_type=F32).astype(BF)
    for h in range(OWN - 1):
        finish(h)
        weight_rows(h)
    to_core(0, 288)
    to_core(384, 96)
    from_core(0, 0, 288)
    from_core(1, 384, 96)
    each_unit(me, to_opposite, None, EARLY)
    finish(OWN - 1)
    weight_rows(OWN - 1)
    to_core(288, 96)
    to_core(480, 96)
    dq_own[...] = dq_ref[...].T
    gain_terms = jnp.zeros((8, D), F32)
    for r in (2, 1, 3, 0):
        at = (y + r) % NY
        rows = rows_at(at * TOK, TOK)
        first_rows = rows_at(at * TOK, half)
        rest_rows = rows_at(at * TOK + half, half)
        part = jnp.dot(dq_own[rows, :], w_ref[:QW, :], preferred_element_type=F32) + jnp.dot(
            out_ref[rows, :], wuse[...], preferred_element_type=F32
        )
        dn_ref[rows, :] = part.astype(BF)
        if r == 2:
            h_up = go(dn_ref.at[first_rows, :], half_r.at[0], ns.at[0], nr.at[0], up)
            h_down = go(dn_ref.at[rest_rows, :], half_r.at[1], ns.at[1], nr.at[1], down)
        if r == 1:
            f_rest = [go(dn_ref.at[rest_rows, :], full_r.at[0, pl.ds(half, half), :], ns.at[4], nr.at[4], up)]
        if r == 3:
            f_rest.append(go(dn_ref.at[first_rows, :], full_r.at[1, pl.ds(0, half), :], ns.at[5], nr.at[5], down))
        terms = part * n_ref[rows, :].astype(F32)
        gain_terms = gain_terms + jnp.sum(terms.reshape(TOK // 8, 8, D), axis=0)
    gain_terms = jnp.sum(gain_terms, axis=0, keepdims=True)
    gg_ref[...] = jnp.zeros((16, 128), F32)
    for k in range(D // 128):
        gg_ref[k : k + 1, :] = gain_terms[:, k * 128 : (k + 1) * 128]
    gcore[me.core] = gg_ref[...]
    g_core = go(gg_ref, gcore.at[me.core], gs.at[0], gr.at[0], me.other_core())
    from_core(2, 288, 96)
    from_core(3, 480, 96)
    each_unit(me, to_opposite, None, LATE)
    each_unit(me, None, pass_on, EARLY)
    g_core.wait_recv()
    gy[y] = gcore[0] + gcore[1]
    g_y = [go(gy.at[y], gy.at[y], gs.at[r], gr.at[r], me.along_y(r)) for r in range(1, NY)]
    h_up.wait_recv()
    block = rows_at(((y + 1) % NY) * TOK, half)
    to_up[...] = (dn_ref[block, :].astype(F32) + half_r[0].astype(F32)).astype(BF)
    f_up = go(to_up, full_r.at[0, pl.ds(0, half), :], ns.at[2], nr.at[2], up)
    h_down.wait_recv()
    block = rows_at(((y + 3) % NY) * TOK + half, half)
    to_down[...] = (dn_ref[block, :].astype(F32) + half_r[1].astype(F32)).astype(BF)
    f_down = go(to_down, full_r.at[1, pl.ds(half, half), :], ns.at[3], nr.at[3], down)

    each_unit(me, None, pass_on, LATE)
    each_unit(me, over_x, None, EARLY)
    for c in g_y:
        c.wait_recv()
    gx[x_at] = gy[0] + gy[1] + gy[2] + gy[3]
    g_x = [go(gx.at[x_at], gx.at[x_at], gs.at[3 + r], gr.at[3 + r], me.along_x(r)) for r in range(1, 4)]

    each_unit(me, over_x, None, LATE)
    for c in g_x:
        c.wait_recv()
    gz[me.z] = gx[0] + gx[1] + gx[2] + gx[3]
    g_z = [go(gz.at[me.z], gz.at[me.z], gs.at[6 + r], gr.at[6 + r], me.along_z(r)) for r in range(1, NZ)]

    own_place = rows_at(me.place * UNIT, UNIT)

    def y_copy(k):
        return remote(yout.at[k], w_sums.at[own_place, :], ys.at[k], yr.at[me.place], me.sources[k])

    @pl.when(me.has)
    def _():
        total = zout[unit_rows(me.unit), :].astype(F32)
        for r in range(1, NZ):
            remote(zbuf.at[r], zbuf.at[r], zs.at[0], zr.at[r], me.along_z(r)).wait_recv()
            total = total + zbuf[r].astype(F32)
        for k in range(NY):
            part = total[:, k * SLAB : (k + 1) * SLAB]
            yout[k] = jnp.concatenate([part, jnp.zeros((UNIT, 128 - SLAB), F32)], axis=1)

    for k in range(NY):
        pl.when(me.gets[k])(lambda: y_copy(k).start())

        @pl.when(me.keeps[k])
        def _():
            w_sums[own_place, :] = yout[k]

    x = x_ref[...].astype(F32)
    centred = x - jnp.mean(x, axis=1, keepdims=True)
    spread = jnp.mean(centred * centred, axis=1, keepdims=True)
    scale = lax.rsqrt(spread + EPS)
    hat = centred * scale
    for c in f_rest + [f_up, f_down]:
        c.wait_recv()
    d_normed = (
        dn_ref[rows_at(y * TOK, TOK), :].astype(F32) + full_r[0].astype(F32) + full_r[1].astype(F32)
    )
    inner = to_natural(d_normed) * gain_ref[...].astype(F32)
    first_mean = jnp.mean(inner, axis=1, keepdims=True)
    second = jnp.mean(inner * hat, axis=1, keepdims=True)
    dx_ref[...] = (scale * (inner - first_mean - hat * second)).astype(BF)

    for c in g_z:
        c.wait_recv()
    total = gz[0]
    for k in range(1, NZ):
        total = total + gz[k]
    total = jnp.concatenate([total[k : k + 1, :] for k in range(D // 128)], axis=1)
    gout_ref[...] = to_natural(total) / gain_ref[...].astype(F32) * FACTOR

    for j in range(SHARD):
        rows = pl.ds(j * UNIT, UNIT)
        pl.when(me.sends[j])(
            lambda: remote(w_sums.at[rows, :], w_sums.at[rows, :], ys.at[0], yr.at[j], me.homes[j]).wait_recv()
        )
    for k in range(NY):
        pl.when(me.gets[k])(lambda: y_copy(k).wait_send())
    wout_ref[...] = w_sums[...][:, :SLAB] * FACTOR
    for c in ctx_copies:
        c.wait_recv()
    ctx_ref[...] = ctx_out[...].T

    def sent_here(u, z):
        rows = unit_rows(u)
        x_copy(u, w_mid.at[rows, :], wr2.at[0, rows, :], 0, right).wait_send()
        pl.when(z != me.z)(lambda: z_copy(u, z).wait_send())

    def sent_there(u):
        rows = unit_rows(u)
        x_copy(u, w_mid.at[rows, :], wr2.at[1, rows, :], 1, right).wait_send()
        x_copy(u, w_mid.at[rows, :], wr2.at[2, rows, :], 2, left).wait_send()

    each_unit(me, sent_here, sent_there, ((0, UNITS),))
    for c in sent:
        c.wait_send()


def block(x, gain, w, cot):
    return pl.pallas_call(
        block_kernel,
        out_shape=(
            jax.ShapeDtypeStruct((TOK, NY * QW), BF),
            jax.ShapeDtypeStruct((TOK, D), BF),
            jax.ShapeDtypeStruct((BLOCK, SLAB), F32),
            jax.ShapeDtypeStruct((1, D), F32),
        ),
        in_specs=[pl.BlockSpec(memory_space=m) for m in (pl.ANY, pltpu.VMEM, pl.ANY, pl.ANY)],
        out_specs=(VMEM,) * 4,
        scratch_shapes=[
            pltpu.VMEM((TOK, D), BF),
            pltpu.VMEM((1, D), F32),
            pltpu.VMEM((BLOCK, SLAB), BF),
            pltpu.VMEM((TOK, NY * QW), BF),
            pltpu.VMEM((ROWS, D), BF),
            pltpu.VMEM((PW, D), BF),
            pltpu.VMEM((QW, ROWS), BF),
            pltpu.VMEM((BLOCK, 128), BF),
            pltpu.VMEM((NY * QW, TOK), BF),
            pltpu.VMEM((NY, UNIT, 128), BF),
            dma(4),
            dma(6), dma(6), dma(4), dma(4), dma(3), dma(4), dma(8), dma(8),
            dma(3, 8), dma(3, 8), dma(2), dma(2),
            pltpu.VMEM((2 * QW, D), BF),
            pltpu.VMEM((SEQ, 2 * QW), BF),
            pltpu.VMEM((SEQ, 2 * QW), BF),
            pltpu.VMEM((QW, ROWS), BF),
            pltpu.VMEM((NY * QW, TOK), BF),
            pltpu.VMEM((QW, ROWS), BF),
            pltpu.VMEM((ROWS, QW), BF),
            pltpu.VMEM((ROWS, 2 * QW), BF),
            pltpu.VMEM((OWN, SEQ, ROWS), F32),
            pltpu.VMEM((SEQ, ROWS), BF),
            pltpu.VMEM((2, ROWS, 2 * QW), BF),
            pltpu.VMEM((ROWS, 2 * QW), BF),
            pltpu.VMEM((ROWS, 2 * QW), BF),
            dma(3, 3), dma(3, 3), dma(3, 3), dma(3, 3), dma(3, 4), dma(3, 4),
            pltpu.VMEM((ROWS, D), BF),
            pltpu.VMEM((PW, D), BF),
            pltpu.VMEM((16, 128), F32),
            pltpu.VMEM((BLOCK, 128), F32),
            pltpu.VMEM((2, TOK // 2, D), BF),
            pltpu.VMEM((TOK // 2, D), BF),
            pltpu.VMEM((TOK // 2, D), BF),
            pltpu.VMEM((2, TOK, D), BF),
            pltpu.VMEM((2, PW, GW), BF),
            pltpu.VMEM((2, PW, GW), BF),
            pltpu.VMEM((3, PW, GW), BF),
            pltpu.VMEM((PW, GW), BF),
            pltpu.VMEM((PW, GW), BF),
            pltpu.VMEM((NZ, UNIT, GW), BF),
            pltpu.VMEM((NY, UNIT, 128), F32),
            pltpu.VMEM((2, 16, 128), F32),
            pltpu.VMEM((NY, 16, 128), F32),
            pltpu.VMEM((4, 16, 128), F32),
            pltpu.VMEM((NZ, 16, 128), F32),
            dma(6), dma(6), dma(2, 4), dma(2, 4), dma(3, 12), dma(3, 12), dma(12), dma(8),
            dma(4), dma(3), dma(14), dma(14),
        ],
        compiler_params=pltpu.CompilerParams(
            collective_id=0, has_side_effects=True, vmem_limit_bytes=56 * 2**20
        ),
        name="block",
    )(x, gain, w, cot)


def hand_over_kernel(a, b, c, g, a_out, b_out, c_out, g_out):
    a_out[...] = a[...]
    b_out[...] = b[...]
    c_out[...] = c[...]
    g_out[...] = g[...].reshape(D)


def hand_over(*arrays):
    shapes = [jax.ShapeDtypeStruct(v.shape, v.dtype) for v in arrays[:3]]
    return pl.pallas_call(
        hand_over_kernel,
        out_shape=tuple(shapes) + (jax.ShapeDtypeStruct((D,), F32),),
        in_specs=[VMEM] * 4,
        out_specs=(VMEM,) * 4,
        name="hand_over",
    )(*arrays)


def shards(tokens, norm_gain, qkv_weight, d_context):
    outputs = block(tokens[0], norm_gain, qkv_weight.T, d_context[0])
    context, d_tokens, weight_grad, gain_grad = hand_over(*outputs)
    return (context[None], d_tokens[None], weight_grad.T, gain_grad)


def solution(mesh):
    in_specs = (P("dp", "sp", None), P(), P("sp", "dp"), P("dp", "sp", None))
    out_specs = (P("dp", "sp", None), P("dp", "sp", None), P("sp", "dp"), P())
    return jax.shard_map(shards, mesh=mesh, in_specs=in_specs, out_specs=out_specs, check_vma=False)
```

```python
import functools
import math

import jax
import jax.numpy as jnp
from jax import lax
from jax.experimental import pallas as pl
from jax.experimental.pallas import tpu as pltpu
from jax.sharding import PartitionSpec as P

MESH = pl.DeviceIdType.MESH
BF = jnp.bfloat16
F32 = jnp.float32

D = 1536
HEAD = 64
OWN = 3
TOK = 128
NY = 4
NZ = 8
NA = 4
ROWS = NY * TOK
SEQ = NA * ROWS
QW = OWN * HEAD
PW = 3 * QW
SLAB = 96
BLOCK = 144
GW = NY * SLAB
EPS = 1e-05
VMEM = pl.BlockSpec(memory_space=pltpu.VMEM)


class Place:
    def __init__(self):
        d, s = lax.axis_index("dp"), lax.axis_index("sp")
        self.x_lo, self.z = d // NZ, d % NZ
        self.x_hi, self.y, self.core = s // 8, (s // 2) % NY, s % 2
        self.group = self.x_hi * 2 + self.core
        self.far_group = (1 - self.x_hi) * 2 + self.core

    def id(self, x_hi=None, x_lo=None, y=None, z=None, core=None):
        x_hi = self.x_hi if x_hi is None else x_hi
        x_lo = self.x_lo if x_lo is None else x_lo
        y = self.y if y is None else y
        z = self.z if z is None else z
        core = self.core if core is None else core
        return {"dp": x_lo * NZ + z, "sp": x_hi * 8 + y * 2 + core}

    def find_units(self):
        self.homes, self.sends = [], []
        for j in range(SHARD):
            y, u = shard_unit(self, j)
            x_lo, z = unit_home(u, y)
            self.homes.append(self.id(x_lo=x_lo, z=z, y=y))
            self.sends.append((y != self.y) | (x_lo != self.x_lo) | (z != self.z))
        self.starts = [((16 * k + 4 * self.y) // SHARD) % NZ for k in range(SHARD)]
        self.has, self.unit = unit_at(self.x_lo, self.z, self.starts)
        volume, self.place = unit_source(self.unit, self.y)
        elsewhere = volume != self.x_lo * NZ + self.z
        self.sources = [self.id(x_lo=volume // NZ, z=volume % NZ, y=k) for k in range(NY)]
        self.gets = [self.has & ((self.y != k) | elsewhere) for k in range(NY)]
        self.keeps = [self.has & (self.y == k) & jnp.logical_not(elsewhere) for k in range(NY)]

    def other_core(self):
        return self.id(core=1 - self.core)

    def mirror(self):
        return self.id(x_hi=1 - self.x_hi, x_lo=1 - self.x_lo)

    def beside(self):
        return self.id(x_lo=1 - self.x_lo)

    def far(self):
        return self.id(x_hi=1 - self.x_hi)

    def along_y(self, step):
        return self.id(y=(self.y + step) % NY)

    def along_z(self, step):
        return self.id(z=(self.z + step) % NZ)

    def along_x(self, step):
        x = (self.x_hi * 2 + self.x_lo + step) % 4
        return self.id(x_hi=x // 2, x_lo=x % 2)


def greet(me):
    barrier = pltpu.get_barrier_semaphore()
    partners = (
        [me.along_z(r) for r in range(1, NZ)]
        + [me.along_y(r) for r in range(1, NY)]
        + [me.along_x(r) for r in range(1, 4)]
        + [me.other_core()]
    )

    def tell(partner):
        pl.semaphore_signal(barrier, inc=1, device_id=partner, device_id_type=MESH)

    for partner in partners:
        tell(partner)
    count = jnp.int32(len(partners))
    for j in range(SHARD):
        pl.when(me.sends[j])(lambda: tell(me.homes[j]))
        count = count + me.sends[j].astype(jnp.int32)
    for k in range(NY):
        pl.when(me.gets[k])(lambda: tell(me.sources[k]))
        count = count + me.gets[k].astype(jnp.int32)
    return functools.partial(pl.semaphore_wait, barrier, count)


def remote(src, dst, send, recv, partner):
    return pltpu.make_async_remote_copy(
        src_ref=src, dst_ref=dst, send_sem=send, recv_sem=recv, device_id=partner, device_id_type=MESH
    )


def rows_at(start, size):
    return pl.ds(pl.multiple_of(start, 16), size)


def lanes_at(start, size):
    return pl.ds(pl.multiple_of(start, 128), size)


def to_grouped(wide):
    parts = []
    for x_hi in range(2):
        for core in range(2):
            for y in range(NY):
                s = x_hi * 8 + y * 2 + core
                parts.append(wide[:, s * SLAB : (s + 1) * SLAB])
    return jnp.concatenate(parts, axis=1)


def to_natural(wide):
    parts = []
    for x_hi in range(2):
        for y in range(NY):
            for core in range(2):
                s = (x_hi * 2 + core) * NY + y
                parts.append(wide[:, s * SLAB : (s + 1) * SLAB])
    return jnp.concatenate(parts, axis=1)


UNIT = 48
UNITS = 12
SHARD = 3


def unit_source(u, y):
    column = (u // 4) * 16 + 4 * y + u % 4
    return column // SHARD, column % SHARD


def unit_home(u, y):
    return u % 2, ((16 * (u // 4) + 4 * y) // SHARD + (u % 4) // 2) % NZ


def unit_at(x_lo, z, starts):
    found, unit = jnp.int32(0), jnp.int32(0)
    for k in range(SHARD):
        ahead = z - starts[k]
        for h in range(2):
            hit = ((ahead == h) | (ahead == h - NZ)).astype(jnp.int32)
            found, unit = found + hit, unit + hit * (4 * k + 2 * h)
    return found > 0, unit + x_lo


def shard_unit(me, j):
    column = (me.x_lo * NZ + me.z) * SHARD + j
    return (column % 16) // 4, (column // 16) * 4 + column % 4


def each_unit(me, here, there, spans):
    def step(u, carry):
        k, i = u // 4, u % 4
        z = jnp.where(k == 0, me.starts[0], jnp.where(k == 1, me.starts[1], me.starts[2])) + i // 2
        x_lo, z = i % 2, jnp.where(z >= NZ, z - NZ, z)
        if here is not None:
            pl.when(x_lo == me.x_lo)(lambda: here(u, z))
        if there is not None:
            pl.when(x_lo != me.x_lo)(lambda: there(u))
        return carry

    for first, end in spans:
        lax.fori_loop(first, end, step, 0)


def near_first(me, x_lo, act, first=0, end=NZ):
    def step(n, carry):
        r = jnp.where(n % 2 == 1, (n + 1) // 2, (NZ - n // 2) % NZ)
        z = me.z - r
        has, u = unit_at(x_lo, jnp.where(z < 0, z + NZ, z), me.starts)
        pl.when(has)(lambda: act(r, u))
        return carry

    lax.fori_loop(first, end, step, 0)


def unit_rows(u):
    return rows_at(u * UNIT, UNIT)


def gather_phase(me, ready, load, x_ref, gain_ref, raw_ref, cot_ref, nall, wall, cots,
                 w_ref, cot_t, ybuf, ns, nr, cs, cr, ys, yr, zs, zr, xs, xr, ds, dr):
    y = me.y
    right, left = me.along_x(1), me.along_x(3)
    x_at = me.x_hi * 2 + me.x_lo
    own = lanes_at(me.group * GW, GW)
    far = lanes_at(me.far_group * GW, GW)
    hi_left, hi_right = ((x_at + 3) % 4) // 2, ((x_at + 1) % 4) // 2
    of_left = lanes_at((hi_left * 2 + me.core) * GW, GW)
    of_right = lanes_at((hi_right * 2 + me.core) * GW, GW)
    load(raw_ref)
    w_ref[...] = jnp.concatenate([raw_ref[...], jnp.zeros((BLOCK, 128 - SLAB), BF)], axis=1)
    ready()

    def y_copy(j):
        return remote(w_ref.at[pl.ds(j * UNIT, UNIT), :], ybuf.at[y], ys.at[j], yr.at[y], me.homes[j])

    for j in range(SHARD):
        pl.when(me.sends[j])(lambda: y_copy(j).start())

    load(x_ref)
    x = x_ref[...].astype(F32)
    centred = x - jnp.mean(x, axis=1, keepdims=True)
    spread = jnp.mean(centred * centred, axis=1, keepdims=True)
    normed = centred * lax.rsqrt(spread + EPS) * gain_ref[...].astype(F32)
    tok_rows = rows_at(y * TOK, TOK)
    nall[tok_rows, :] = to_grouped(normed).astype(BF)
    up, down = me.along_y(1), me.along_y(3)
    half = TOK // 2
    low, high = rows_at(y * TOK, half), rows_at(y * TOK + half, half)

    def n_copy(rows, k, to):
        c = remote(nall.at[rows, :], nall.at[rows, :], ns.at[k], nr.at[k], to)
        c.start()
        return c

    n_up, n_down = n_copy(low, 0, up), n_copy(high, 1, down)
    n_rest = [n_copy(high, 4, up), n_copy(low, 5, down)]
    for k in range(NY):
        pl.when(me.gets[k])(lambda: remote(ybuf.at[k], ybuf.at[k], ys.at[0], yr.at[k], me.sources[k]).wait_recv())

        @pl.when(me.keeps[k])
        def _():
            ybuf[k] = w_ref[rows_at(me.place * UNIT, UNIT), :]

    @pl.when(me.has)
    def _():
        parts = [ybuf[k][:, :SLAB].astype(F32) for k in range(NY)]
        wall[unit_rows(me.unit), own] = jnp.concatenate(parts, axis=1).astype(BF)

    def piece(u, lanes):
        return wall.at[unit_rows(u), lanes]

    def z_copy(u, r):
        return remote(piece(u, own), piece(u, own), zs.at[r], zr.at[r], me.along_z(r))

    def x_copy(u, r, lanes, kind, to):
        return remote(piece(u, lanes), piece(u, lanes), xs.at[kind, r], xr.at[kind, r], to)

    @pl.when(me.has)
    def _():
        for r in (1, 7, 2, 6, 3, 5, 4):
            z_copy(me.unit, r).start()

    cot_copies = []
    load(cot_ref)
    cot_t[...] = cot_ref[...].T
    cot_lanes = lanes_at(y * TOK, TOK)
    for r in range(1, NY):
        to = (y + r) % NY
        c = remote(cot_t.at[rows_at(to * QW, QW), :], cots.at[:, cot_lanes], cs.at[r], cr.at[r], me.along_y(r))
        c.start()
        cot_copies.append(c)
    cots[:, cot_lanes] = cot_t[rows_at(y * QW, QW), :]

    def spread_x(r, u):
        pl.when(r != 0)(lambda: z_copy(u, r).wait_recv())
        x_copy(u, r, own, 0, right).start()
        x_copy(u, r, own, 1, left).start()

    near_first(me, me.x_lo, spread_x, 0, 3)
    from_down = rows_at(((y + 3) % NY) * TOK, half)
    from_up = rows_at(((y + 1) % NY) * TOK + half, half)
    n_up.wait_recv()
    f_up = n_copy(from_down, 2, up)
    n_down.wait_recv()
    f_down = n_copy(from_up, 3, down)
    near_first(me, me.x_lo, spread_x, 3, NZ)

    def relay(r, u):
        x_copy(u, r, of_left, 0, right).wait_recv()
        pl.when((u // 2) % 2 == 0)(lambda: x_copy(u, r, of_left, 2, right).start())
        x_copy(u, r, of_right, 1, left).wait_recv()
        pl.when((u // 2) % 2 == 1)(lambda: x_copy(u, r, of_right, 2, left).start())

    near_first(me, 1 - me.x_lo, relay)
    near_first(me, me.x_lo, lambda r, u: x_copy(u, r, far, 2, right).wait_recv())

    core_copies = []
    for x_hi in range(2):
        lanes = lanes_at((x_hi * 2 + me.core) * GW, GW)
        c = remote(wall.at[:, lanes], wall.at[:, lanes], ds.at[x_hi], dr.at[x_hi], me.other_core())
        c.start()
        core_copies.append(c)
    for c in core_copies:
        c.wait_recv()
    for c in n_rest + [f_up, f_down]:
        c.wait_recv()
    for c in cot_copies:
        c.wait_recv()

    def drain():
        @pl.when(me.has)
        def _():
            for r in range(1, NZ):
                z_copy(me.unit, r).wait_send()

        def sent_here(r, u):
            x_copy(u, r, own, 0, right).wait_send()
            x_copy(u, r, own, 1, left).wait_send()

        near_first(me, me.x_lo, sent_here)
        near_first(me, 1 - me.x_lo, lambda r, u: x_copy(u, r, own, 2, right).wait_send())
        for j in range(SHARD):
            pl.when(me.sends[j])(lambda: y_copy(j).wait_send())
        for c in cot_copies + core_copies + n_rest + [n_up, n_down, f_up, f_down]:
            c.wait_send()

    return drain


def dma(*shape):
    return pltpu.SemaphoreType.DMA(shape)


FACTOR = 1.0 / math.sqrt(16 * SEQ)
CHUNK = 256
EARLY = ((0, 6), (8, 10))
LATE = ((6, 8), (10, 12))


def block_kernel(x_hbm, gain_in, w_hbm, cot_hbm, ctx_ref, dx_ref, wout_ref, gout_ref,
                 x_ref, gain_ref, shard_ref, d_ctx, n_ref, w_ref, cot_ref, w_pad, cot_t, ybuf, ls,
                 *rest):
    me = Place()
    y = me.y
    me.find_units()
    ready = greet(me)
    gain_ref[...] = gain_in[...].astype(F32).reshape(1, D)
    loads = {}
    for k, (src, dst) in enumerate(
        ((w_hbm, shard_ref), (x_hbm, x_ref), (cot_hbm, d_ctx))
    ):
        c = pltpu.make_async_copy(src, dst, ls.at[k])
        c.start()
        loads[id(dst)] = c
    drain = gather_phase(
        me, ready, lambda ref: loads[id(ref)].wait(), x_ref, gain_ref, shard_ref, d_ctx,
        n_ref, w_ref, cot_ref, w_pad, cot_t, ybuf, *rest[:12],
    )
    back_phase(
        me, drain, n_ref, w_ref, cot_ref, x_ref, gain_ref, ctx_ref, dx_ref, wout_ref, gout_ref, *rest[12:]
    )


def back_phase(me, drain, n_ref, w_ref, cot_ref, x_ref, gain_ref, ctx_ref, dx_ref, wout_ref, gout_ref,
               wuse, kvall, dkv, ctx_own, ctx_out, dq_ref, dq_own, out_ref, s_buf, e_buf, r1, mid, r2,
               ks, kr, ss, rs, cs, cr,
               dn_ref, wg_ref, gg_ref, w_sums,
               half_r, to_up, to_down, full_r, s1, wr1, wr2, w_mid, zout, zbuf, yout,
               gcore, gy, gx, gz,
               ns, nr, ws, wr, xs, xr, zs, zr, ys, yr, gs, gr):
    y = me.y
    own = rows_at(me.group * ROWS, ROWS)
    far = rows_at(me.far_group * ROWS, ROWS)
    near = me.x_hi * 2 + 1 - me.core
    beyond = (1 - me.x_hi) * 2 + 1 - me.core
    own_there = rows_at(near * ROWS, ROWS)
    far_there = rows_at(beyond * ROWS, ROWS)
    groups = (me.group, near, me.far_group, beyond)

    def chunks(at):
        for i in range(ROWS // CHUNK):
            here = at * ROWS + i * CHUNK
            yield rows_at(groups[at] * ROWS + i * CHUNK, CHUNK), slice(here, here + CHUNK)

    mine = y * QW
    sent = []

    def go(*args):
        c = remote(*args)
        c.start()
        sent.append(c)
        return c

    def head_lanes(h):
        return slice(h * 128, (h + 1) * 128)

    nt = (((1,), (1,)), ((), ()))
    k_far, k_core = [], []
    for h in range(OWN):
        lanes = head_lanes(h)
        for which in range(2):
            row = QW * (1 + which) + h * HEAD
            wuse[h * 128 + which * HEAD : h * 128 + (which + 1) * HEAD, :] = w_ref[row : row + HEAD, :]
        kvall[own, lanes] = lax.dot_general(n_ref[...], wuse[lanes, :], nt, preferred_element_type=F32).astype(BF)
        k_far.append(go(kvall.at[own, lanes], kvall.at[own, lanes], ks.at[0, h], kr.at[0, h], me.far()))
        k_core.append(go(kvall.at[own, lanes], kvall.at[own, lanes], ks.at[1, h], kr.at[1, h], me.other_core()))
    queries = lax.dot_general(w_ref[:QW, :], n_ref[...], nt, preferred_element_type=F32).astype(BF)
    k_pass = []
    d_far, d_own, d_x, ctx_copies = [], [], [], []

    def pass_keys(h):
        k_far[h].wait_recv()
        k_pass.append(go(kvall.at[far, head_lanes(h)], kvall.at[far, head_lanes(h)], ks.at[2, h], kr.at[2, h], me.other_core()))

    def pass_sums(h):
        lanes = head_lanes(h)
        d_far[h].wait_recv()
        mid[:, lanes] = (dkv[far, lanes].astype(F32) + r1[0, :, lanes].astype(F32)).astype(BF)
        d_x.append(go(mid.at[:, lanes], r2.at[:, lanes], ss.at[2, h], rs.at[2, h], me.far()))

    def finish(h):
        lanes = head_lanes(h)
        d_own[h].wait_recv()
        d_x[h].wait_recv()
        out_ref[:, lanes] = (
            dkv[own, lanes].astype(F32) + r1[1, :, lanes].astype(F32) + r2[:, lanes].astype(F32)
        ).astype(BF)

    zeros = jnp.zeros((HEAD, ROWS), BF)
    q_pads, tops = [], []

    def score(h, at):
        for keys, rows in chunks(at):
            s = jnp.dot(kvall[keys, head_lanes(h)], q_pads[h], preferred_element_type=F32)
            s_buf[h, rows, :] = s
            tops[h] = jnp.maximum(tops[h], jnp.max(s.reshape(CHUNK // 8, 8, ROWS), axis=0))

    for h in range(OWN):
        q = queries[h * HEAD : (h + 1) * HEAD, :] * jnp.asarray(HEAD**-0.5, BF)
        q_pads.append(jnp.concatenate([q, zeros], axis=0))
        tops.append(jnp.full((8, ROWS), -jnp.inf, F32))
        score(h, 0)
    for h in range(OWN):
        k_core[h].wait_recv()
        score(h, 1)
    drain()
    pass_keys(0)
    for h in range(OWN):
        lanes = head_lanes(h)
        head_rows = slice(h * HEAD, (h + 1) * HEAD)
        q_pad = q_pads[h]
        score(h, 2)
        k_pass[h].wait_recv()
        score(h, 3)
        top = tops[h]
        top = jnp.max(top, axis=0, keepdims=True)
        total = jnp.zeros((8, ROWS), F32)
        ctx = jnp.zeros((HEAD, ROWS), F32)
        for at in range(NA):
            for keys, rows in chunks(at):
                e = jnp.exp(s_buf[h, rows, :] - top)
                total = total + jnp.sum(e.reshape(CHUNK // 8, 8, ROWS), axis=0)
                e_low = e.astype(BF)
                e_buf[rows, :] = e_low
                v_t = kvall[keys, lanes].T[HEAD:, :]
                ctx = ctx + jnp.dot(v_t, e_low, preferred_element_type=F32)
        inverse = 1.0 / jnp.sum(total, axis=0, keepdims=True)
        ctx = ctx * inverse
        ctx_own[head_rows, :] = ctx.astype(BF)
        rows_there = rows_at(mine + h * HEAD, HEAD)
        for r in range(1, NY):
            to = lanes_at(((y + r) % NY) * TOK, TOK)
            ctx_copies.append(go(ctx_own.at[head_rows, to], ctx_out.at[rows_there, :], cs.at[h, r], cr.at[h, r], me.along_y(r)))
        ctx_out[rows_there, :] = ctx_own[head_rows, lanes_at(y * TOK, TOK)]
        if h + 1 < OWN:
            pass_keys(h + 1)
        cot = (cot_ref[head_rows, :].astype(F32) * inverse).astype(BF)
        row_dot = jnp.sum(cot.astype(F32) * ctx, axis=0, keepdims=True)
        cot_pad = jnp.concatenate([zeros, cot], axis=0)
        q_side = q_pad.T
        cot_side = cot_pad.T
        dq = jnp.zeros((HEAD, ROWS), F32)
        for at in (3, 2, 1, 0):
            for keys, rows in chunks(at):
                d_attn = jnp.dot(kvall[keys, lanes], cot_pad, preferred_element_type=F32)
                e_low = e_buf[rows, :]
                slopes = (e_low.astype(F32) * (d_attn - row_dot)).astype(BF)
                k_t = kvall[keys, lanes].T[:HEAD, :]
                dq = dq + jnp.dot(k_t, slopes, preferred_element_type=F32)
                dkv[keys, lanes] = (
                    jnp.dot(slopes, q_side, preferred_element_type=F32)
                    + jnp.dot(e_low, cot_side, preferred_element_type=F32)
                ).astype(BF)
            if at == 3:
                d_far.append(go(dkv.at[far_there, lanes], r1.at[0, :, lanes], ss.at[0, h], rs.at[0, h], me.other_core()))
            if at == 1:
                d_own.append(go(dkv.at[own_there, lanes], r1.at[1, :, lanes], ss.at[1, h], rs.at[1, h], me.other_core()))
                pass_sums(h)
        dq_ref[head_rows, :] = (dq * HEAD**-0.5).astype(BF)

    right, left = me.along_x(1), me.along_x(3)
    x_at = me.x_hi * 2 + me.x_lo
    hi_left, hi_right = ((x_at + 3) % 4) // 2, ((x_at + 1) % 4) // 2
    half = TOK // 2
    up, down = me.along_y(1), me.along_y(3)
    opposite = (y + 2) % NY

    def weight_rows(h):
        rows = jnp.dot(out_ref[:, head_lanes(h)].T, n_ref[...], preferred_element_type=F32).astype(BF)
        for which in range(2):
            row = QW * (1 + which) + h * HEAD
            wg_ref[row : row + HEAD, :] = rows[which * HEAD : (which + 1) * HEAD, :]

    w_core = []

    def to_core(first, size):
        rows = pl.ds(first, size)
        k = len(w_core) // 2
        for x_hi in range(2):
            there = lanes_at((x_hi * 2 + 1 - me.core) * GW, GW)
            w_core.append(go(wg_ref.at[rows, there], wr1.at[x_hi, rows, :], ws.at[x_hi, k], wr.at[x_hi, k], me.other_core()))

    def from_core(k, first, size):
        rows = slice(first, first + size)
        for x_hi in range(2):
            w_core[2 * k + x_hi].wait_recv()
            here = lanes_at((x_hi * 2 + me.core) * GW, GW)
            s1[x_hi, rows, :] = (wg_ref[rows, here].astype(F32) + wr1[x_hi, rows, :].astype(F32)).astype(BF)

    def x_copy(u, src, dst, kind, to):
        return remote(src, dst, xs.at[kind, u], xr.at[kind, u], to)

    def to_opposite(u, z):
        src = s1.at[1 - me.x_hi, unit_rows(u), :]
        dst = wr2.at[0, unit_rows(u), :]
        pl.when((u // 2) % 2 == 0)(lambda: x_copy(u, src, dst, 0, right).start())
        pl.when((u // 2) % 2 == 1)(lambda: x_copy(u, src, dst, 0, left).start())

    def straight(u):
        rows = unit_rows(u)
        x_copy(u, s1.at[hi_left, rows, :], wr2.at[2, rows, :], 2, left).start()
        x_copy(u, s1.at[hi_right, rows, :], wr2.at[1, rows, :], 1, right).start()

    def straight_opposite(u, z):
        rows = unit_rows(u)
        x_copy(u, s1.at[1 - me.x_hi, rows, :], wr2.at[0, rows, :], 0, me.far()).start()

    def pass_on(u):
        rows = unit_rows(u)
        pl.when((u // 2) % 2 == 0)(lambda: x_copy(u, s1.at[hi_left, rows, :], wr2.at[2, rows, :], 2, left).start())
        pl.when((u // 2) % 2 == 1)(lambda: x_copy(u, s1.at[hi_right, rows, :], wr2.at[1, rows, :], 1, right).start())
        x_copy(u, s1.at[0, rows, :], wr2.at[0, rows, :], 0, right).wait_recv()

        @pl.when((u // 2) % 2 == 0)
        def _():
            w_mid[rows, :] = (s1[hi_right, rows, :].astype(F32) + wr2[0, rows, :].astype(F32)).astype(BF)
            x_copy(u, w_mid.at[rows, :], wr2.at[1, rows, :], 1, right).start()

        @pl.when((u // 2) % 2 == 1)
        def _():
            w_mid[rows, :] = (s1[hi_left, rows, :].astype(F32) + wr2[0, rows, :].astype(F32)).astype(BF)
            x_copy(u, w_mid.at[rows, :], wr2.at[2, rows, :], 2, left).start()


    def z_copy(u, z):
        distance = (z + NZ - me.z) % NZ
        return remote(zout.at[unit_rows(u), :], zbuf.at[distance], zs.at[u], zr.at[distance], me.id(z=z))

    def over_x(u, z):
        rows = unit_rows(u)
        x_copy(u, s1.at[0, rows, :], wr2.at[1, rows, :], 1, right).wait_recv()
        x_copy(u, s1.at[0, rows, :], wr2.at[2, rows, :], 2, left).wait_recv()
        zout[rows, :] = (
            s1[me.x_hi, rows, :].astype(F32) + wr2[1, rows, :].astype(F32) + wr2[2, rows, :].astype(F32)
        ).astype(BF)
        pl.when(z != me.z)(lambda: z_copy(u, z).start())

    def over_x_straight(u, z):
        rows = unit_rows(u)
        for kind in range(3):
            x_copy(u, s1.at[0, rows, :], wr2.at[kind, rows, :], kind, right).wait_recv()
        zout[rows, :] = (
            s1[me.x_hi, rows, :].astype(F32) + wr2[0, rows, :].astype(F32)
            + wr2[1, rows, :].astype(F32) + wr2[2, rows, :].astype(F32)
        ).astype(BF)
        pl.when(z != me.z)(lambda: z_copy(u, z).start())


    wg_ref[:QW, :] = jnp.dot(dq_ref[...], n_ref[...], preferred_element_type=F32).astype(BF)
    for h in range(OWN - 1):
        finish(h)
        weight_rows(h)
    to_core(0, 288)
    to_core(384, 96)
    from_core(0, 0, 288)
    from_core(1, 384, 96)
    each_unit(me, to_opposite, None, EARLY)
    finish(OWN - 1)
    weight_rows(OWN - 1)
    to_core(288, 96)
    to_core(480, 96)
    dq_own[...] = dq_ref[...].T
    gain_terms = jnp.zeros((8, D), F32)
    for r in (2, 1, 3, 0):
        at = (y + r) % NY
        rows = rows_at(at * TOK, TOK)
        first_rows = rows_at(at * TOK, half)
        rest_rows = rows_at(at * TOK + half, half)
        part = jnp.dot(dq_own[rows, :], w_ref[:QW, :], preferred_element_type=F32) + jnp.dot(
            out_ref[rows, :], wuse[...], preferred_element_type=F32
        )
        dn_ref[rows, :] = part.astype(BF)
        if r == 2:
            h_up = go(dn_ref.at[first_rows, :], half_r.at[0], ns.at[0], nr.at[0], up)
            h_down = go(dn_ref.at[rest_rows, :], half_r.at[1], ns.at[1], nr.at[1], down)
        if r == 1:
            f_rest = [go(dn_ref.at[rest_rows, :], full_r.at[0, pl.ds(half, half), :], ns.at[4], nr.at[4], up)]
        if r == 3:
            f_rest.append(go(dn_ref.at[first_rows, :], full_r.at[1, pl.ds(0, half), :], ns.at[5], nr.at[5], down))
        terms = part * n_ref[rows, :].astype(F32)
        gain_terms = gain_terms + jnp.sum(terms.reshape(TOK // 8, 8, D), axis=0)
    gain_terms = jnp.sum(gain_terms, axis=0, keepdims=True)
    gg_ref[...] = jnp.zeros((16, 128), F32)
    for k in range(D // 128):
        gg_ref[k : k + 1, :] = gain_terms[:, k * 128 : (k + 1) * 128]
    gcore[me.core] = gg_ref[...]
    g_core = go(gg_ref, gcore.at[me.core], gs.at[0], gr.at[0], me.other_core())
    from_core(2, 288, 96)
    from_core(3, 480, 96)
    each_unit(me, to_opposite, None, LATE)
    each_unit(me, None, pass_on, EARLY)
    g_core.wait_recv()
    gy[y] = gcore[0] + gcore[1]
    g_y = [go(gy.at[y], gy.at[y], gs.at[r], gr.at[r], me.along_y(r)) for r in range(1, NY)]
    h_up.wait_recv()
    block = rows_at(((y + 1) % NY) * TOK, half)
    to_up[...] = (dn_ref[block, :].astype(F32) + half_r[0].astype(F32)).astype(BF)
    f_up = go(to_up, full_r.at[0, pl.ds(0, half), :], ns.at[2], nr.at[2], up)
    h_down.wait_recv()
    block = rows_at(((y + 3) % NY) * TOK + half, half)
    to_down[...] = (dn_ref[block, :].astype(F32) + half_r[1].astype(F32)).astype(BF)
    f_down = go(to_down, full_r.at[1, pl.ds(half, half), :], ns.at[3], nr.at[3], down)

    each_unit(me, None, pass_on, LATE)
    each_unit(me, over_x, None, EARLY)
    for c in g_y:
        c.wait_recv()
    gx[x_at] = gy[0] + gy[1] + gy[2] + gy[3]
    g_x = [go(gx.at[x_at], gx.at[x_at], gs.at[3 + r], gr.at[3 + r], me.along_x(r)) for r in range(1, 4)]

    each_unit(me, over_x, None, LATE)
    for c in g_x:
        c.wait_recv()
    gz[me.z] = gx[0] + gx[1] + gx[2] + gx[3]
    g_z = [go(gz.at[me.z], gz.at[me.z], gs.at[6 + r], gr.at[6 + r], me.along_z(r)) for r in range(1, NZ)]

    own_place = rows_at(me.place * UNIT, UNIT)

    def y_copy(k):
        return remote(yout.at[k], w_sums.at[own_place, :], ys.at[k], yr.at[me.place], me.sources[k])

    @pl.when(me.has)
    def _():
        total = zout[unit_rows(me.unit), :].astype(F32)
        for r in range(1, NZ):
            remote(zbuf.at[r], zbuf.at[r], zs.at[0], zr.at[r], me.along_z(r)).wait_recv()
            total = total + zbuf[r].astype(F32)
        for k in range(NY):
            part = total[:, k * SLAB : (k + 1) * SLAB]
            yout[k] = jnp.concatenate([part, jnp.zeros((UNIT, 128 - SLAB), F32)], axis=1)

    for k in range(NY):
        pl.when(me.gets[k])(lambda: y_copy(k).start())

        @pl.when(me.keeps[k])
        def _():
            w_sums[own_place, :] = yout[k]

    x = x_ref[...].astype(F32)
    centred = x - jnp.mean(x, axis=1, keepdims=True)
    spread = jnp.mean(centred * centred, axis=1, keepdims=True)
    scale = lax.rsqrt(spread + EPS)
    hat = centred * scale
    for c in f_rest + [f_up, f_down]:
        c.wait_recv()
    d_normed = (
        dn_ref[rows_at(y * TOK, TOK), :].astype(F32) + full_r[0].astype(F32) + full_r[1].astype(F32)
    )
    inner = to_natural(d_normed) * gain_ref[...].astype(F32)
    first_mean = jnp.mean(inner, axis=1, keepdims=True)
    second = jnp.mean(inner * hat, axis=1, keepdims=True)
    dx_ref[...] = (scale * (inner - first_mean - hat * second)).astype(BF)

    for c in g_z:
        c.wait_recv()
    total = gz[0]
    for k in range(1, NZ):
        total = total + gz[k]
    total = jnp.concatenate([total[k : k + 1, :] for k in range(D // 128)], axis=1)
    gout_ref[...] = to_natural(total) / gain_ref[...].astype(F32) * FACTOR

    for c in ctx_copies:
        c.wait_recv()
    ctx_ref[...] = ctx_out[...].T

    def sent_here(u, z):
        rows = unit_rows(u)
        x_copy(u, w_mid.at[rows, :], wr2.at[0, rows, :], 0, right).wait_send()
        pl.when(z != me.z)(lambda: z_copy(u, z).wait_send())

    def sent_there(u):
        rows = unit_rows(u)
        x_copy(u, w_mid.at[rows, :], wr2.at[1, rows, :], 1, right).wait_send()
        x_copy(u, w_mid.at[rows, :], wr2.at[2, rows, :], 2, left).wait_send()

    each_unit(me, sent_here, sent_there, ((0, UNITS),))
    for c in sent:
        c.wait_send()

    for j in range(SHARD):
        rows = pl.ds(j * UNIT, UNIT)
        pl.when(me.sends[j])(
            lambda: remote(w_sums.at[rows, :], w_sums.at[rows, :], ys.at[0], yr.at[j], me.homes[j]).wait_recv()
        )
    for k in range(NY):
        pl.when(me.gets[k])(lambda: y_copy(k).wait_send())
    wout_ref[...] = w_sums[...][:, :SLAB] * FACTOR


def block(x, gain, w, cot):
    return pl.pallas_call(
        block_kernel,
        out_shape=(
            jax.ShapeDtypeStruct((TOK, NY * QW), BF),
            jax.ShapeDtypeStruct((TOK, D), BF),
            jax.ShapeDtypeStruct((BLOCK, SLAB), F32),
            jax.ShapeDtypeStruct((1, D), F32),
        ),
        in_specs=[pl.BlockSpec(memory_space=m) for m in (pl.ANY, pltpu.VMEM, pl.ANY, pl.ANY)],
        out_specs=(VMEM,) * 4,
        scratch_shapes=[
            pltpu.VMEM((TOK, D), BF),
            pltpu.VMEM((1, D), F32),
            pltpu.VMEM((BLOCK, SLAB), BF),
            pltpu.VMEM((TOK, NY * QW), BF),
            pltpu.VMEM((ROWS, D), BF),
            pltpu.VMEM((PW, D), BF),
            pltpu.VMEM((QW, ROWS), BF),
            pltpu.VMEM((BLOCK, 128), BF),
            pltpu.VMEM((NY * QW, TOK), BF),
            pltpu.VMEM((NY, UNIT, 128), BF),
            dma(4),
            dma(6), dma(6), dma(4), dma(4), dma(3), dma(4), dma(8), dma(8),
            dma(3, 8), dma(3, 8), dma(2), dma(2),
            pltpu.VMEM((2 * QW, D), BF),
            pltpu.VMEM((SEQ, 2 * QW), BF),
            pltpu.VMEM((SEQ, 2 * QW), BF),
            pltpu.VMEM((QW, ROWS), BF),
            pltpu.VMEM((NY * QW, TOK), BF),
            pltpu.VMEM((QW, ROWS), BF),
            pltpu.VMEM((ROWS, QW), BF),
            pltpu.VMEM((ROWS, 2 * QW), BF),
            pltpu.VMEM((OWN, SEQ, ROWS), F32),
            pltpu.VMEM((SEQ, ROWS), BF),
            pltpu.VMEM((2, ROWS, 2 * QW), BF),
            pltpu.VMEM((ROWS, 2 * QW), BF),
            pltpu.VMEM((ROWS, 2 * QW), BF),
            dma(3, 3), dma(3, 3), dma(3, 3), dma(3, 3), dma(3, 4), dma(3, 4),
            pltpu.VMEM((ROWS, D), BF),
            pltpu.VMEM((PW, D), BF),
            pltpu.VMEM((16, 128), F32),
            pltpu.VMEM((BLOCK, 128), F32),
            pltpu.VMEM((2, TOK // 2, D), BF),
            pltpu.VMEM((TOK // 2, D), BF),
            pltpu.VMEM((TOK // 2, D), BF),
            pltpu.VMEM((2, TOK, D), BF),
            pltpu.VMEM((2, PW, GW), BF),
            pltpu.VMEM((2, PW, GW), BF),
            pltpu.VMEM((3, PW, GW), BF),
            pltpu.VMEM((PW, GW), BF),
            pltpu.VMEM((PW, GW), BF),
            pltpu.VMEM((NZ, UNIT, GW), BF),
            pltpu.VMEM((NY, UNIT, 128), F32),
            pltpu.VMEM((2, 16, 128), F32),
            pltpu.VMEM((NY, 16, 128), F32),
            pltpu.VMEM((4, 16, 128), F32),
            pltpu.VMEM((NZ, 16, 128), F32),
            dma(6), dma(6), dma(2, 4), dma(2, 4), dma(3, 12), dma(3, 12), dma(12), dma(8),
            dma(4), dma(3), dma(14), dma(14),
        ],
        compiler_params=pltpu.CompilerParams(
            collective_id=0, has_side_effects=True, vmem_limit_bytes=56 * 2**20
        ),
        name="block",
    )(x, gain, w, cot)


def hand_over_kernel(a, b, c, g, a_out, b_out, c_out, g_out):
    a_out[...] = a[...]
    b_out[...] = b[...]
    c_out[...] = c[...]
    g_out[...] = g[...].reshape(D)


def hand_over(*arrays):
    shapes = [jax.ShapeDtypeStruct(v.shape, v.dtype) for v in arrays[:3]]
    return pl.pallas_call(
        hand_over_kernel,
        out_shape=tuple(shapes) + (jax.ShapeDtypeStruct((D,), F32),),
        in_specs=[VMEM] * 4,
        out_specs=(VMEM,) * 4,
        name="hand_over",
    )(*arrays)


def shards(tokens, norm_gain, qkv_weight, d_context):
    outputs = block(tokens[0], norm_gain, qkv_weight.T, d_context[0])
    context, d_tokens, weight_grad, gain_grad = hand_over(*outputs)
    return (context[None], d_tokens[None], weight_grad.T, gain_grad)


def solution(mesh):
    in_specs = (P("dp", "sp", None), P(), P("sp", "dp"), P("dp", "sp", None))
    out_specs = (P("dp", "sp", None), P("dp", "sp", None), P("sp", "dp"), P())
    return jax.shard_map(shards, mesh=mesh, in_specs=in_specs, out_specs=out_specs, check_vma=False)
```
